128 devices in a mesh: patch: 32 (over z, x, core), feat: 4 (over y).
Axes of the slice: x: 4, y: 4, z: 4, core: 2. Of those that a mesh axis runs over, the one named last changes fastest.
Arguments:
- node_lat: bfloat16 [32768, 512], P(('patch', 'feat')), may hold values from -6 to 6
- edge_lat: bfloat16 [262144, 512], P(('patch', 'feat')), may hold values from -6 to 6
- edge_src: int32 [262144], P(('patch', 'feat')), may hold values from 0 to 831, as said below
- edge_dst: int32 [262144], P(('patch', 'feat')), may hold values from 0 to 255
- edge_count: int32 [128], P(('patch', 'feat')), may hold values from 512 to 2048, as said below
- halo_send: int32 [128, 2, 32], P(('patch', 'feat')), may hold values from 0 to 255
- coarse_of: int32 [128, 4], P(('patch', 'feat')), may hold values from 0 to 255
- edge_w1: bfloat16 [3, 512, 512], P(None, None, 'feat'), may hold values from -0.15625 to 0.15625
- edge_w2: bfloat16 [512, 512], P('feat'), may hold values from -0.25 to 0.25
- node_w1: bfloat16 [2, 512, 512], P(None, None, 'feat'), may hold values from -0.1875 to 0.1875
- node_w2: bfloat16 [512, 512], P('feat'), may hold values from -0.25 to 0.25
- grad_node: bfloat16 [32768, 512], P(('patch', 'feat')), may hold values from -6 to 6
- grad_edge: bfloat16 [262144, 512], P(('patch', 'feat')), may hold values from -6 to 6
Outputs:
- edge_out: bfloat16 [262144, 512], P(('patch', 'feat'))
- node_out: bfloat16 [32768, 512], P(('patch', 'feat'))
- node_grad: float32 [32768, 512], P(('patch', 'feat'))
- edge_grad: bfloat16 [262144, 512], P(('patch', 'feat'))
- edge_w1_grad: float32 [3, 512, 512], P(None, None, 'feat')
- edge_w2_grad: float32 [512, 512], P('feat')
- node_w1_grad: float32 [2, 512, 512], P(None, None, 'feat')
- node_w2_grad: float32 [512, 512], P('feat')
The draws below stay inside these ranges and needn't reach their ends.
Inputs may be any that keep to these rules, and one draw needn't show every extreme that they name: `edge_src`: below 256: a node of the device; then 32 rows from the previous device, 32 rows from the next device, then the 512 coarse rows, all in the order of the lookup. `edge_count`: A multiple of 128; the first that many edge slots of the device are live, the others are padding; some device is full. `halo_send`: node rows of the device; list 0 goes to the previous device, list 1 to the next. `coarse_of`: node rows of the device. `edge_dst`: A node row of the device.
All inputs are finite; a program needn't handle non-finite values.
Results may differ from the reference program's by a relative error of at most 0.013.
Values may be sent and summed in bfloat16 or wider, within the bound.
No kernel may reach another device: no remote copies, remote signals or barrier semaphores. Data moves between devices by JAX's collectives and lax.ppermute only.
A program may use at most 128 MiB of HBM per device.

```python
import jax
import jax.numpy as jnp
from jax import lax

D = 512
INNER = 512
EDGE_DEV = 2048
NODE_DEV = 256
HALO = 32
COARSE_DEV = 4
NDEV = 128
NODES = 32768
EDGES = 262144
COARSE = 512


def draw_edge_src(key, part):
    key = jax.random.fold_in(key, 11)
    kind_key, local_key, halo_key, coarse_key = jax.random.split(key, 4)
    kinds = jax.random.randint(kind_key, (EDGES,), 0, 8)
    local_pick = jax.random.randint(local_key, (EDGES,), 0, NODE_DEV)
    halo_pick = jax.random.randint(halo_key, (EDGES,), 0, HALO)
    coarse_pick = jax.random.randint(coarse_key, (EDGES,), 0, COARSE)
    chosen = jnp.where(kinds == 0, NODE_DEV + halo_pick, jnp.where(kinds == 1, NODE_DEV + HALO + halo_pick, jnp.where(kinds == 2, NODE_DEV + 2 * HALO + coarse_pick, local_pick)))
    return chosen.astype(jnp.int32)


def draw_edge_count(key, part):
    key = jax.random.fold_in(key, 23)
    block_key, full_key = jax.random.split(key, 2)
    block_total = EDGE_DEV // 128
    lowest = max(1, block_total // 4)
    blocks = jax.random.randint(block_key, (NDEV,), lowest, block_total + 1)
    full_device = jax.random.randint(full_key, (), 0, NDEV)
    blocks = jnp.where(jnp.arange(NDEV) == full_device, block_total, blocks)
    return (blocks * 128).astype(jnp.int32)


def plant(array, rng, smallest, high):
    longest = array.shape.index(max(array.shape))
    spots = []
    for shift in (0, 1):
        where = [jax.random.randint(jax.random.fold_in(rng, axis), (), 0, length) for axis, length in enumerate(array.shape)]
        where[longest] = (where[longest] + shift) % array.shape[longest]
        spots.append(tuple(where))
    return array.at[spots[0]].set(smallest).at[spots[1]].set(high)


def shard_levels(stream_key, extent, shards, least, top_value):
    loudness, own = 1.0, jax.random.fold_in(stream_key, 6)
    for dim, parts in shards:
        heights = jnp.exp(jax.random.uniform(jax.random.fold_in(own, dim), (parts,), jnp.float32, least / len(shards), top_value / len(shards)))
        loudness = loudness * jnp.repeat(heights, extent[dim] // parts).reshape([-1 if axis == dim else 1 for axis in range(len(extent))])
    return loudness


def noise(key, extent, deviation, limit, cuts=(), dtype=jnp.bfloat16):
    level = shard_levels(key, extent, cuts, -0.22, 0.18) if cuts else 1.0
    array = jax.random.normal(key, extent, jnp.float32) * deviation * level
    return jnp.minimum(jnp.maximum(array, -limit), limit).astype(dtype)


def setup_inputs(seed: int = 0) -> dict:
    key_of = jax.random.split(jax.random.key(seed), 14)
    node_lat = noise(key_of[0], (NODES, D), 1.0, 6.0, ((0, 128),))
    edge_lat = noise(key_of[1], (EDGES, D), 1.0, 6.0, ((0, 128),))
    edge_src = draw_edge_src(jax.random.fold_in(key_of[13], 71), 0)
    edge_dst = plant(jax.random.randint(key_of[3], (EDGES,), 0, NODE_DEV), jax.random.fold_in(key_of[3], 1), 0, NODE_DEV - 1).astype(jnp.int32)
    edge_count = draw_edge_count(jax.random.fold_in(key_of[13], 71), 0)
    halo_send = plant(jax.random.randint(key_of[5], (NDEV, 2, HALO), 0, NODE_DEV), jax.random.fold_in(key_of[5], 1), 0, NODE_DEV - 1).astype(jnp.int32)
    coarse_of = plant(jax.random.randint(key_of[6], (NDEV, COARSE_DEV), 0, NODE_DEV), jax.random.fold_in(key_of[6], 1), 0, NODE_DEV - 1).astype(jnp.int32)
    edge_w1 = noise(key_of[7], (3, D, INNER), (3 * D) ** -0.5, 0.15625, ((2, 4),))
    edge_w2 = noise(key_of[8], (INNER, D), INNER ** -0.5, 0.25, ((0, 4),))
    node_w1 = noise(key_of[9], (2, D, INNER), (2 * D) ** -0.5, 0.1875, ((2, 4),))
    node_w2 = noise(key_of[10], (INNER, D), INNER ** -0.5, 0.25, ((0, 4),))
    grad_node = noise(key_of[11], (NODES, D), 1.0, 6.0, ((0, 128),))
    grad_edge = noise(key_of[12], (EDGES, D), 1.0, 6.0, ((0, 128),))
    return {"node_lat": node_lat, "edge_lat": edge_lat, "edge_src": edge_src, "edge_dst": edge_dst, "edge_count": edge_count, "halo_send": halo_send, "coarse_of": coarse_of, "edge_w1": edge_w1, "edge_w2": edge_w2, "node_w1": node_w1, "node_w2": node_w2, "grad_node": grad_node, "grad_edge": grad_edge}


EPSILON = 1e-05

def product(left, right):
    return jnp.dot(left, right, preferred_element_type=jnp.float32)

def contract_rows(left, right):
    return lax.dot_general(left, right, (((0,), (0,)), ((), ())), preferred_element_type=jnp.float32)

def times_transposed(left, right):
    return lax.dot_general(left, right, (((1,), (1,)), ((), ())), preferred_element_type=jnp.float32)

def normalize(values):
    centre = values - lax.optimization_barrier(jnp.mean(values, axis=-1, keepdims=True))
    factor = lax.rsqrt(lax.optimization_barrier(jnp.mean(centre * centre, axis=-1, keepdims=True)) + EPSILON)
    return (centre * factor, factor)

def normalize_back(upstream, normed, factor):
    first_mean = lax.optimization_barrier(jnp.mean(upstream, axis=-1, keepdims=True))
    second_mean = lax.optimization_barrier(jnp.mean(upstream * normed, axis=-1, keepdims=True))
    return factor * (upstream - first_mean - normed * second_mean)

def swish_slope(values):
    sigmoid = jax.nn.sigmoid(values)
    return sigmoid * (1.0 + values * (1.0 - sigmoid))

def local_step(node_rows, lookup_table, edge_rows, senders, receivers, live_count, upstream_node, upstream_edge, edge_first, edge_second, node_first, node_second):
    node_number = node_rows.shape[0]
    sender_rows = lookup_table[senders]
    receiver_rows = node_rows[receivers]
    edge_pre = product(edge_rows, edge_first[0]) + product(sender_rows, edge_first[1]) + product(receiver_rows, edge_first[2])
    edge_act = jax.nn.silu(edge_pre).astype(jnp.bfloat16)
    edge_normed, edge_factor = normalize(product(edge_act, edge_second))
    active = (jnp.arange(edge_rows.shape[0]) < live_count).astype(jnp.float32)[:, None]
    edge_new = (edge_rows.astype(jnp.float32) + active * edge_normed).astype(jnp.bfloat16)
    incoming = jax.ops.segment_sum(active * edge_new.astype(jnp.float32), receivers, num_segments=node_number).astype(jnp.bfloat16)
    node_pre = product(node_rows, node_first[0]) + product(incoming, node_first[1])
    node_act = jax.nn.silu(node_pre).astype(jnp.bfloat16)
    node_normed, node_factor = normalize(product(node_act, node_second))
    node_new = (node_rows.astype(jnp.float32) + node_normed).astype(jnp.bfloat16)
    upstream = upstream_node.astype(jnp.float32)
    node_delta = normalize_back(upstream, node_normed, node_factor).astype(jnp.bfloat16)
    grad_node_second = contract_rows(node_act, node_delta)
    node_pre_grad = (times_transposed(node_delta, node_second) * swish_slope(node_pre)).astype(jnp.bfloat16)
    grad_node_first = jnp.stack([contract_rows(node_rows, node_pre_grad), contract_rows(incoming, node_pre_grad)])
    node_total = upstream + times_transposed(node_pre_grad, node_first[0])
    incoming_grad = times_transposed(node_pre_grad, node_first[1])
    edge_total = upstream_edge.astype(jnp.float32) + active * incoming_grad[receivers]
    edge_delta = normalize_back(active * edge_total, edge_normed, edge_factor).astype(jnp.bfloat16)
    grad_edge_second = contract_rows(edge_act, edge_delta)
    edge_pre_grad = (times_transposed(edge_delta, edge_second) * swish_slope(edge_pre)).astype(jnp.bfloat16)
    grad_edge_first = jnp.stack([contract_rows(edge_rows, edge_pre_grad), contract_rows(sender_rows, edge_pre_grad), contract_rows(receiver_rows, edge_pre_grad)])
    edge_out_grad = (edge_total + times_transposed(edge_pre_grad, edge_first[0])).astype(jnp.bfloat16)
    node_total = node_total + jax.ops.segment_sum(times_transposed(edge_pre_grad, edge_first[2]), receivers, num_segments=node_number)
    lookup_grad = jax.ops.segment_sum(times_transposed(edge_pre_grad, edge_first[1]), senders, num_segments=lookup_table.shape[0])
    node_total = node_total + lookup_grad[:node_number]
    return (edge_new, node_new, edge_out_grad, node_total, lookup_grad[node_number:], (grad_edge_first, grad_edge_second, grad_node_first, grad_node_second))

def reference(node_lat, edge_lat, edge_src, edge_dst, edge_count, halo_send, coarse_of, edge_w1, edge_w2, node_w1, node_w2, grad_node, grad_edge):
    node_blocks = node_lat.reshape(NDEV, NODE_DEV, D)
    pick_rows = jax.vmap(lambda block_rows, positions: block_rows[positions])
    to_prev = pick_rows(node_blocks, halo_send[:, 0])
    to_next = pick_rows(node_blocks, halo_send[:, 1])
    from_prev = jnp.roll(to_next, 1, axis=0)
    from_next = jnp.roll(to_prev, -1, axis=0)
    coarse_rows = pick_rows(node_blocks, coarse_of).reshape(COARSE, D)

    def visit(running, inputs):
        weight_sums, coarse_grad = running
        node_rows, prev_rows, next_rows, edge_rows, senders, receivers, live_count, upstream_node, upstream_edge = inputs
        lookup_table = jnp.concatenate([node_rows, prev_rows, next_rows, coarse_rows], axis=0)
        edge_new, node_new, edge_out_grad, node_total, remote_grad, weight_grads = local_step(node_rows, lookup_table, edge_rows, senders, receivers, live_count, upstream_node, upstream_edge, edge_w1, edge_w2, node_w1, node_w2)
        weight_sums = jax.tree.map(jnp.add, weight_sums, weight_grads)
        coarse_grad = coarse_grad + remote_grad[2 * HALO:]
        return ((weight_sums, coarse_grad), (edge_new, node_new, edge_out_grad, node_total, remote_grad[:HALO], remote_grad[HALO:2 * HALO]))
    start_sums = (jnp.zeros((3, D, INNER), jnp.float32), jnp.zeros((INNER, D), jnp.float32), jnp.zeros((2, D, INNER), jnp.float32), jnp.zeros((INNER, D), jnp.float32))
    inputs = (node_blocks, from_prev, from_next, edge_lat.reshape(NDEV, EDGE_DEV, D), edge_src.reshape(NDEV, EDGE_DEV), edge_dst.reshape(NDEV, EDGE_DEV), edge_count, grad_node.reshape(NDEV, NODE_DEV, D), grad_edge.reshape(NDEV, EDGE_DEV, D))
    (weight_sums, coarse_grad), outputs = lax.scan(visit, (start_sums, jnp.zeros((COARSE, D), jnp.float32)), inputs)
    edge_new, node_new, edge_out_grad, node_total, prev_back, next_back = outputs
    add_rows = jax.vmap(lambda target, positions, values: target.at[positions].add(values))
    node_total = add_rows(node_total, halo_send[:, 1], jnp.roll(prev_back, -1, axis=0))
    node_total = add_rows(node_total, halo_send[:, 0], jnp.roll(next_back, 1, axis=0))
    node_total = add_rows(node_total, coarse_of, coarse_grad.reshape(NDEV, COARSE_DEV, D))
    return (edge_new.reshape(EDGES, D), node_new.reshape(NODES, D), node_total.reshape(NODES, D), edge_out_grad.reshape(EDGES, D), weight_sums[0], weight_sums[1], weight_sums[2], weight_sums[3])
```

```python
import jax
import jax.numpy as jnp
from jax import lax
from jax.experimental import pallas as pl
from jax.experimental.pallas import tpu as pltpu
from jax.sharding import PartitionSpec as P

EPSILON = 1e-05
BF16 = jnp.bfloat16
F32 = jnp.float32
BOTH = ("patch", "feat")
CHUNK = 512
STEPS = 4
TABLE = 896
VMEM_BYTES = 60 * 1024 * 1024


def send(value, dz=0, dx=0, dc=0, dy=0):
    pairs = []
    for z in range(4):
        for x in range(4):
            for c in range(2):
                for y in range(4):
                    source = ((z * 4 + x) * 2 + c) * 4 + y
                    target = (((z + dz) % 4 * 4 + (x + dx) % 4) * 2 + (c ^ dc)) * 4 + (y + dy) % 4
                    pairs.append((source, target))
    return lax.ppermute(value, BOTH, pairs)


def shifted(value, steps):
    return lax.ppermute(value, BOTH, [(k, (k + steps) % 128) for k in range(128)])


def dot(left, right):
    return lax.dot_general(left, right, (((1,), (0,)), ((), ())), preferred_element_type=F32)


def dot_nt(left, right):
    return lax.dot_general(left, right, (((1,), (1,)), ((), ())), preferred_element_type=F32)


def dot_tn(left, right):
    return lax.dot_general(left, right, (((0,), (0,)), ((), ())), preferred_element_type=F32)


def mean(values):
    return jnp.mean(values, axis=-1, keepdims=True)


def normalize(values):
    centre = values - mean(values)
    factor = lax.rsqrt(mean(centre * centre) + EPSILON)
    return centre * factor, factor


def normalize_back(upstream, normed, factor):
    return factor * (upstream - mean(upstream) - normed * mean(upstream * normed))


def swish(pre):
    sigmoid = 0.5 + 0.5 * jnp.tanh(0.5 * pre)
    act = pre * sigmoid
    return act, sigmoid + act * (1.0 - sigmoid)


def hot_tiles(rows, count):
    lanes = lax.broadcasted_iota(jnp.int32, (128, 128), 1)
    spread = jnp.transpose(jnp.broadcast_to(rows, (128, 128)))
    return [jnp.where(spread == lanes + 128 * j, 1.0, 0.0).astype(BF16) for j in range(count)]


def live_rows(step, count):
    place = lax.broadcasted_iota(jnp.int32, (CHUNK, 1), 0) + step * CHUNK
    return jnp.where(place < count, 1.0, 0.0)


def place_weights(co, own_first, own_second, near, far, first, second):
    core, y = co[2], co[3]
    kinds = first.shape[0]
    for s in range(4):
        yy = (y - s) & 3
        columns = pl.ds(pl.multiple_of(yy * 128, 128), 128)
        if s == 0:
            for m in range(kinds):
                first[m, :, columns] = own_first[m]
            second[columns, :] = own_second[...]
            continue
        for part, half in ((near[s - 1], core), (far[s - 1], 1 - core)):
            rows = pl.ds(pl.multiple_of(half * 256, 256), 256)
            for m in range(kinds):
                first[m, rows, columns] = part[m * 256 : (m + 1) * 256, :]
            rows = pl.ds(pl.multiple_of(yy * 128 + half * 64, 64), 64)
            for b in range(4):
                start = kinds * 256 + b * 64
                second[rows, b * 128 : (b + 1) * 128] = part[start : start + 64, :]


def forward_kernel(co, node, prev, after, *refs):
    coarse, refs = refs[:16], refs[16:]
    own_first, own_second = refs[:2]
    near, far = refs[2:5], refs[5:8]
    src, dst, dst_wide, edge = refs[8:12]
    edge_out, incoming, act_out, normed_out, slope_out, factor_out, lookup, first, second = refs[12:21]
    table, total = refs[21:]
    step = pl.program_id(0)

    @pl.when(step == 0)
    def _():
        lookup[0:256, :] = node[...]
        lookup[256:288, :] = prev[...]
        lookup[288:320, :] = after[...]
        lookup[832:896, :] = jnp.zeros((64, 512), BF16)
        for dz in range(4):
            for dx in range(4):
                place = ((co[0] - dz) & 3) * 4 + ((co[1] - dx) & 3)
                rows = pl.ds(pl.multiple_of(320 + place * 32, 32), 32)
                lookup[rows, :] = coarse[dz * 4 + dx][...]
        place_weights(co, own_first, own_second, near, far, first, second)
        table[0:TABLE, :] = dot(lookup[...], first[1]).astype(BF16)
        table[TABLE:, :] = dot(node[...], first[2]).astype(BF16)
        total[...] = jnp.zeros_like(total)

    hots = []
    for r in range(CHUNK // 128):
        row = pl.ds(step * (CHUNK // 128) + r, 1)
        tiles = hot_tiles(src[row, :], TABLE // 128) + hot_tiles(dst[row, :], 2)
        hots.append(jnp.concatenate(tiles, axis=1))
    hot = jnp.concatenate(hots, axis=0)
    rows = edge[...]
    pre = dot(rows, first[0]) + dot(hot, table[...])
    act, slope = swish(pre)
    act = act.astype(BF16)
    act_out[...] = act
    slope_out[...] = slope.astype(BF16)
    normed, factor = normalize(dot(act, second[...]))
    normed_out[...] = normed.astype(BF16)
    factor_out[...] = jnp.broadcast_to(factor, (CHUNK, 128))
    new = (rows.astype(F32) + live_rows(step, co[4]) * normed).astype(BF16)
    edge_out[...] = new
    place = lax.broadcasted_iota(jnp.int32, (256, CHUNK), 1) + step * CHUNK
    node_of = lax.broadcasted_iota(jnp.int32, (256, CHUNK), 0)
    match = (node_of == dst_wide[pl.ds(step, 1), :]) & (place < co[4])
    total[...] += dot(jnp.where(match, 1.0, 0.0).astype(BF16), new)

    @pl.when(step == STEPS - 1)
    def _():
        incoming[...] = total[...].astype(BF16)


def put_columns(co, grad, slot, scratch, keep, give):
    scratch[...] = grad.astype(BF16).reshape(16, 2, 16, 512)
    for target, core in ((keep, co[2]), (give, 1 - co[2])):
        value = scratch[:, pl.ds(core, 1), :, :].reshape(8, 2, 16, 512)
        for y in range(4):
            target[:, :, y, slot * 16 : (slot + 1) * 16, :] = value[:, :, :, y * 128 : (y + 1) * 128]


def put_rows(co, grad, slot, scratch, keep, give):
    for b in range(4):
        scratch[b] = grad[:, b * 128 : (b + 1) * 128].astype(BF16)
    for target, core in ((keep, co[2]), (give, 1 - co[2])):
        for h in range(2):
            value = scratch[2 * h + core].reshape(4, 8, 16, 128)
            for y in range(4):
                target[:, h, y, slot * 16 : (slot + 1) * 16, :] = value[y]


def backward_kernel(co, node, incoming, grad_node, own_first, own_second, *refs):
    near, far, refs = refs[:3], refs[3:6], refs[6:]
    edge_first, edge_second, lookup, dst, src_wide, dst_wide = refs[:6]
    edge, act, normed, slope, factor, grad_edge = refs[6:12]
    node_out, node_total, edge_grad, to_prev, to_next, keep, give = refs[12:19]
    first, second, spread, sum_second, sum_first, sums, columns, rows = refs[19:]
    step = pl.program_id(0)

    @pl.when(step == 0)
    def _():
        place_weights(co, own_first, own_second, near, far, first, second)
        lat, summed = node[...], incoming[...]
        pre = dot(lat, first[0]) + dot(summed, first[1])
        node_act, node_slope = swish(pre)
        node_act = node_act.astype(BF16)
        node_normed, node_factor = normalize(dot(node_act, second[...]))
        node_out[...] = (lat.astype(F32) + node_normed).astype(BF16)
        upstream = grad_node[...].astype(F32)
        delta = normalize_back(upstream, node_normed, node_factor).astype(BF16)
        put_rows(co, dot_tn(node_act, delta), 7, rows, keep, give)
        pre_grad = (dot_nt(delta, second[...]) * node_slope).astype(BF16)
        put_columns(co, dot_tn(lat, pre_grad), 3, columns, keep, give)
        put_columns(co, dot_tn(summed, pre_grad), 4, columns, keep, give)
        node_total[...] = upstream + dot_nt(pre_grad, first[0])
        spread[...] = dot_nt(pre_grad, first[1]).astype(BF16)
        sum_second[...] = jnp.zeros_like(sum_second)
        sum_first[...] = jnp.zeros_like(sum_first)
        sums[...] = jnp.zeros_like(sums)

    hots = []
    for r in range(CHUNK // 128):
        row = pl.ds(step * (CHUNK // 128) + r, 1)
        hots.append(jnp.concatenate(hot_tiles(dst[row, :], 2), axis=1))
    live = live_rows(step, co[4])
    total = grad_edge[...].astype(F32) + live * dot(jnp.concatenate(hots, axis=0), spread[...])
    delta = normalize_back(live * total, normed[...].astype(F32), factor[:, 0:1]).astype(BF16)
    pre_grad = (dot_nt(delta, edge_second[...]) * slope[...].astype(F32)).astype(BF16)
    edge_grad[...] = (total + dot_nt(pre_grad, edge_first[0])).astype(BF16)
    sum_second[...] += dot_tn(act[...], delta)
    sum_first[...] += dot_tn(edge[...], pre_grad)
    place = lax.broadcasted_iota(jnp.int32, (128, CHUNK), 0)
    src_row, dst_row = src_wide[pl.ds(step, 1), :], dst_wide[pl.ds(step, 1), :]
    for j in range(9):
        match = place + 128 * j == src_row if j < 7 else place + 128 * (j - 7) == dst_row
        hot = jnp.where(match, 1.0, 0.0).astype(BF16)
        sums[j * 128 : (j + 1) * 128, :] += dot(hot, pre_grad)

    @pl.when(step == STEPS - 1)
    def _():
        put_rows(co, sum_second[...], 6, rows, keep, give)
        put_columns(co, sum_first[...], 0, columns, keep, give)
        sent = sums[0:TABLE, :].astype(BF16)
        received = sums[TABLE:, :].astype(BF16)
        put_columns(co, dot_tn(lookup[...], sent), 1, columns, keep, give)
        put_columns(co, dot_tn(node[...], received), 2, columns, keep, give)
        back = dot_nt(sent, edge_first[1])
        node_total[...] += back[0:256] + dot_nt(received, edge_first[2])
        to_prev[...] = back[256:288].astype(BF16)
        to_next[...] = back[288:320].astype(BF16)
        put_columns(co, back[320:832], 5, columns, keep, give)


def summed(*values):
    values = [value.astype(F32) for value in values]
    if len(values) == 4:
        return (values[0] + values[2]) + (values[1] + values[3])
    return values[0] + values[1]


def core_kernel(co, keep, got, *outs):
    z, x, y = co[0], co[1], co[3]
    for s in range(4):
        at = (slice(None), slice(None), pl.ds((y + s) & 3, 1), slice(0, 48))
        outs[s][...] = summed(keep[at], got[at]).astype(BF16).reshape(4, 4, 48, 128)
        at = (slice(None), pl.ds((x + s) & 3, 1), slice(None), slice(48, 96))
        outs[4 + s][...] = summed(keep[at], got[at]).astype(BF16).reshape(4, 4, 48, 128)
        at = (pl.ds((z + s) & 3, 1), slice(None), slice(None), slice(96, 128))
        outs[8 + s][...] = summed(keep[at], got[at]).astype(BF16).reshape(4, 4, 32, 128)


def second_kernel(co, *refs):
    one, two, three, outs = refs[:4], refs[4:8], refs[8:12], refs[12:]
    x, y = co[1], co[3]
    for s in range(4):
        at = (slice(None), pl.ds((x + s) & 3, 1))
        outs[s][...] = summed(*[r[at] for r in one]).astype(BF16).reshape(4, 48, 128)
        at = (slice(None), pl.ds((y + s) & 3, 1))
        outs[4 + s][:, 0:48, :] = summed(*[r[at] for r in two]).astype(BF16).reshape(4, 48, 128)
        outs[4 + s][:, 48:80, :] = summed(*[r[at] for r in three]).astype(BF16).reshape(4, 32, 128)


def third_kernel(*refs):
    one, two, (wide, narrow) = refs[:4], refs[4:8], refs[8:]
    wide[:, 0:48, :] = summed(*[r[...] for r in one]).astype(BF16)
    value = summed(*[r[...] for r in two]).astype(BF16)
    wide[:, 48:96, :] = value[:, 0:48]
    narrow[...] = value[:, 48:80]


def fourth_kernel(co, *refs):
    one, two, (wide, narrow, coarse) = refs[:4], refs[4:8], refs[8:]
    wide[...] = summed(*[r[:, 0:80, :] for r in one]).astype(BF16)
    narrow[...] = summed(*[r[...] for r in two]).astype(BF16)
    at = (pl.ds(co[0], 1), slice(80, 96))
    coarse[...] = summed(*[r[at] for r in one]).astype(BF16).reshape(16, 128)


def final_kernel(co, *refs):
    wide, narrow, coarse, refs = refs[:8], refs[8:16], refs[16:20], refs[20:]
    ahead, behind, targets, node_total = refs[:4]
    edge_first, edge_second, node_first, node_second, node_grad = refs[4:9]
    blocks, rows = refs[9:]
    z, x, core, y = co[0], co[1], co[2], co[3]
    for dc in range(2):
        cc = core ^ dc
        for d in range(4):
            piece = wide[dc * 4 + d][...].astype(F32)
            xx = (x - d) & 3
            for m in range(5):
                value = piece[:, m * 16 : (m + 1) * 16].reshape(4, 1, 1, 16, 128)
                target = edge_first if m < 3 else node_first
                target[m if m < 3 else m - 3, :, pl.ds(xx, 1), pl.ds(cc, 1)] = value
            piece = narrow[dc * 4 + d][...].astype(F32)
            zz = (z - d) & 3
            for k in range(2):
                for xs in range(4):
                    value = piece[xs, k * 16 : (k + 1) * 16]
                    blocks[k, zz * 2 + xs // 2, (xs % 2) * 2 + cc] = value
    for k, target in enumerate((edge_second, node_second)):
        for r in range(8):
            for b in range(4):
                target[r * 16 : (r + 1) * 16, b * 128 : (b + 1) * 128] = blocks[k, r, b]
    rows[0:32, :] = ahead[...]
    rows[32:64, :] = behind[...]
    for d in range(4):
        columns = pl.ds(pl.multiple_of(((y - d) & 3) * 128, 128), 128)
        rows[64:80, columns] = coarse[d][...]
    rows[80:128, :] = jnp.zeros((48, 512), BF16)
    match = lax.broadcasted_iota(jnp.int32, (256, 128), 0) == targets[...]
    hot = jnp.where(match, 1.0, 0.0).astype(BF16)
    node_grad[...] = node_total[...] + dot(hot, rows[...])


SMEM = pl.BlockSpec(memory_space=pltpu.SMEM)
WHOLE = pl.BlockSpec(memory_space=pltpu.VMEM)


def shape(*dims, dtype=BF16):
    return jax.ShapeDtypeStruct(dims, dtype)


def plain_call(kernel, scalars, operands, outs, scratch=()):
    return pl.pallas_call(
        kernel,
        in_specs=[SMEM] * len(scalars) + [WHOLE] * len(operands),
        out_specs=[WHOLE] * len(outs),
        out_shape=list(outs),
        scratch_shapes=list(scratch),
        compiler_params=pltpu.CompilerParams(vmem_limit_bytes=VMEM_BYTES),
    )(*scalars, *operands)


def same(*dims):
    return pl.BlockSpec(dims, lambda i: (0,) * len(dims))


def chunk(*dims):
    return pl.BlockSpec(dims, lambda i: (i,) + (0,) * (len(dims) - 1))


def like(value):
    return same(*value.shape)


def halves(first, second, core):
    kinds = first.shape[0]
    top = lax.dynamic_slice_in_dim(first, core * 256, 256, 1).reshape(kinds * 256, 128)
    rest = lax.dynamic_slice_in_dim(second, core * 64, 64, 0)
    rest = rest.reshape(64, 4, 128).transpose(1, 0, 2).reshape(256, 128)
    return jnp.concatenate([top, rest], axis=0)


def shards(
    node_lat,
    edge_lat,
    edge_src,
    edge_dst,
    edge_count,
    halo_send,
    coarse_of,
    edge_w1,
    edge_w2,
    node_w1,
    node_w2,
    grad_node,
    grad_edge,
):
    patch, y = lax.axis_index("patch"), lax.axis_index("feat")
    z, x, core = patch // 8, (patch // 2) % 4, patch % 2
    co = jnp.stack([z, x, core, y, edge_count[0]]).astype(jnp.int32)
    lists, owned = halo_send[0], coarse_of[0]
    mine = jnp.where(jnp.arange(16) // 4 == y, jnp.tile(owned, 4), -1)
    unused = jnp.full((48,), -1, jnp.int32)
    targets = jnp.concatenate([lists[1], lists[0], mine, unused]).reshape(1, 128)

    edge_half = halves(edge_w1, edge_w2, core)
    edge_near = [send(edge_half, dy=s) for s in (1, 2, 3)]
    coarse_own = node_lat[owned]
    others = [(dc, dy) for dc in range(2) for dy in range(4)]
    pieces = [coarse_own if o == (0, 0) else send(coarse_own, dc=o[0], dy=o[1]) for o in others]
    from_prev = shifted(node_lat[lists[1]], 1)
    from_next = shifted(node_lat[lists[0]], -1)
    edge_far = [send(part, dc=1) for part in edge_near]
    place = jnp.arange(32, dtype=jnp.int32)
    wanted = ((place // 16) ^ core) * 16 + ((y - (place // 4) % 4) % 4) * 4 + place % 4
    order = (wanted[:, None] == place[None, :]).astype(BF16)
    block = dot(order, jnp.concatenate(pieces, axis=0)).astype(BF16)
    blocks = [
        block if (dz, dx) == (0, 0) else send(block, dz=dz, dx=dx)
        for dz in range(4)
        for dx in range(4)
    ]
    node_half = halves(node_w1, node_w2, core)
    node_near = [send(node_half, dy=s) for s in (1, 2, 3)]
    node_far = [send(part, dc=1) for part in node_near]

    src, dst = edge_src.reshape(16, 128), edge_dst.reshape(16, 128)
    src_wide, dst_wide = edge_src.reshape(STEPS, CHUNK), edge_dst.reshape(STEPS, CHUNK)
    fixed = [node_lat, from_prev, from_next, *blocks, edge_w1, edge_w2, *edge_near, *edge_far]
    fixed += [src, dst, dst_wide]
    wide = chunk(CHUNK, 512)
    params = pltpu.CompilerParams(vmem_limit_bytes=VMEM_BYTES, dimension_semantics=("arbitrary",))
    edge_out, incoming, act, normed, slope, factor, lookup, first, second = pl.pallas_call(
        forward_kernel,
        grid=(STEPS,),
        in_specs=[SMEM] + [like(v) for v in fixed] + [wide],
        out_specs=[wide, same(256, 512), wide, wide, wide, chunk(CHUNK, 128)]
        + [same(TABLE, 512), same(3, 512, 512), same(512, 512)],
        out_shape=[
            shape(2048, 512),
            shape(256, 512),
            shape(2048, 512),
            shape(2048, 512),
            shape(2048, 512),
            shape(2048, 128, dtype=F32),
            shape(TABLE, 512),
            shape(3, 512, 512),
            shape(512, 512),
        ],
        scratch_shapes=[pltpu.VMEM((TABLE + 256, 512), BF16), pltpu.VMEM((256, 512), F32)],
        compiler_params=params,
        cost_estimate=pl.CostEstimate(
            flops=7_000_000_000, bytes_accessed=18_000_000, transcendentals=1_000_000
        ),
    )(co, *fixed, edge_lat)

    fixed = [node_lat, incoming, grad_node, node_w1, node_w2, *node_near, *node_far]
    fixed += [first, second, lookup, dst, src_wide, dst_wide]
    moving = [edge_lat, act, normed, slope, factor, grad_edge]
    tiles = (8, 2, 4, 128, 128)
    node_out, node_total, edge_grad, to_prev, to_next, keep, give = pl.pallas_call(
        backward_kernel,
        grid=(STEPS,),
        in_specs=[SMEM]
        + [like(v) for v in fixed]
        + [wide, wide, wide, wide, chunk(CHUNK, 128), wide],
        out_specs=[same(256, 512), same(256, 512), wide, same(32, 512), same(32, 512)]
        + [same(*tiles), same(*tiles)],
        out_shape=[
            shape(256, 512),
            shape(256, 512, dtype=F32),
            shape(2048, 512),
            shape(32, 512),
            shape(32, 512),
            shape(*tiles),
            shape(*tiles),
        ],
        scratch_shapes=[
            pltpu.VMEM((2, 512, 512), BF16),
            pltpu.VMEM((512, 512), BF16),
            pltpu.VMEM((256, 512), BF16),
            pltpu.VMEM((512, 512), F32),
            pltpu.VMEM((512, 512), F32),
            pltpu.VMEM((TABLE + 256, 512), F32),
            pltpu.VMEM((16, 2, 16, 512), BF16),
            pltpu.VMEM((4, 512, 128), BF16),
        ],
        compiler_params=params,
        cost_estimate=pl.CostEstimate(
            flops=9_000_000_000, bytes_accessed=24_000_000, transcendentals=100_000
        ),
    )(co, *fixed, *moving)

    ahead = shifted(to_prev, -1)
    behind = shifted(to_next, 1)
    got = send(give, dc=1)
    sizes = [shape(4, 4, rows, 128) for rows in (48, 48, 32) for _ in range(4)]
    cube = (4, 4, 4, 128, 128)
    outs = plain_call(core_kernel, [co], [keep.reshape(cube), got.reshape(cube)], sizes)
    along = (dict(dy=1), dict(dx=1), dict(dz=1))
    held = []
    for part, step in enumerate(along):
        (axis,) = step
        held.append(outs[4 * part])
        held += [send(outs[4 * part + s], **{axis: s}) for s in (1, 2, 3)]
    sizes = [shape(4, rows, 128) for rows in (48, 80) for _ in range(4)]
    outs = plain_call(second_kernel, [co], held, sizes)
    held = [outs[0]] + [send(outs[s], dx=s) for s in (1, 2, 3)]
    held += [outs[4]] + [send(outs[4 + s], dy=s) for s in (1, 2, 3)]
    major, minor = plain_call(third_kernel, [], held, [shape(4, 96, 128), shape(4, 32, 128)])
    held = [major] + [send(major, dz=s) for s in (1, 2, 3)]
    held += [minor] + [send(minor, dx=s) for s in (1, 2, 3)]
    major, minor, coarse = plain_call(
        fourth_kernel, [co], held, [shape(4, 80, 128), shape(4, 32, 128), shape(16, 128)]
    )
    held = [
        major if (dc, d) == (0, 0) else send(major, dc=dc, dx=d)
        for dc in range(2)
        for d in range(4)
    ]
    held += [
        minor if (dc, d) == (0, 0) else send(minor, dc=dc, dz=d)
        for dc in range(2)
        for d in range(4)
    ]
    held += [coarse] + [send(coarse, dy=s) for s in (1, 2, 3)]
    edge_first, edge_second, node_first, node_second, node_grad = plain_call(
        final_kernel,
        [co],
        held + [ahead, behind, targets, node_total],
        [
            shape(3, 4, 4, 2, 16, 128, dtype=F32),
            shape(128, 512, dtype=F32),
            shape(2, 4, 4, 2, 16, 128, dtype=F32),
            shape(128, 512, dtype=F32),
            shape(256, 512, dtype=F32),
        ],
        [
            pltpu.VMEM((2, 8, 4, 16, 128), F32),
            pltpu.VMEM((128, 512), BF16),
        ],
    )
    return (
        edge_out,
        node_out,
        node_grad,
        edge_grad,
        edge_first.reshape(3, 512, 128),
        edge_second,
        node_first.reshape(2, 512, 128),
        node_second,
    )


def solution(mesh):
    rows = P(("patch", "feat"), None)
    flat = P(("patch", "feat"))
    first, second = P(None, None, "feat"), P("feat", None)
    return jax.shard_map(
        shards,
        mesh=mesh,
        in_specs=(
            rows,
            rows,
            flat,
            flat,
            flat,
            P(("patch", "feat"), None, None),
            rows,
            first,
            second,
            first,
            second,
            rows,
            rows,
        ),
        out_specs=(rows, rows, rows, rows, first, second, first, second),
        check_vma=False,
    )
```

```python
import jax
import jax.numpy as jnp
from jax import lax
from jax.experimental import pallas as pl
from jax.experimental.pallas import tpu as pltpu
from jax.sharding import Mesh
from jax.sharding import PartitionSpec as P

EPSILON = 1e-05
BF16 = jnp.bfloat16
F32 = jnp.float32
BOTH = ("z", "x", "core", "feat")
CHUNK = 512
STEPS = 4
TABLE = 896
VMEM_BYTES = 60 * 1024 * 1024


def other_core(value):
    return lax.ppermute(value, "core", [(0, 1), (1, 0)])


def shifted(value, steps):
    return lax.ppermute(value, BOTH, [(k, (k + steps) % 128) for k in range(128)])


def exchange(value, axes):
    return lax.all_to_all(value, axes, 0, 0, tiled=True)


def repeated(value, count):
    return jnp.broadcast_to(value[None], (count,) + value.shape)


def dot(left, right):
    return lax.dot_general(left, right, (((1,), (0,)), ((), ())), preferred_element_type=F32)


def dot_nt(left, right):
    return lax.dot_general(left, right, (((1,), (1,)), ((), ())), preferred_element_type=F32)


def dot_tn(left, right):
    return lax.dot_general(left, right, (((0,), (0,)), ((), ())), preferred_element_type=F32)


def mean(values):
    return jnp.mean(values, axis=-1, keepdims=True)


def normalize(values):
    centre = values - mean(values)
    factor = lax.rsqrt(mean(centre * centre) + EPSILON)
    return centre * factor, factor


def normalize_back(upstream, normed, factor):
    return factor * (upstream - mean(upstream) - normed * mean(upstream * normed))


def swish(pre):
    sigmoid = 0.5 + 0.5 * jnp.tanh(0.5 * pre)
    act = pre * sigmoid
    return act, sigmoid + act * (1.0 - sigmoid)


def hot_tiles(rows, count):
    lanes = lax.broadcasted_iota(jnp.int32, (128, 128), 1)
    spread = jnp.transpose(jnp.broadcast_to(rows, (128, 128)))
    return [jnp.where(spread == lanes + 128 * j, 1.0, 0.0).astype(BF16) for j in range(count)]


def live_rows(step, count):
    place = lax.broadcasted_iota(jnp.int32, (CHUNK, 1), 0) + step * CHUNK
    return jnp.where(place < count, 1.0, 0.0)


def place_weights(core, near, far, first, second):
    kinds = first.shape[0]
    for part, half in ((near, core), (far, 1 - core)):
        for y in range(4):
            rows = pl.ds(pl.multiple_of(half * 256, 256), 256)
            for m in range(kinds):
                first[m, rows, y * 128 : (y + 1) * 128] = part[y, m * 256 : (m + 1) * 256, :]
            rows = pl.ds(pl.multiple_of(y * 128 + half * 64, 64), 64)
            for b in range(4):
                start = kinds * 256 + b * 64
                second[rows, b * 128 : (b + 1) * 128] = part[y, start : start + 64, :]


def forward_kernel(co, node, prev, after, coarse, near, far, src, dst, dst_wide, edge, *refs):
    edge_out, incoming, act_out, normed_out, slope_out, factor_out, lookup, first, second = refs[:9]
    table, total = refs[9:]
    step = pl.program_id(0)

    @pl.when(step == 0)
    def _():
        lookup[0:256, :] = node[...]
        lookup[256:288, :] = prev[...]
        lookup[288:320, :] = after[...]
        lookup[832:896, :] = jnp.zeros((64, 512), BF16)
        lookup[320:832, :] = coarse[...]
        place_weights(co[2], near, far, first, second)
        table[0:TABLE, :] = dot(lookup[...], first[1]).astype(BF16)
        table[TABLE:, :] = dot(node[...], first[2]).astype(BF16)
        total[...] = jnp.zeros_like(total)

    hots = []
    for r in range(CHUNK // 128):
        row = pl.ds(step * (CHUNK // 128) + r, 1)
        tiles = hot_tiles(src[row, :], TABLE // 128) + hot_tiles(dst[row, :], 2)
        hots.append(jnp.concatenate(tiles, axis=1))
    hot = jnp.concatenate(hots, axis=0)
    rows = edge[...]
    pre = dot(rows, first[0]) + dot(hot, table[...])
    act, slope = swish(pre)
    act = act.astype(BF16)
    act_out[...] = act
    slope_out[...] = slope.astype(BF16)
    normed, factor = normalize(dot(act, second[...]))
    normed_out[...] = normed.astype(BF16)
    factor_out[...] = jnp.broadcast_to(factor, (CHUNK, 128))
    new = (rows.astype(F32) + live_rows(step, co[4]) * normed).astype(BF16)
    edge_out[...] = new
    place = lax.broadcasted_iota(jnp.int32, (256, CHUNK), 1) + step * CHUNK
    node_of = lax.broadcasted_iota(jnp.int32, (256, CHUNK), 0)
    match = (node_of == dst_wide[pl.ds(step, 1), :]) & (place < co[4])
    total[...] += dot(jnp.where(match, 1.0, 0.0).astype(BF16), new)

    @pl.when(step == STEPS - 1)
    def _():
        incoming[...] = total[...].astype(BF16)


def put_columns(co, grad, slot, scratch, keep, give):
    scratch[...] = grad.astype(BF16).reshape(16, 2, 16, 512)
    for target, core in ((keep, co[2]), (give, 1 - co[2])):
        value = scratch[:, pl.ds(core, 1), :, :].reshape(8, 2, 16, 512)
        for y in range(4):
            target[:, :, y, slot * 16 : (slot + 1) * 16, :] = value[:, :, :, y * 128 : (y + 1) * 128]


def put_rows(co, grad, slot, scratch, keep, give):
    for b in range(4):
        scratch[b] = grad[:, b * 128 : (b + 1) * 128].astype(BF16)
    for target, core in ((keep, co[2]), (give, 1 - co[2])):
        for h in range(2):
            value = scratch[2 * h + core].reshape(4, 8, 16, 128)
            for y in range(4):
                target[:, h, y, slot * 16 : (slot + 1) * 16, :] = value[y]


def put_owned(co, grad, scratch, keep, give):
    rows = grad.reshape(64, 8, 512)
    turned = pltpu.roll(rows, 4, 1)
    low = lax.broadcasted_iota(jnp.int32, (64, 8, 128), 1) < 4
    for odd in range(2):
        left, right = (turned, rows) if odd else (rows, turned)
        parts = [
            jnp.where(low, left[:, :, b : b + 128], right[:, :, b + 128 : b + 256]) for b in (0, 256)
        ]
        tile = jnp.concatenate(parts, axis=1).astype(BF16).reshape(16, 2, 2, 16, 128)
        for pair in range(2):
            scratch[:, :, pair * 2 + odd] = tile[:, :, pair]
    for target, core in ((keep, co[2]), (give, 1 - co[2])):
        value = scratch[:, pl.ds(core, 1)].reshape(8, 2, 4, 16, 128)
        target[:, :, :, 112:128, :] = value


def backward_kernel(co, node, incoming, grad_node, near, far, *refs):
    edge_first, edge_second, lookup, dst, src_wide, dst_wide = refs[:6]
    edge, act, normed, slope, factor, grad_edge = refs[6:12]
    node_out, node_total, edge_grad, to_prev, to_next, keep, give = refs[12:19]
    first, second, spread, sum_second, sum_first, sums, columns, rows, owned = refs[19:]
    step = pl.program_id(0)

    @pl.when(step == 0)
    def _():
        place_weights(co[2], near, far, first, second)
        lat, summed = node[...], incoming[...]
        pre = dot(lat, first[0]) + dot(summed, first[1])
        node_act, node_slope = swish(pre)
        node_act = node_act.astype(BF16)
        node_normed, node_factor = normalize(dot(node_act, second[...]))
        node_out[...] = (lat.astype(F32) + node_normed).astype(BF16)
        upstream = grad_node[...].astype(F32)
        delta = normalize_back(upstream, node_normed, node_factor).astype(BF16)
        put_rows(co, dot_tn(node_act, delta), 6, rows, keep, give)
        pre_grad = (dot_nt(delta, second[...]) * node_slope).astype(BF16)
        put_columns(co, dot_tn(lat, pre_grad), 3, columns, keep, give)
        put_columns(co, dot_tn(summed, pre_grad), 4, columns, keep, give)
        node_total[...] = upstream + dot_nt(pre_grad, first[0])
        spread[...] = dot_nt(pre_grad, first[1]).astype(BF16)
        sum_second[...] = jnp.zeros_like(sum_second)
        sum_first[...] = jnp.zeros_like(sum_first)
        sums[...] = jnp.zeros_like(sums)

    hots = []
    for r in range(CHUNK // 128):
        row = pl.ds(step * (CHUNK // 128) + r, 1)
        hots.append(jnp.concatenate(hot_tiles(dst[row, :], 2), axis=1))
    live = live_rows(step, co[4])
    total = grad_edge[...].astype(F32) + live * dot(jnp.concatenate(hots, axis=0), spread[...])
    delta = normalize_back(live * total, normed[...].astype(F32), factor[:, 0:1]).astype(BF16)
    pre_grad = (dot_nt(delta, edge_second[...]) * slope[...].astype(F32)).astype(BF16)
    edge_grad[...] = (total + dot_nt(pre_grad, edge_first[0])).astype(BF16)
    sum_second[...] += dot_tn(act[...], delta)
    sum_first[...] += dot_tn(edge[...], pre_grad)
    place = lax.broadcasted_iota(jnp.int32, (128, CHUNK), 0)
    src_row, dst_row = src_wide[pl.ds(step, 1), :], dst_wide[pl.ds(step, 1), :]
    for j in range(9):
        match = place + 128 * j == src_row if j < 7 else place + 128 * (j - 7) == dst_row
        hot = jnp.where(match, 1.0, 0.0).astype(BF16)
        sums[j * 128 : (j + 1) * 128, :] += dot(hot, pre_grad)

    @pl.when(step == STEPS - 1)
    def _():
        put_rows(co, sum_second[...], 5, rows, keep, give)
        put_columns(co, sum_first[...], 0, columns, keep, give)
        sent = sums[0:TABLE, :].astype(BF16)
        received = sums[TABLE:, :].astype(BF16)
        put_columns(co, dot_tn(lookup[...], sent), 1, columns, keep, give)
        put_columns(co, dot_tn(node[...], received), 2, columns, keep, give)
        back = dot_nt(sent, edge_first[1])
        node_total[...] += back[0:256] + dot_nt(received, edge_first[2])
        to_prev[...] = back[256:288].astype(BF16)
        to_next[...] = back[288:320].astype(BF16)
        put_owned(co, back[320:832], owned, keep, give)


def final_kernel(tiles, own, ahead, behind, targets, node_total, *refs):
    edge_first, edge_second, node_first, node_second, node_grad, rows = refs
    for m in range(5):
        value = tiles[:, m * 16 : (m + 1) * 16, :].astype(F32)
        if m < 3:
            edge_first[m] = value
        else:
            node_first[m - 3] = value
    for p in range(32):
        r, b = p // 4 * 16, p % 4 * 128
        edge_second[r : r + 16, b : b + 128] = tiles[p, 80:96, :].astype(F32)
        node_second[r : r + 16, b : b + 128] = tiles[p, 96:112, :].astype(F32)
    rows[0:32, :] = ahead[...]
    rows[32:64, :] = behind[...]
    group = lax.broadcasted_iota(jnp.int32, (16, 128), 0) // 4
    for b in range(4):
        value = jnp.where(group == b, own[112:128, :].astype(F32), 0.0)
        rows[64:80, b * 128 : (b + 1) * 128] = value.astype(BF16)
    rows[80:128, :] = jnp.zeros((48, 512), BF16)
    match = lax.broadcasted_iota(jnp.int32, (256, 128), 0) == targets[...]
    hot = jnp.where(match, 1.0, 0.0).astype(BF16)
    node_grad[...] = node_total[...] + dot(hot, rows[...])


SMEM = pl.BlockSpec(memory_space=pltpu.SMEM)
WHOLE = pl.BlockSpec(memory_space=pltpu.VMEM)


def shape(*dims, dtype=BF16):
    return jax.ShapeDtypeStruct(dims, dtype)


def plain_call(kernel, scalars, operands, outs, scratch=()):
    return pl.pallas_call(
        kernel,
        in_specs=[SMEM] * len(scalars) + [WHOLE] * len(operands),
        out_specs=[WHOLE] * len(outs),
        out_shape=list(outs),
        scratch_shapes=list(scratch),
        compiler_params=pltpu.CompilerParams(vmem_limit_bytes=VMEM_BYTES),
    )(*scalars, *operands)


def same(*dims):
    return pl.BlockSpec(dims, lambda i: (0,) * len(dims))


def chunk(*dims):
    return pl.BlockSpec(dims, lambda i: (i,) + (0,) * (len(dims) - 1))


def like(value):
    return same(*value.shape)


def halves(first, second, core):
    kinds = first.shape[0]
    top = lax.dynamic_slice_in_dim(first, core * 256, 256, 1).reshape(kinds * 256, 128)
    rest = lax.dynamic_slice_in_dim(second, core * 64, 64, 0)
    rest = rest.reshape(64, 4, 128).transpose(1, 0, 2).reshape(256, 128)
    return jnp.concatenate([top, rest], axis=0)


def shards(
    node_lat,
    edge_lat,
    edge_src,
    edge_dst,
    edge_count,
    halo_send,
    coarse_of,
    edge_w1,
    edge_w2,
    node_w1,
    node_w2,
    grad_node,
    grad_edge,
):
    core = lax.axis_index("core")
    co = jnp.stack([core, core, core, core, edge_count[0]]).astype(jnp.int32)
    lists, owned = halo_send[0], coarse_of[0]
    unused = jnp.full((48,), -1, jnp.int32)
    targets = jnp.concatenate([lists[1], lists[0], jnp.tile(owned, 4), unused]).reshape(1, 128)

    edge_near = exchange(repeated(halves(edge_w1, edge_w2, core), 4), "feat")
    from_prev = shifted(node_lat[lists[1]], 1)
    from_next = shifted(node_lat[lists[0]], -1)
    edge_far = other_core(edge_near)
    coarse = exchange(repeated(node_lat[owned], 128), BOTH).reshape(512, 512)
    node_near = exchange(repeated(halves(node_w1, node_w2, core), 4), "feat")
    node_far = other_core(node_near)

    src, dst = edge_src.reshape(16, 128), edge_dst.reshape(16, 128)
    src_wide, dst_wide = edge_src.reshape(STEPS, CHUNK), edge_dst.reshape(STEPS, CHUNK)
    fixed = [node_lat, from_prev, from_next, coarse, edge_near, edge_far]
    fixed += [src, dst, dst_wide]
    wide = chunk(CHUNK, 512)
    params = pltpu.CompilerParams(vmem_limit_bytes=VMEM_BYTES, dimension_semantics=("arbitrary",))
    edge_out, incoming, act, normed, slope, factor, lookup, first, second = pl.pallas_call(
        forward_kernel,
        grid=(STEPS,),
        in_specs=[SMEM] + [like(v) for v in fixed] + [wide],
        out_specs=[wide, same(256, 512), wide, wide, wide, chunk(CHUNK, 128)]
        + [same(TABLE, 512), same(3, 512, 512), same(512, 512)],
        out_shape=[
            shape(2048, 512),
            shape(256, 512),
            shape(2048, 512),
            shape(2048, 512),
            shape(2048, 512),
            shape(2048, 128, dtype=F32),
            shape(TABLE, 512),
            shape(3, 512, 512),
            shape(512, 512),
        ],
        scratch_shapes=[pltpu.VMEM((TABLE + 256, 512), BF16), pltpu.VMEM((256, 512), F32)],
        compiler_params=params,
        cost_estimate=pl.CostEstimate(
            flops=7_000_000_000, bytes_accessed=18_000_000, transcendentals=1_000_000
        ),
    )(co, *fixed, edge_lat)

    fixed = [node_lat, incoming, grad_node, node_near, node_far]
    fixed += [first, second, lookup, dst, src_wide, dst_wide]
    moving = [edge_lat, act, normed, slope, factor, grad_edge]
    tiles = (8, 2, 4, 128, 128)
    node_out, node_total, edge_grad, to_prev, to_next, keep, give = pl.pallas_call(
        backward_kernel,
        grid=(STEPS,),
        in_specs=[SMEM]
        + [like(v) for v in fixed]
        + [wide, wide, wide, wide, chunk(CHUNK, 128), wide],
        out_specs=[same(256, 512), same(256, 512), wide, same(32, 512), same(32, 512)]
        + [same(*tiles), same(*tiles)],
        out_shape=[
            shape(256, 512),
            shape(256, 512, dtype=F32),
            shape(2048, 512),
            shape(32, 512),
            shape(32, 512),
            shape(*tiles),
            shape(*tiles),
        ],
        scratch_shapes=[
            pltpu.VMEM((2, 512, 512), BF16),
            pltpu.VMEM((512, 512), BF16),
            pltpu.VMEM((256, 512), BF16),
            pltpu.VMEM((512, 512), F32),
            pltpu.VMEM((512, 512), F32),
            pltpu.VMEM((TABLE + 256, 512), F32),
            pltpu.VMEM((16, 2, 16, 512), BF16),
            pltpu.VMEM((4, 512, 128), BF16),
            pltpu.VMEM((16, 2, 4, 16, 128), BF16),
        ],
        compiler_params=params,
        cost_estimate=pl.CostEstimate(
            flops=9_000_000_000, bytes_accessed=24_000_000, transcendentals=100_000
        ),
    )(co, *fixed, *moving)

    ahead = shifted(to_prev, -1)
    behind = shifted(to_next, 1)
    pair = (keep.astype(F32) + other_core(give).astype(F32)).astype(BF16).reshape(64, 128, 128)
    own = jnp.sum(exchange(pair, ("z", "x", "feat")).astype(F32), axis=0).astype(BF16)
    tiles = exchange(repeated(own[:112], 32), ("z", "x", "core"))
    edge_first, edge_second, node_first, node_second, node_grad = plain_call(
        final_kernel,
        [],
        [tiles, own, ahead, behind, targets, node_total],
        [
            shape(3, 32, 16, 128, dtype=F32),
            shape(128, 512, dtype=F32),
            shape(2, 32, 16, 128, dtype=F32),
            shape(128, 512, dtype=F32),
            shape(256, 512, dtype=F32),
        ],
        [pltpu.VMEM((128, 512), BF16)],
    )
    return (
        edge_out,
        node_out,
        node_grad,
        edge_grad,
        edge_first.reshape(3, 512, 128),
        edge_second,
        node_first.reshape(2, 512, 128),
        node_second,
    )


def solution(mesh):
    cube = Mesh(mesh.devices.reshape(4, 4, 2, 4), BOTH)
    rows = P(BOTH, None)
    flat = P(BOTH)
    first, second = P(None, None, "feat"), P("feat", None)
    return jax.shard_map(
        shards,
        mesh=cube,
        in_specs=(
            rows,
            rows,
            flat,
            flat,
            flat,
            P(BOTH, None, None),
            rows,
            first,
            second,
            first,
            second,
            rows,
            rows,
        ),
        out_specs=(rows, rows, rows, rows, first, second, first, second),
        check_vma=False,
    )
```

```python
import jax
import jax.numpy as jnp
from jax import lax
from jax.experimental import pallas as pl
from jax.experimental.pallas import tpu as pltpu
from jax.sharding import Mesh
from jax.sharding import PartitionSpec as P

EPSILON = 1e-05
BF16 = jnp.bfloat16
F32 = jnp.float32
BOTH = ("z", "x", "core", "feat")
CHUNK = 512
STEPS = 4
TABLE = 896
VMEM_BYTES = 60 * 1024 * 1024


def other_core(value):
    return lax.ppermute(value, "core", [(0, 1), (1, 0)])


def shifted(value, steps):
    return lax.ppermute(value, BOTH, [(k, (k + steps) % 128) for k in range(128)])


def exchange(value, axes):
    return lax.all_to_all(value, axes, 0, 0, tiled=True)


def after(value, *earlier):
    return lax.optimization_barrier((value, *earlier))[0]


def repeated(value, count):
    return jnp.broadcast_to(value[None], (count,) + value.shape)


def dot(left, right):
    return lax.dot_general(left, right, (((1,), (0,)), ((), ())), preferred_element_type=F32)


def dot_nt(left, right):
    return lax.dot_general(left, right, (((1,), (1,)), ((), ())), preferred_element_type=F32)


def dot_tn(left, right):
    return lax.dot_general(left, right, (((0,), (0,)), ((), ())), preferred_element_type=F32)


def mean(values):
    return jnp.mean(values, axis=-1, keepdims=True)


def normalize(values):
    centre = values - mean(values)
    factor = lax.rsqrt(mean(centre * centre) + EPSILON)
    return centre * factor, factor


def normalize_back(upstream, normed, factor):
    return factor * (upstream - mean(upstream) - normed * mean(upstream * normed))


def swish(pre):
    sigmoid = 0.5 + 0.5 * jnp.tanh(0.5 * pre)
    act = pre * sigmoid
    return act, sigmoid + act * (1.0 - sigmoid)


def hot_tiles(rows, count):
    lanes = lax.broadcasted_iota(jnp.int32, (128, 128), 1)
    spread = jnp.transpose(jnp.broadcast_to(rows, (128, 128)))
    return [jnp.where(spread == lanes + 128 * j, 1.0, 0.0).astype(BF16) for j in range(count)]


def live_rows(step, count):
    place = lax.broadcasted_iota(jnp.int32, (CHUNK, 1), 0) + step * CHUNK
    return jnp.where(place < count, 1.0, 0.0)


def place_weights(core, near, far, first, second):
    kinds = first.shape[0]
    for part, half in ((near, core), (far, 1 - core)):
        for y in range(4):
            rows = pl.ds(pl.multiple_of(half * 256, 256), 256)
            for m in range(kinds):
                first[m, rows, y * 128 : (y + 1) * 128] = part[y, m * 256 : (m + 1) * 256, :]
            rows = pl.ds(pl.multiple_of(y * 128 + half * 64, 64), 64)
            for b in range(4):
                start = kinds * 256 + b * 64
                second[rows, b * 128 : (b + 1) * 128] = part[y, start : start + 64, :]


def whole(first, m):
    return first[m].reshape(512, 512)


def place_tiles(own_core, near, far, lookup, first, second, coarse):
    for part, core in ((near, own_core), (far, 1 - own_core)):
        for y in range(4):
            block = slice(y * 128, (y + 1) * 128)
            for m in range(3):
                value = part[:, y, m * 16 : (m + 1) * 16, :].reshape(16, 1, 16, 128)
                first[m, :, pl.ds(core, 1), :, block] = value
            for k in range(16):
                rows = slice(y * 128 + k // 2 * 16, y * 128 + k // 2 * 16 + 16)
                columns = pl.ds(pl.multiple_of((k % 2 * 2 + core) * 128, 128), 128)
                second[rows, columns] = part[k, y, 48:64, :]
            coarse[:, pl.ds(core, 1), y] = part[:, y, 64:80, :].reshape(16, 1, 16, 128)
    low = lax.broadcasted_iota(jnp.int32, (64, 8, 128), 1) < 4
    pairs = coarse[...].reshape(64, 2, 16, 128).astype(F32)
    for half in range(2):
        even, odd = pairs[:, 0, half * 8 : half * 8 + 8], pairs[:, 1, half * 8 : half * 8 + 8]
        first_block = jnp.where(low, even, pltpu.roll(odd, 4, 1)).reshape(512, 128)
        other_block = jnp.where(low, pltpu.roll(even, 4, 1), odd).reshape(512, 128)
        lookup[320:832, half * 256 : half * 256 + 128] = first_block.astype(BF16)
        lookup[320:832, half * 256 + 128 : half * 256 + 256] = other_block.astype(BF16)


def forward_kernel(co, node, prev, following, near, far, src, dst, dst_wide, edge, *refs):
    edge_out, incoming, act_out, normed_out, slope_out, factor_out, lookup, first, second = refs[:9]
    table, total, coarse = refs[9:]
    step = pl.program_id(0)

    @pl.when(step == 0)
    def _():
        lookup[0:256, :] = node[...]
        lookup[256:288, :] = prev[...]
        lookup[288:320, :] = following[...]
        lookup[832:896, :] = jnp.zeros((64, 512), BF16)
        place_tiles(co[2], near, far, lookup, first, second, coarse)
        table[0:TABLE, :] = dot(lookup[...], whole(first, 1)).astype(BF16)
        table[TABLE:, :] = dot(node[...], whole(first, 2)).astype(BF16)
        total[...] = jnp.zeros_like(total)

    hots = []
    for r in range(CHUNK // 128):
        row = pl.ds(step * (CHUNK // 128) + r, 1)
        tiles = hot_tiles(src[row, :], TABLE // 128) + hot_tiles(dst[row, :], 2)
        hots.append(jnp.concatenate(tiles, axis=1))
    hot = jnp.concatenate(hots, axis=0)
    rows = edge[...]
    pre = dot(rows, whole(first, 0)) + dot(hot, table[...])
    act, slope = swish(pre)
    act = act.astype(BF16)
    act_out[...] = act
    slope_out[...] = slope.astype(BF16)
    normed, factor = normalize(dot(act, second[...]))
    normed_out[...] = normed.astype(BF16)
    factor_out[...] = jnp.broadcast_to(factor, (CHUNK, 128))
    new = (rows.astype(F32) + live_rows(step, co[4]) * normed).astype(BF16)
    edge_out[...] = new
    place = lax.broadcasted_iota(jnp.int32, (256, CHUNK), 1) + step * CHUNK
    node_of = lax.broadcasted_iota(jnp.int32, (256, CHUNK), 0)
    match = (node_of == dst_wide[pl.ds(step, 1), :]) & (place < co[4])
    total[...] += dot(jnp.where(match, 1.0, 0.0).astype(BF16), new)

    @pl.when(step == STEPS - 1)
    def _():
        incoming[...] = total[...].astype(BF16)


def put_columns(co, grad, slot, scratch, keep, give):
    scratch[...] = grad.astype(BF16).reshape(16, 2, 16, 512)
    for target, core in ((keep, co[2]), (give, 1 - co[2])):
        value = scratch[:, pl.ds(core, 1), :, :].reshape(8, 2, 16, 512)
        for y in range(4):
            target[:, :, y, slot * 16 : (slot + 1) * 16, :] = value[:, :, :, y * 128 : (y + 1) * 128]


def put_rows(co, grad, slot, scratch, keep, give):
    for b in range(4):
        scratch[b] = grad[:, b * 128 : (b + 1) * 128].astype(BF16)
    for target, core in ((keep, co[2]), (give, 1 - co[2])):
        for h in range(2):
            value = scratch[2 * h + core].reshape(4, 8, 16, 128)
            for y in range(4):
                target[:, h, y, slot * 16 : (slot + 1) * 16, :] = value[y]


def put_owned(co, grad, scratch, keep, give):
    rows = grad.reshape(64, 8, 512)
    turned = pltpu.roll(rows, 4, 1)
    low = lax.broadcasted_iota(jnp.int32, (64, 8, 128), 1) < 4
    for odd in range(2):
        left, right = (turned, rows) if odd else (rows, turned)
        parts = [
            jnp.where(low, left[:, :, b : b + 128], right[:, :, b + 128 : b + 256]) for b in (0, 256)
        ]
        tile = jnp.concatenate(parts, axis=1).astype(BF16).reshape(16, 2, 2, 16, 128)
        for pair in range(2):
            scratch[:, :, pair * 2 + odd] = tile[:, :, pair]
    for target, core in ((keep, co[2]), (give, 1 - co[2])):
        value = scratch[:, pl.ds(core, 1)].reshape(8, 2, 4, 16, 128)
        target[:, :, :, 112:128, :] = value


def backward_kernel(co, node, incoming, grad_node, near, far, *refs):
    edge_first, edge_second, lookup, dst, src_wide, dst_wide = refs[:6]
    edge, act, normed, slope, factor, grad_edge = refs[6:12]
    node_out, node_total, edge_grad, to_prev, to_next, keep, give = refs[12:19]
    first, second, spread, sum_second, sum_first, sums, columns, rows, owned = refs[19:]
    step = pl.program_id(0)

    @pl.when(step == 0)
    def _():
        place_weights(co[2], near, far, first, second)
        lat, summed = node[...], incoming[...]
        pre = dot(lat, first[0]) + dot(summed, first[1])
        node_act, node_slope = swish(pre)
        node_act = node_act.astype(BF16)
        node_normed, node_factor = normalize(dot(node_act, second[...]))
        node_out[...] = (lat.astype(F32) + node_normed).astype(BF16)
        upstream = grad_node[...].astype(F32)
        delta = normalize_back(upstream, node_normed, node_factor).astype(BF16)
        put_rows(co, dot_tn(node_act, delta), 6, rows, keep, give)
        pre_grad = (dot_nt(delta, second[...]) * node_slope).astype(BF16)
        put_columns(co, dot_tn(lat, pre_grad), 3, columns, keep, give)
        put_columns(co, dot_tn(summed, pre_grad), 4, columns, keep, give)
        node_total[...] = upstream + dot_nt(pre_grad, first[0])
        spread[...] = dot_nt(pre_grad, first[1]).astype(BF16)
        sum_second[...] = jnp.zeros_like(sum_second)
        sum_first[...] = jnp.zeros_like(sum_first)
        sums[...] = jnp.zeros_like(sums)

    hots = []
    for r in range(CHUNK // 128):
        row = pl.ds(step * (CHUNK // 128) + r, 1)
        hots.append(jnp.concatenate(hot_tiles(dst[row, :], 2), axis=1))
    live = live_rows(step, co[4])
    total = grad_edge[...].astype(F32) + live * dot(jnp.concatenate(hots, axis=0), spread[...])
    delta = normalize_back(live * total, normed[...].astype(F32), factor[:, 0:1]).astype(BF16)
    pre_grad = (dot_nt(delta, edge_second[...]) * slope[...].astype(F32)).astype(BF16)
    edge_grad[...] = (total + dot_nt(pre_grad, whole(edge_first, 0))).astype(BF16)
    sum_second[...] += dot_tn(act[...], delta)
    sum_first[...] += dot_tn(edge[...], pre_grad)
    place = lax.broadcasted_iota(jnp.int32, (128, CHUNK), 0)
    src_row, dst_row = src_wide[pl.ds(step, 1), :], dst_wide[pl.ds(step, 1), :]
    for j in range(9):
        match = place + 128 * j == src_row if j < 7 else place + 128 * (j - 7) == dst_row
        hot = jnp.where(match, 1.0, 0.0).astype(BF16)
        sums[j * 128 : (j + 1) * 128, :] += dot(hot, pre_grad)

    @pl.when(step == STEPS - 1)
    def _():
        put_rows(co, sum_second[...], 5, rows, keep, give)
        put_columns(co, sum_first[...], 0, columns, keep, give)
        sent = sums[0:TABLE, :].astype(BF16)
        received = sums[TABLE:, :].astype(BF16)
        put_columns(co, dot_tn(lookup[...], sent), 1, columns, keep, give)
        put_columns(co, dot_tn(node[...], received), 2, columns, keep, give)
        back = dot_nt(sent, whole(edge_first, 1))
        node_total[...] += back[0:256] + dot_nt(received, whole(edge_first, 2))
        to_prev[...] = back[256:288].astype(BF16)
        to_next[...] = back[288:320].astype(BF16)
        put_owned(co, back[320:832], owned, keep, give)


def final_kernel(co, tiles, far, own, ahead, behind, targets, node_total, *refs):
    edge_first, edge_second, node_first, node_second, node_grad, rows = refs
    for part, core in ((tiles, co[2]), (far, 1 - co[2])):
        for m in range(3):
            value = part[:, m * 16 : (m + 1) * 16, :].astype(F32)
            edge_first[m, :, pl.ds(core, 1)] = value.reshape(16, 1, 16, 128)
        for m in range(2):
            value = part[:, 48 + m * 16 : 64 + m * 16, :].astype(F32)
            node_first[m, :, pl.ds(core, 1)] = value.reshape(16, 1, 16, 128)
        for k in range(16):
            r = k // 2 * 16
            b = pl.ds(pl.multiple_of((k % 2 * 2 + core) * 128, 128), 128)
            edge_second[r : r + 16, b] = part[k, 80:96, :].astype(F32)
            node_second[r : r + 16, b] = part[k, 96:112, :].astype(F32)
    rows[0:32, :] = ahead[...]
    rows[32:64, :] = behind[...]
    group = lax.broadcasted_iota(jnp.int32, (16, 128), 0) // 4
    for b in range(4):
        value = jnp.where(group == b, own[112:128, :].astype(F32), 0.0)
        rows[64:80, b * 128 : (b + 1) * 128] = value.astype(BF16)
    rows[80:128, :] = jnp.zeros((48, 512), BF16)
    match = lax.broadcasted_iota(jnp.int32, (256, 128), 0) == targets[...]
    hot = jnp.where(match, 1.0, 0.0).astype(BF16)
    node_grad[...] = node_total[...] + dot(hot, rows[...])


SMEM = pl.BlockSpec(memory_space=pltpu.SMEM)
WHOLE = pl.BlockSpec(memory_space=pltpu.VMEM)


def shape(*dims, dtype=BF16):
    return jax.ShapeDtypeStruct(dims, dtype)


def plain_call(kernel, scalars, operands, outs, scratch=()):
    return pl.pallas_call(
        kernel,
        in_specs=[SMEM] * len(scalars) + [WHOLE] * len(operands),
        out_specs=[WHOLE] * len(outs),
        out_shape=list(outs),
        scratch_shapes=list(scratch),
        compiler_params=pltpu.CompilerParams(vmem_limit_bytes=VMEM_BYTES),
    )(*scalars, *operands)


def same(*dims):
    return pl.BlockSpec(dims, lambda i: (0,) * len(dims))


def chunk(*dims):
    return pl.BlockSpec(dims, lambda i: (i,) + (0,) * (len(dims) - 1))


def like(value):
    return same(*value.shape)


def halves(first, second, core):
    kinds = first.shape[0]
    top = lax.dynamic_slice_in_dim(first, core * 256, 256, 1).reshape(kinds * 256, 128)
    rest = lax.dynamic_slice_in_dim(second, core * 64, 64, 0)
    rest = rest.reshape(64, 4, 128).transpose(1, 0, 2).reshape(256, 128)
    return jnp.concatenate([top, rest], axis=0)


def shards(
    node_lat,
    edge_lat,
    edge_src,
    edge_dst,
    edge_count,
    halo_send,
    coarse_of,
    edge_w1,
    edge_w2,
    node_w1,
    node_w2,
    grad_node,
    grad_edge,
):
    core = lax.axis_index("core")
    patch = (lax.axis_index("z") * 4 + lax.axis_index("x")) * 2 + core
    co = jnp.stack([core, core, core, core, edge_count[0]]).astype(jnp.int32)
    lists, owned = halo_send[0], coarse_of[0]
    unused = jnp.full((48,), -1, jnp.int32)
    targets = jnp.concatenate([lists[1], lists[0], jnp.tile(owned, 4), unused]).reshape(1, 128)

    first_part = lax.dynamic_slice_in_dim(edge_w1, patch * 16, 16, 1).reshape(48, 128)
    second_part = lax.dynamic_slice(edge_w2, (patch // 4 * 16, patch % 4 * 128), (16, 128))
    coarse_own = node_lat[owned].reshape(4, 4, 128).transpose(1, 0, 2).reshape(16, 128)
    tile = jnp.concatenate([first_part, second_part, coarse_own], axis=0)
    from_prev = shifted(node_lat[lists[1]], 1)
    from_next = shifted(node_lat[lists[0]], -1)
    near = exchange(repeated(tile, 64), ("z", "x", "feat")).reshape(16, 4, 80, 128)
    near = after(near, from_prev, from_next)
    far = other_core(near)
    node_half = after(repeated(halves(node_w1, node_w2, core), 4), near, far)
    node_near = exchange(node_half, "feat")

    src, dst = edge_src.reshape(16, 128), edge_dst.reshape(16, 128)
    src_wide, dst_wide = edge_src.reshape(STEPS, CHUNK), edge_dst.reshape(STEPS, CHUNK)
    fixed = [node_lat, from_prev, from_next, near, far]
    fixed += [src, dst, dst_wide]
    wide = chunk(CHUNK, 512)
    params = pltpu.CompilerParams(vmem_limit_bytes=VMEM_BYTES, dimension_semantics=("arbitrary",))
    edge_out, incoming, act, normed, slope, factor, lookup, first, second = pl.pallas_call(
        forward_kernel,
        grid=(STEPS,),
        in_specs=[SMEM] + [like(v) for v in fixed] + [wide],
        out_specs=[wide, same(256, 512), wide, wide, wide, chunk(CHUNK, 128)]
        + [same(TABLE, 512), same(3, 16, 2, 16, 512), same(512, 512)],
        out_shape=[
            shape(2048, 512),
            shape(256, 512),
            shape(2048, 512),
            shape(2048, 512),
            shape(2048, 512),
            shape(2048, 128, dtype=F32),
            shape(TABLE, 512),
            shape(3, 16, 2, 16, 512),
            shape(512, 512),
        ],
        scratch_shapes=[
            pltpu.VMEM((TABLE + 256, 512), BF16),
            pltpu.VMEM((256, 512), F32),
            pltpu.VMEM((16, 2, 4, 16, 128), BF16),
        ],
        compiler_params=params,
        cost_estimate=pl.CostEstimate(
            flops=7_000_000_000, bytes_accessed=18_000_000, transcendentals=1_000_000
        ),
    )(co, *fixed, edge_lat)

    node_near = after(node_near, incoming)
    node_far = other_core(node_near)
    fixed = [node_lat, incoming, grad_node, node_near, node_far]
    fixed += [first, second, lookup, dst, src_wide, dst_wide]
    moving = [edge_lat, act, normed, slope, factor, grad_edge]
    tiles = (8, 2, 4, 128, 128)
    node_out, node_total, edge_grad, to_prev, to_next, keep, give = pl.pallas_call(
        backward_kernel,
        grid=(STEPS,),
        in_specs=[SMEM]
        + [like(v) for v in fixed]
        + [wide, wide, wide, wide, chunk(CHUNK, 128), wide],
        out_specs=[same(256, 512), same(256, 512), wide, same(32, 512), same(32, 512)]
        + [same(*tiles), same(*tiles)],
        out_shape=[
            shape(256, 512),
            shape(256, 512, dtype=F32),
            shape(2048, 512),
            shape(32, 512),
            shape(32, 512),
            shape(*tiles),
            shape(*tiles),
        ],
        scratch_shapes=[
            pltpu.VMEM((2, 512, 512), BF16),
            pltpu.VMEM((512, 512), BF16),
            pltpu.VMEM((256, 512), BF16),
            pltpu.VMEM((512, 512), F32),
            pltpu.VMEM((512, 512), F32),
            pltpu.VMEM((TABLE + 256, 512), F32),
            pltpu.VMEM((16, 2, 16, 512), BF16),
            pltpu.VMEM((4, 512, 128), BF16),
            pltpu.VMEM((16, 2, 4, 16, 128), BF16),
        ],
        compiler_params=params,
        cost_estimate=pl.CostEstimate(
            flops=9_000_000_000, bytes_accessed=24_000_000, transcendentals=100_000
        ),
    )(co, *fixed, *moving)

    pair = (keep.astype(F32) + other_core(give).astype(F32)).astype(BF16).reshape(64, 128, 128)
    ahead = shifted(after(to_prev, pair), -1)
    behind = shifted(after(to_next, pair), 1)
    own = jnp.sum(exchange(pair, ("z", "x", "feat")).astype(F32), axis=0).astype(BF16)
    own = after(own, ahead, behind)
    tiles = exchange(repeated(own[:112], 16), ("z", "x"))
    far_tiles = other_core(tiles)
    edge_first, edge_second, node_first, node_second, node_grad = plain_call(
        final_kernel,
        [co],
        [tiles, far_tiles, own, ahead, behind, targets, node_total],
        [
            shape(3, 16, 2, 16, 128, dtype=F32),
            shape(128, 512, dtype=F32),
            shape(2, 16, 2, 16, 128, dtype=F32),
            shape(128, 512, dtype=F32),
            shape(256, 512, dtype=F32),
        ],
        [pltpu.VMEM((128, 512), BF16)],
    )
    return (
        edge_out,
        node_out,
        node_grad,
        edge_grad,
        edge_first.reshape(3, 512, 128),
        edge_second,
        node_first.reshape(2, 512, 128),
        node_second,
    )


def solution(mesh):
    cube = Mesh(mesh.devices.reshape(4, 4, 2, 4), BOTH)
    rows = P(BOTH, None)
    flat = P(BOTH)
    first, second = P(None, None, "feat"), P("feat", None)
    return jax.shard_map(
        shards,
        mesh=cube,
        in_specs=(
            rows,
            rows,
            flat,
            flat,
            flat,
            P(BOTH, None, None),
            rows,
            first,
            second,
            first,
            second,
            rows,
            rows,
        ),
        out_specs=(rows, rows, rows, rows, first, second, first, second),
        check_vma=False,
    )
```

```python
import jax
import jax.numpy as jnp
from jax import lax
from jax.experimental import pallas as pl
from jax.experimental.pallas import tpu as pltpu
from jax.sharding import Mesh
from jax.sharding import PartitionSpec as P

EPSILON = 1e-05
BF16 = jnp.bfloat16
F32 = jnp.float32
BOTH = ("z", "x", "core", "feat")
CHUNK = 512
STEPS = 4
TABLE = 896
VMEM_BYTES = 60 * 1024 * 1024


def other_core(value):
    return lax.ppermute(value, "core", [(0, 1), (1, 0)])


def shifted(value, steps):
    return lax.ppermute(value, BOTH, [(k, (k + steps) % 128) for k in range(128)])


def exchange(value, axes):
    return lax.all_to_all(value, axes, 0, 0, tiled=True)


def after(value, *earlier):
    return lax.optimization_barrier((value, *earlier))[0]


def repeated(value, count):
    return jnp.broadcast_to(value[None], (count,) + value.shape)


def dot(left, right):
    return lax.dot_general(left, right, (((1,), (0,)), ((), ())), preferred_element_type=F32)


def dot_nt(left, right):
    return lax.dot_general(left, right, (((1,), (1,)), ((), ())), preferred_element_type=F32)


def dot_tn(left, right):
    return lax.dot_general(left, right, (((0,), (0,)), ((), ())), preferred_element_type=F32)


def mean(values):
    return jnp.mean(values, axis=-1, keepdims=True)


def normalize(values):
    centre = values - mean(values)
    factor = lax.rsqrt(mean(centre * centre) + EPSILON)
    return centre * factor, factor


def normalize_back(upstream, normed, factor):
    return factor * (upstream - mean(upstream) - normed * mean(upstream * normed))


def swish(pre):
    half = 0.5 * pre
    tanh = jnp.tanh(half)
    act = half + half * tanh
    return act, 0.5 * (1.0 + act + tanh * (1.0 - act))


def hot_tiles(rows, count):
    lanes = lax.broadcasted_iota(jnp.int32, (128, 128), 1)
    spread = jnp.transpose(jnp.broadcast_to(rows, (128, 128)))
    return [jnp.where(spread == lanes + 128 * j, 1.0, 0.0).astype(BF16) for j in range(count)]


def hot_kernel(co, src, dst, src_wide, dst_wide, hot, turned):
    step = pl.program_id(0)
    lanes = lax.broadcasted_iota(jnp.int32, (1, 128), 1)
    for r in range(CHUNK // 128):
        row = pl.ds(step * (CHUNK // 128) + r, 1)
        live = lanes + step * CHUNK + r * 128 < co[4]
        tiles = hot_tiles(jnp.where(live, dst[row, :], -1), 2) + hot_tiles(src[row, :], 7)
        hot[r * 128 : (r + 1) * 128, :] = jnp.concatenate(tiles, axis=1)
    place = lax.broadcasted_iota(jnp.int32, (128, CHUNK), 0)
    lanes = lax.broadcasted_iota(jnp.int32, (1, CHUNK), 1)
    src_row = src_wide[pl.ds(step, 1), :]
    dst_row = jnp.where(lanes + step * CHUNK < co[4], dst_wide[pl.ds(step, 1), :], -1)
    for j in range(9):
        match = place + 128 * j == dst_row if j < 2 else place + 128 * (j - 2) == src_row
        turned[j * 128 : (j + 1) * 128, :] = jnp.where(match, 1.0, 0.0).astype(BF16)


def pack_kernel(co, node, targets, edge_first, edge_second, tiles, to_next, to_prev):
    match = lax.broadcasted_iota(jnp.int32, (256, 128), 0) == targets[...]
    rows = dot_tn(jnp.where(match, 1.0, 0.0).astype(BF16), node[...])
    to_next[...] = rows[0:32].astype(BF16)
    to_prev[...] = rows[32:64].astype(BF16)
    group = lax.broadcasted_iota(jnp.int32, (16, 128), 0) // 4
    coarse = jnp.zeros((16, 128), F32)
    for b in range(4):
        coarse = jnp.where(group == b, rows[64:80, b * 128 : (b + 1) * 128], coarse)
    patch = co[0]
    at = pl.ds(pl.multiple_of(patch * 16, 16), 16)
    parts = [edge_first[m, at, :] for m in range(3)]
    row = pl.ds(pl.multiple_of(patch // 4 * 16, 16), 16)
    parts.append(edge_second[row, pl.ds(pl.multiple_of(patch % 4 * 128, 128), 128)])
    parts.append(coarse.astype(BF16))
    tile = jnp.concatenate(parts, axis=0)
    for k in range(64):
        tiles[k] = tile


def live_rows(step, count):
    place = lax.broadcasted_iota(jnp.int32, (CHUNK, 1), 0) + step * CHUNK
    return jnp.where(place < count, 1.0, 0.0)


HALVES = (slice(0, CHUNK // 2), slice(CHUNK // 2, CHUNK))


def place_weights(core, near, far, first, second):
    kinds = first.shape[0]
    for part, half in ((near, core), (far, 1 - core)):
        for y in range(4):
            rows = pl.ds(pl.multiple_of(half * 256, 256), 256)
            for m in range(kinds):
                first[m, rows, y * 128 : (y + 1) * 128] = part[y, m * 256 : (m + 1) * 256, :]
            rows = pl.ds(pl.multiple_of(y * 128 + half * 64, 64), 64)
            for b in range(4):
                start = kinds * 256 + b * 64
                second[rows, b * 128 : (b + 1) * 128] = part[y, start : start + 64, :]


def whole(first, m):
    return first[m].reshape(512, 512)


def place_tiles(own_core, near, far, lookup, first, second, coarse):
    for part, core in ((near, own_core), (far, 1 - own_core)):
        for y in range(4):
            block = slice(y * 128, (y + 1) * 128)
            for m in range(3):
                value = part[:, y, m * 16 : (m + 1) * 16, :].reshape(16, 1, 16, 128)
                first[m, :, pl.ds(core, 1), :, block] = value
            for k in range(16):
                rows = slice(y * 128 + k // 2 * 16, y * 128 + k // 2 * 16 + 16)
                columns = pl.ds(pl.multiple_of((k % 2 * 2 + core) * 128, 128), 128)
                second[rows, columns] = part[k, y, 48:64, :]
            coarse[:, pl.ds(core, 1), y] = part[:, y, 64:80, :].reshape(16, 1, 16, 128)
    low = lax.broadcasted_iota(jnp.int32, (64, 8, 128), 1) < 4
    pairs = coarse[...].reshape(64, 2, 16, 128).astype(F32)
    for half in range(2):
        even, odd = pairs[:, 0, half * 8 : half * 8 + 8], pairs[:, 1, half * 8 : half * 8 + 8]
        first_block = jnp.where(low, even, pltpu.roll(odd, 4, 1)).reshape(512, 128)
        other_block = jnp.where(low, pltpu.roll(even, 4, 1), odd).reshape(512, 128)
        lookup[320:832, half * 256 : half * 256 + 128] = first_block.astype(BF16)
        lookup[320:832, half * 256 + 128 : half * 256 + 256] = other_block.astype(BF16)


def forward_kernel(co, node, prev, following, near, far, edge, hot, turned, *refs):
    edge_out, incoming, act_out, normed_out, slope_out, factor_out, lookup, first, second = refs[:9]
    table, total, coarse = refs[9:]
    step = pl.program_id(0)

    @pl.when(step == 0)
    def _():
        lookup[0:256, :] = node[...]
        lookup[256:288, :] = prev[...]
        lookup[288:320, :] = following[...]
        lookup[832:896, :] = jnp.zeros((64, 512), BF16)
        place_tiles(co[2], near, far, lookup, first, second, coarse)
        table[0:256, :] = dot(node[...], whole(first, 2)).astype(BF16)
        table[256:, :] = dot(lookup[...], whole(first, 1)).astype(BF16)
        total[...] = jnp.zeros_like(total)

    live = live_rows(step, co[4])
    pres = [dot(edge[h, :], whole(first, 0)) + dot(hot[h, :], table[...]) for h in HALVES]
    acts = []
    for h, pre in zip(HALVES, pres):
        act, slope = swish(pre)
        acts.append(act.astype(BF16))
        act_out[h, :] = acts[-1]
        slope_out[h, :] = slope.astype(BF16)
    values = [dot(act, second[...]) for act in acts]
    for h, value in zip(HALVES, values):
        centre = value - mean(value)
        factor = lax.rsqrt(mean(centre * centre) + EPSILON) * live[h]
        normed = centre * factor
        normed_out[h, :] = normed.astype(BF16)
        factor_out[h, :] = jnp.broadcast_to(factor, (CHUNK // 2, 128))
        edge_out[h, :] = (edge[h, :].astype(F32) + normed).astype(BF16)
    total[...] += dot(turned[...], edge_out[...])

    @pl.when(step == STEPS - 1)
    def _():
        incoming[...] = total[...].astype(BF16)


def put_columns(co, grad, slot, scratch, keep, give):
    scratch[...] = grad.astype(BF16).reshape(16, 2, 16, 512)
    for target, core in ((keep, co[2]), (give, 1 - co[2])):
        value = scratch[:, pl.ds(core, 1), :, :].reshape(8, 2, 16, 512)
        for y in range(4):
            target[:, :, y, slot * 16 : (slot + 1) * 16, :] = value[:, :, :, y * 128 : (y + 1) * 128]


def put_rows(co, grad, slot, scratch, keep, give):
    for b in range(4):
        scratch[b] = grad[:, b * 128 : (b + 1) * 128].astype(BF16)
    for target, core in ((keep, co[2]), (give, 1 - co[2])):
        for h in range(2):
            value = scratch[2 * h + core].reshape(4, 8, 16, 128)
            for y in range(4):
                target[:, h, y, slot * 16 : (slot + 1) * 16, :] = value[y]


def put_owned(co, grad, scratch, keep, give):
    rows = grad.reshape(64, 8, 512)
    turned = pltpu.roll(rows, 4, 1)
    low = lax.broadcasted_iota(jnp.int32, (64, 8, 128), 1) < 4
    for odd in range(2):
        left, right = (turned, rows) if odd else (rows, turned)
        parts = [
            jnp.where(low, left[:, :, b : b + 128], right[:, :, b + 128 : b + 256]) for b in (0, 256)
        ]
        tile = jnp.concatenate(parts, axis=1).astype(BF16).reshape(16, 2, 2, 16, 128)
        for pair in range(2):
            scratch[:, :, pair * 2 + odd] = tile[:, :, pair]
    for target, core in ((keep, co[2]), (give, 1 - co[2])):
        value = scratch[:, pl.ds(core, 1)].reshape(8, 2, 4, 16, 128)
        target[:, :, :, 112:128, :] = value


def backward_kernel(co, node, incoming, grad_node, near, far, *refs):
    edge_first, edge_second, lookup = refs[:3]
    edge, act, normed, slope, factor, grad_edge, hot, turned = refs[3:11]
    node_out, node_total, edge_grad, to_prev, to_next, keep, give = refs[11:18]
    first, second, spread, sum_second, sum_first, sums, columns, rows, owned = refs[18:]
    step = pl.program_id(0)

    @pl.when(step == 0)
    def _():
        place_weights(co[2], near, far, first, second)
        lat, summed = node[...], incoming[...]
        pre = dot(lat, first[0]) + dot(summed, first[1])
        node_act, node_slope = swish(pre)
        node_act = node_act.astype(BF16)
        node_normed, node_factor = normalize(dot(node_act, second[...]))
        node_out[...] = (lat.astype(F32) + node_normed).astype(BF16)
        upstream = grad_node[...].astype(F32)
        delta = normalize_back(upstream, node_normed, node_factor).astype(BF16)
        put_rows(co, dot_tn(node_act, delta), 6, rows, keep, give)
        pre_grad = (dot_nt(delta, second[...]) * node_slope).astype(BF16)
        put_columns(co, dot_tn(lat, pre_grad), 3, columns, keep, give)
        put_columns(co, dot_tn(summed, pre_grad), 4, columns, keep, give)
        node_total[...] = upstream + dot_nt(pre_grad, first[0])
        spread[...] = dot_nt(pre_grad, first[1]).astype(BF16)
        sum_second[...] = jnp.zeros_like(sum_second)
        sum_first[...] = jnp.zeros_like(sum_first)
        sums[...] = jnp.zeros_like(sums)

    totals = [grad_edge[h, :].astype(F32) + dot(hot[h, :], spread[...]) for h in HALVES]
    deltas = []
    for h, total in zip(HALVES, totals):
        delta = normalize_back(total, normed[h, :].astype(F32), factor[h, 0:1])
        deltas.append(delta.astype(BF16))
    grads = [dot_nt(delta, edge_second[...]) for delta in deltas]
    pre_grads = [(g * slope[h, :].astype(F32)).astype(BF16) for h, g in zip(HALVES, grads)]
    for h, total, pre_grad in zip(HALVES, totals, pre_grads):
        edge_grad[h, :] = (total + dot_nt(pre_grad, whole(edge_first, 0))).astype(BF16)
    pre_grad = jnp.concatenate(pre_grads, axis=0)
    sum_second[...] += dot_tn(act[...], jnp.concatenate(deltas, axis=0))
    sum_first[...] += dot_tn(edge[...], pre_grad)
    sums[...] += dot(turned[...], pre_grad)

    @pl.when(step == STEPS - 1)
    def _():
        put_rows(co, sum_second[...], 5, rows, keep, give)
        put_columns(co, sum_first[...], 0, columns, keep, give)
        received = sums[0:256, :].astype(BF16)
        sent = sums[256:, :].astype(BF16)
        put_columns(co, dot_tn(lookup[...], sent), 1, columns, keep, give)
        put_columns(co, dot_tn(node[...], received), 2, columns, keep, give)
        back = dot_nt(sent, whole(edge_first, 1))
        node_total[...] += back[0:256] + dot_nt(received, whole(edge_first, 2))
        to_prev[...] = back[256:288].astype(BF16)
        to_next[...] = back[288:320].astype(BF16)
        put_owned(co, back[320:832], owned, keep, give)


def final_kernel(co, tiles, far, own, ahead, behind, targets, node_total, *refs):
    edge_first, edge_second, node_first, node_second, node_grad, rows = refs
    for part, core in ((tiles, co[2]), (far, 1 - co[2])):
        for m in range(3):
            value = part[:, m * 16 : (m + 1) * 16, :].astype(F32)
            edge_first[m, :, pl.ds(core, 1)] = value.reshape(16, 1, 16, 128)
        for m in range(2):
            value = part[:, 48 + m * 16 : 64 + m * 16, :].astype(F32)
            node_first[m, :, pl.ds(core, 1)] = value.reshape(16, 1, 16, 128)
        for k in range(16):
            r = k // 2 * 16
            b = pl.ds(pl.multiple_of((k % 2 * 2 + core) * 128, 128), 128)
            edge_second[r : r + 16, b] = part[k, 80:96, :].astype(F32)
            node_second[r : r + 16, b] = part[k, 96:112, :].astype(F32)
    rows[0:32, :] = ahead[...]
    rows[32:64, :] = behind[...]
    group = lax.broadcasted_iota(jnp.int32, (16, 128), 0) // 4
    for b in range(4):
        value = jnp.where(group == b, own[112:128, :].astype(F32), 0.0)
        rows[64:80, b * 128 : (b + 1) * 128] = value.astype(BF16)
    rows[80:128, :] = jnp.zeros((48, 512), BF16)
    match = lax.broadcasted_iota(jnp.int32, (256, 128), 0) == targets[...]
    hot = jnp.where(match, 1.0, 0.0).astype(BF16)
    node_grad[...] = node_total[...] + dot(hot, rows[...])


SMEM = pl.BlockSpec(memory_space=pltpu.SMEM)
WHOLE = pl.BlockSpec(memory_space=pltpu.VMEM)


def shape(*dims, dtype=BF16):
    return jax.ShapeDtypeStruct(dims, dtype)


def plain_call(kernel, scalars, operands, outs, scratch=()):
    return pl.pallas_call(
        kernel,
        in_specs=[SMEM] * len(scalars) + [WHOLE] * len(operands),
        out_specs=[WHOLE] * len(outs),
        out_shape=list(outs),
        scratch_shapes=list(scratch),
        compiler_params=pltpu.CompilerParams(vmem_limit_bytes=VMEM_BYTES),
    )(*scalars, *operands)


def same(*dims):
    return pl.BlockSpec(dims, lambda i: (0,) * len(dims))


def chunk(*dims):
    return pl.BlockSpec(dims, lambda i: (i,) + (0,) * (len(dims) - 1))


def like(value):
    return same(*value.shape)


def halves(first, second, core):
    kinds = first.shape[0]
    top = lax.dynamic_slice_in_dim(first, core * 256, 256, 1).reshape(kinds * 256, 128)
    rest = lax.dynamic_slice_in_dim(second, core * 64, 64, 0)
    rest = rest.reshape(64, 4, 128).transpose(1, 0, 2).reshape(256, 128)
    return jnp.concatenate([top, rest], axis=0)


def shards(
    node_lat,
    edge_lat,
    edge_src,
    edge_dst,
    edge_count,
    halo_send,
    coarse_of,
    edge_w1,
    edge_w2,
    node_w1,
    node_w2,
    grad_node,
    grad_edge,
):
    core = lax.axis_index("core")
    patch = (lax.axis_index("z") * 4 + lax.axis_index("x")) * 2 + core
    co = jnp.stack([patch, patch, core, core, edge_count[0]]).astype(jnp.int32)
    lists, owned = halo_send[0], coarse_of[0]
    unused = jnp.full((48,), -1, jnp.int32)
    targets = jnp.concatenate([lists[1], lists[0], jnp.tile(owned, 4), unused]).reshape(1, 128)

    packed, to_next, to_prev = plain_call(
        pack_kernel,
        [co],
        [node_lat, targets, edge_w1, edge_w2],
        [shape(64, 80, 128), shape(32, 512), shape(32, 512)],
    )
    from_prev = shifted(to_next, 1)
    from_next = shifted(to_prev, -1)
    near = exchange(packed, ("z", "x", "feat")).reshape(16, 4, 80, 128)
    indices = [edge_src.reshape(16, 128), edge_dst.reshape(16, 128)]
    indices += [edge_src.reshape(STEPS, CHUNK), edge_dst.reshape(STEPS, CHUNK)]
    indices = [after(value, packed) for value in indices]
    params = pltpu.CompilerParams(vmem_limit_bytes=VMEM_BYTES, dimension_semantics=("arbitrary",))
    high = TABLE + 256
    hot, turned = pl.pallas_call(
        hot_kernel,
        grid=(STEPS,),
        in_specs=[SMEM] + [like(v) for v in indices],
        out_specs=[chunk(CHUNK, high), pl.BlockSpec((high, CHUNK), lambda i: (0, i))],
        out_shape=[shape(2048, high), shape(high, 2048)],
        compiler_params=params,
        cost_estimate=pl.CostEstimate(
            flops=20_000_000, bytes_accessed=10_000_000, transcendentals=0
        ),
    )(co, *indices)
    near = after(near, from_prev, from_next, hot)
    far = other_core(near)
    node_half = after(repeated(halves(node_w1, node_w2, core), 4), near, far)
    node_near = exchange(node_half, "feat")

    fixed = [node_lat, from_prev, from_next, near, far]
    wide = chunk(CHUNK, 512)
    edge_out, incoming, act, normed, slope, factor, lookup, first, second = pl.pallas_call(
        forward_kernel,
        grid=(STEPS,),
        in_specs=[SMEM]
        + [like(v) for v in fixed]
        + [wide, chunk(CHUNK, high), pl.BlockSpec((256, CHUNK), lambda i: (0, i))],
        out_specs=[wide, same(256, 512), wide, wide, wide, chunk(CHUNK, 128)]
        + [same(TABLE, 512), same(3, 16, 2, 16, 512), same(512, 512)],
        out_shape=[
            shape(2048, 512),
            shape(256, 512),
            shape(2048, 512),
            shape(2048, 512),
            shape(2048, 512),
            shape(2048, 128, dtype=F32),
            shape(TABLE, 512),
            shape(3, 16, 2, 16, 512),
            shape(512, 512),
        ],
        scratch_shapes=[
            pltpu.VMEM((TABLE + 256, 512), BF16),
            pltpu.VMEM((256, 512), F32),
            pltpu.VMEM((16, 2, 4, 16, 128), BF16),
        ],
        compiler_params=params,
        cost_estimate=pl.CostEstimate(
            flops=7_000_000_000, bytes_accessed=18_000_000, transcendentals=1_000_000
        ),
    )(co, *fixed, edge_lat, hot, turned)

    node_near = after(node_near, incoming)
    node_far = other_core(node_near)
    fixed = [node_lat, incoming, grad_node, node_near, node_far]
    fixed += [first, second, lookup]
    moving = [edge_lat, act, normed, slope, factor, grad_edge, hot, turned]
    tiles = (8, 2, 4, 128, 128)
    node_out, node_total, edge_grad, to_prev, to_next, keep, give = pl.pallas_call(
        backward_kernel,
        grid=(STEPS,),
        in_specs=[SMEM]
        + [like(v) for v in fixed]
        + [wide, wide, wide, wide, chunk(CHUNK, 128), wide, chunk(CHUNK, 256)]
        + [pl.BlockSpec((high, CHUNK), lambda i: (0, i))],
        out_specs=[same(256, 512), same(256, 512), wide, same(32, 512), same(32, 512)]
        + [same(*tiles), same(*tiles)],
        out_shape=[
            shape(256, 512),
            shape(256, 512, dtype=F32),
            shape(2048, 512),
            shape(32, 512),
            shape(32, 512),
            shape(*tiles),
            shape(*tiles),
        ],
        scratch_shapes=[
            pltpu.VMEM((2, 512, 512), BF16),
            pltpu.VMEM((512, 512), BF16),
            pltpu.VMEM((256, 512), BF16),
            pltpu.VMEM((512, 512), F32),
            pltpu.VMEM((512, 512), F32),
            pltpu.VMEM((TABLE + 256, 512), F32),
            pltpu.VMEM((16, 2, 16, 512), BF16),
            pltpu.VMEM((4, 512, 128), BF16),
            pltpu.VMEM((16, 2, 4, 16, 128), BF16),
        ],
        compiler_params=params,
        cost_estimate=pl.CostEstimate(
            flops=9_000_000_000, bytes_accessed=24_000_000, transcendentals=100_000
        ),
    )(co, *fixed, *moving)

    pair = (keep.astype(F32) + other_core(give).astype(F32)).astype(BF16).reshape(64, 128, 128)
    ahead = shifted(after(to_prev, pair), -1)
    behind = shifted(after(to_next, pair), 1)
    own = jnp.sum(exchange(pair, ("z", "x", "feat")).astype(F32), axis=0).astype(BF16)
    own = after(own, ahead, behind)
    tiles = exchange(repeated(own[:112], 16), ("z", "x"))
    far_tiles = other_core(tiles)
    edge_first, edge_second, node_first, node_second, node_grad = plain_call(
        final_kernel,
        [co],
        [tiles, far_tiles, own, ahead, behind, targets, node_total],
        [
            shape(3, 16, 2, 16, 128, dtype=F32),
            shape(128, 512, dtype=F32),
            shape(2, 16, 2, 16, 128, dtype=F32),
            shape(128, 512, dtype=F32),
            shape(256, 512, dtype=F32),
        ],
        [pltpu.VMEM((128, 512), BF16)],
    )
    return (
        edge_out,
        node_out,
        node_grad,
        edge_grad,
        edge_first.reshape(3, 512, 128),
        edge_second,
        node_first.reshape(2, 512, 128),
        node_second,
    )


def solution(mesh):
    cube = Mesh(mesh.devices.reshape(4, 4, 2, 4), BOTH)
    rows = P(BOTH, None)
    flat = P(BOTH)
    first, second = P(None, None, "feat"), P("feat", None)
    return jax.shard_map(
        shards,
        mesh=cube,
        in_specs=(
            rows,
            rows,
            flat,
            flat,
            flat,
            P(BOTH, None, None),
            rows,
            first,
            second,
            first,
            second,
            rows,
            rows,
        ),
        out_specs=(rows, rows, rows, rows, first, second, first, second),
        check_vma=False,
    )
```

```python
import jax
import jax.numpy as jnp
from jax import lax
from jax.experimental import pallas as pl
from jax.experimental.pallas import tpu as pltpu
from jax.sharding import Mesh
from jax.sharding import PartitionSpec as P

EPSILON = 1e-05
BF16 = jnp.bfloat16
F32 = jnp.float32
BOTH = ("z", "x", "core", "feat")
CHUNK = 1024
STEPS = 2
TABLE = 896
VMEM_BYTES = 60 * 1024 * 1024


def other_core(value):
    return lax.ppermute(value, "core", [(0, 1), (1, 0)])


def shifted(value, steps):
    return lax.ppermute(value, BOTH, [(k, (k + steps) % 128) for k in range(128)])


def exchange(value, axes):
    return lax.all_to_all(value, axes, 0, 0, tiled=True)


def after(value, *earlier):
    return lax.optimization_barrier((value, *earlier))[0]


def repeated(value, count):
    return jnp.broadcast_to(value[None], (count,) + value.shape)


def dot(left, right):
    return lax.dot_general(left, right, (((1,), (0,)), ((), ())), preferred_element_type=F32)


def dot_nt(left, right):
    return lax.dot_general(left, right, (((1,), (1,)), ((), ())), preferred_element_type=F32)


def dot_tn(left, right):
    return lax.dot_general(left, right, (((0,), (0,)), ((), ())), preferred_element_type=F32)


def mean(values):
    return jnp.mean(values, axis=-1, keepdims=True)


def normalize(values):
    centre = values - mean(values)
    factor = lax.rsqrt(mean(centre * centre) + EPSILON)
    return centre * factor, factor


def normalize_back(upstream, normed, factor):
    return factor * (upstream - mean(upstream) - normed * mean(upstream * normed))


def swish(pre):
    half = 0.5 * pre
    tanh = jnp.tanh(half)
    act = half + half * tanh
    return act, 0.5 * (1.0 + act + tanh * (1.0 - act))


def hot_tiles(rows, count):
    lanes = lax.broadcasted_iota(jnp.int32, (128, 128), 1)
    spread = jnp.transpose(jnp.broadcast_to(rows, (128, 128)))
    return [jnp.where(spread == lanes + 128 * j, 1.0, 0.0).astype(BF16) for j in range(count)]


def hot_kernel(co, src, dst, src_wide, dst_wide, edge, hot, turned, edge_turned):
    step = pl.program_id(0)
    edge_turned[...] = jnp.transpose(edge[...])
    lanes = lax.broadcasted_iota(jnp.int32, (1, 128), 1)
    for r in range(CHUNK // 128):
        row = pl.ds(step * (CHUNK // 128) + r, 1)
        live = lanes + step * CHUNK + r * 128 < co[4]
        tiles = hot_tiles(jnp.where(live, dst[row, :], -1), 2) + hot_tiles(src[row, :], 7)
        hot[r * 128 : (r + 1) * 128, :] = jnp.concatenate(tiles, axis=1)
    place = lax.broadcasted_iota(jnp.int32, (128, CHUNK), 0)
    lanes = lax.broadcasted_iota(jnp.int32, (1, CHUNK), 1)
    src_row = src_wide[pl.ds(step, 1), :]
    dst_row = jnp.where(lanes + step * CHUNK < co[4], dst_wide[pl.ds(step, 1), :], -1)
    for j in range(9):
        match = place + 128 * j == dst_row if j < 2 else place + 128 * (j - 2) == src_row
        turned[j * 128 : (j + 1) * 128, :] = jnp.where(match, 1.0, 0.0).astype(BF16)


def pack_kernel(co, node, targets, edge_first, edge_second, first, second, *outs):
    tiles, to_next, to_prev, packed = outs
    match = lax.broadcasted_iota(jnp.int32, (256, 128), 0) == targets[...]
    rows = dot_tn(jnp.where(match, 1.0, 0.0).astype(BF16), node[...])
    to_next[...] = rows[0:32].astype(BF16)
    to_prev[...] = rows[32:64].astype(BF16)
    group = lax.broadcasted_iota(jnp.int32, (16, 128), 0) // 4
    coarse = jnp.zeros((16, 128), F32)
    for b in range(4):
        coarse = jnp.where(group == b, rows[64:80, b * 128 : (b + 1) * 128], coarse)
    patch = co[0]
    at = pl.ds(pl.multiple_of(patch * 16, 16), 16)
    parts = [edge_first[m, at, :] for m in range(3)]
    row = pl.ds(pl.multiple_of(patch // 4 * 16, 16), 16)
    parts.append(edge_second[row, pl.ds(pl.multiple_of(patch % 4 * 128, 128), 128)])
    parts.append(coarse.astype(BF16))
    tile = jnp.concatenate(parts, axis=0)
    for k in range(64):
        tiles[k] = tile
    at = pl.ds(pl.multiple_of(co[2] * 256, 256), 256)
    row = pl.ds(pl.multiple_of(co[2] * 64, 64), 64)
    for y in range(4):
        for m in range(2):
            packed[y, m * 256 : (m + 1) * 256, :] = first[m, at, :]
        for b in range(4):
            rows = slice(512 + b * 64, 576 + b * 64)
            packed[y, rows, :] = second[row, b * 128 : (b + 1) * 128]


def live_rows(step, count):
    place = lax.broadcasted_iota(jnp.int32, (CHUNK, 1), 0) + step * CHUNK
    return jnp.where(place < count, 1.0, 0.0)


HALVES = (slice(0, CHUNK // 2), slice(CHUNK // 2, CHUNK))


def place_weights(core, near, far, first, second):
    kinds = first.shape[0]
    for part, half in ((near, core), (far, 1 - core)):
        for y in range(4):
            rows = pl.ds(pl.multiple_of(half * 256, 256), 256)
            for m in range(kinds):
                first[m, rows, y * 128 : (y + 1) * 128] = part[y, m * 256 : (m + 1) * 256, :]
            rows = pl.ds(pl.multiple_of(y * 128 + half * 64, 64), 64)
            for b in range(4):
                start = kinds * 256 + b * 64
                second[rows, b * 128 : (b + 1) * 128] = part[y, start : start + 64, :]


def whole(first, m):
    return first[m].reshape(512, 512)


def place_tiles(own_core, near, far, lookup, first, second, coarse):
    for part, core in ((near, own_core), (far, 1 - own_core)):
        for y in range(4):
            block = slice(y * 128, (y + 1) * 128)
            for m in range(3):
                value = part[:, y, m * 16 : (m + 1) * 16, :].reshape(16, 1, 16, 128)
                first[m, :, pl.ds(core, 1), :, block] = value
            for k in range(16):
                rows = slice(y * 128 + k // 2 * 16, y * 128 + k // 2 * 16 + 16)
                columns = pl.ds(pl.multiple_of((k % 2 * 2 + core) * 128, 128), 128)
                second[rows, columns] = part[k, y, 48:64, :]
            coarse[:, pl.ds(core, 1), y] = part[:, y, 64:80, :].reshape(16, 1, 16, 128)
    low = lax.broadcasted_iota(jnp.int32, (64, 8, 128), 1) < 4
    pairs = coarse[...].reshape(64, 2, 16, 128).astype(F32)
    for half in range(2):
        even, odd = pairs[:, 0, half * 8 : half * 8 + 8], pairs[:, 1, half * 8 : half * 8 + 8]
        first_block = jnp.where(low, even, pltpu.roll(odd, 4, 1)).reshape(512, 128)
        other_block = jnp.where(low, pltpu.roll(even, 4, 1), odd).reshape(512, 128)
        lookup[320:832, half * 256 : half * 256 + 128] = first_block.astype(BF16)
        lookup[320:832, half * 256 + 128 : half * 256 + 256] = other_block.astype(BF16)


def forward_kernel(co, node, prev, following, near, far, edge, hot, turned, *refs):
    edge_out, incoming, act_out, normed_out, slope_out, factor_out, lookup, first, second = refs[:9]
    table, total, coarse = refs[9:]
    step = pl.program_id(0)

    @pl.when(step == 0)
    def _():
        lookup[0:256, :] = node[...]
        lookup[256:288, :] = prev[...]
        lookup[288:320, :] = following[...]
        lookup[832:896, :] = jnp.zeros((64, 512), BF16)
        place_tiles(co[2], near, far, lookup, first, second, coarse)
        table[0:256, :] = dot(node[...], whole(first, 2)).astype(BF16)
        table[256:, :] = dot(lookup[...], whole(first, 1)).astype(BF16)
        total[...] = jnp.zeros_like(total)

    live = live_rows(step, co[4])
    pres = [dot(edge[h, :], whole(first, 0)) + dot(hot[h, :], table[...]) for h in HALVES]
    acts = []
    for h, pre in zip(HALVES, pres):
        act, slope = swish(pre)
        acts.append(act.astype(BF16))
        act_out[h, :] = acts[-1]
        slope_out[h, :] = slope.astype(BF16)
    values = [dot(act, second[...]) for act in acts]
    for h, value in zip(HALVES, values):
        centre = value - mean(value)
        factor = lax.rsqrt(mean(centre * centre) + EPSILON) * live[h]
        normed = centre * factor
        normed_out[h, :] = normed.astype(BF16)
        factor_out[h, :] = jnp.broadcast_to(factor, (CHUNK // 2, 128))
        edge_out[h, :] = (edge[h, :].astype(F32) + normed).astype(BF16)
    total[...] += dot(turned[...], edge_out[...])

    @pl.when(step == STEPS - 1)
    def _():
        incoming[...] = total[...].astype(BF16)


def put_columns(co, grad, slot, scratch, keep, give):
    scratch[...] = grad.astype(BF16).reshape(16, 2, 16, 512)
    for target, core in ((keep, co[2]), (give, 1 - co[2])):
        value = scratch[:, pl.ds(core, 1), :, :].reshape(8, 2, 16, 512)
        for y in range(4):
            target[:, :, y, slot * 16 : (slot + 1) * 16, :] = value[:, :, :, y * 128 : (y + 1) * 128]


def put_rows(co, grad, slot, scratch, keep, give):
    for b in range(4):
        scratch[b] = grad[:, b * 128 : (b + 1) * 128].astype(BF16)
    for target, core in ((keep, co[2]), (give, 1 - co[2])):
        for h in range(2):
            value = scratch[2 * h + core].reshape(4, 8, 16, 128)
            for y in range(4):
                target[:, h, y, slot * 16 : (slot + 1) * 16, :] = value[y]


def put_owned(co, grad, scratch, keep, give):
    rows = grad.reshape(64, 8, 512)
    turned = pltpu.roll(rows, 4, 1)
    low = lax.broadcasted_iota(jnp.int32, (64, 8, 128), 1) < 4
    for odd in range(2):
        left, right = (turned, rows) if odd else (rows, turned)
        parts = [
            jnp.where(low, left[:, :, b : b + 128], right[:, :, b + 128 : b + 256]) for b in (0, 256)
        ]
        tile = jnp.concatenate(parts, axis=1).astype(BF16).reshape(16, 2, 2, 16, 128)
        for pair in range(2):
            scratch[:, :, pair * 2 + odd] = tile[:, :, pair]
    for target, core in ((keep, co[2]), (give, 1 - co[2])):
        value = scratch[:, pl.ds(core, 1)].reshape(8, 2, 4, 16, 128)
        target[:, :, :, 112:128, :] = value


def backward_kernel(co, node, incoming, grad_node, near, far, *refs):
    edge_first, edge_second, lookup = refs[:3]
    edge_turned, act, normed, slope, factor, grad_edge, hot, turned = refs[3:11]
    node_out, node_total, edge_grad, to_prev, to_next, keep, give = refs[11:18]
    first, second, spread, sum_second, sum_first, sums, columns, rows, owned = refs[18:]
    step = pl.program_id(0)

    @pl.when(step == 0)
    def _():
        place_weights(co[2], near, far, first, second)
        lat, summed = node[...], incoming[...]
        pre = dot(lat, first[0]) + dot(summed, first[1])
        node_act, node_slope = swish(pre)
        node_act = node_act.astype(BF16)
        node_normed, node_factor = normalize(dot(node_act, second[...]))
        node_out[...] = (lat.astype(F32) + node_normed).astype(BF16)
        upstream = grad_node[...].astype(F32)
        delta = normalize_back(upstream, node_normed, node_factor).astype(BF16)
        put_rows(co, dot_tn(node_act, delta), 6, rows, keep, give)
        pre_grad = (dot_nt(delta, second[...]) * node_slope).astype(BF16)
        put_columns(co, dot_tn(lat, pre_grad), 3, columns, keep, give)
        put_columns(co, dot_tn(summed, pre_grad), 4, columns, keep, give)
        node_total[...] = upstream + dot_nt(pre_grad, first[0])
        spread[...] = dot_nt(pre_grad, first[1]).astype(BF16)
        sum_second[...] = jnp.zeros_like(sum_second)
        sum_first[...] = jnp.zeros_like(sum_first)
        sums[...] = jnp.zeros_like(sums)

    totals = [grad_edge[h, :].astype(F32) + dot(hot[h, :], spread[...]) for h in HALVES]
    deltas = []
    for h, total in zip(HALVES, totals):
        delta = normalize_back(total, normed[h, :].astype(F32), factor[h, 0:1])
        deltas.append(delta.astype(BF16))
    grads = [dot_nt(delta, edge_second[...]) for delta in deltas]
    pre_grads = [(g * slope[h, :].astype(F32)).astype(BF16) for h, g in zip(HALVES, grads)]
    for h, total, pre_grad in zip(HALVES, totals, pre_grads):
        edge_grad[h, :] = (total + dot_nt(pre_grad, whole(edge_first, 0))).astype(BF16)
    pre_grad = jnp.concatenate(pre_grads, axis=0)
    sum_second[...] += dot_tn(act[...], jnp.concatenate(deltas, axis=0))
    sum_first[...] += dot(edge_turned[...], pre_grad)
    sums[...] += dot(turned[...], pre_grad)

    @pl.when(step == STEPS - 1)
    def _():
        put_rows(co, sum_second[...], 5, rows, keep, give)
        put_columns(co, sum_first[...], 0, columns, keep, give)
        received = sums[0:256, :].astype(BF16)
        sent = sums[256:, :].astype(BF16)
        put_columns(co, dot_tn(lookup[...], sent), 1, columns, keep, give)
        put_columns(co, dot_tn(node[...], received), 2, columns, keep, give)
        back = dot_nt(sent, whole(edge_first, 1))
        node_total[...] += back[0:256] + dot_nt(received, whole(edge_first, 2))
        to_prev[...] = back[256:288].astype(BF16)
        to_next[...] = back[288:320].astype(BF16)
        put_owned(co, back[320:832], owned, keep, give)


def final_kernel(co, tiles, far, own, ahead, behind, targets, node_total, *refs):
    edge_first, edge_second, node_first, node_second, node_grad, rows = refs
    for part, core in ((tiles, co[2]), (far, 1 - co[2])):
        for m in range(3):
            value = part[:, m * 16 : (m + 1) * 16, :].astype(F32)
            edge_first[m, :, pl.ds(core, 1)] = value.reshape(16, 1, 16, 128)
        for m in range(2):
            value = part[:, 48 + m * 16 : 64 + m * 16, :].astype(F32)
            node_first[m, :, pl.ds(core, 1)] = value.reshape(16, 1, 16, 128)
        for k in range(16):
            r = k // 2 * 16
            b = pl.ds(pl.multiple_of((k % 2 * 2 + core) * 128, 128), 128)
            edge_second[r : r + 16, b] = part[k, 80:96, :].astype(F32)
            node_second[r : r + 16, b] = part[k, 96:112, :].astype(F32)
    rows[0:32, :] = ahead[...]
    rows[32:64, :] = behind[...]
    group = lax.broadcasted_iota(jnp.int32, (16, 128), 0) // 4
    for b in range(4):
        value = jnp.where(group == b, own[112:128, :].astype(F32), 0.0)
        rows[64:80, b * 128 : (b + 1) * 128] = value.astype(BF16)
    rows[80:128, :] = jnp.zeros((48, 512), BF16)
    match = lax.broadcasted_iota(jnp.int32, (256, 128), 0) == targets[...]
    hot = jnp.where(match, 1.0, 0.0).astype(BF16)
    node_grad[...] = node_total[...] + dot(hot, rows[...])


SMEM = pl.BlockSpec(memory_space=pltpu.SMEM)
WHOLE = pl.BlockSpec(memory_space=pltpu.VMEM)


def shape(*dims, dtype=BF16):
    return jax.ShapeDtypeStruct(dims, dtype)


def plain_call(kernel, scalars, operands, outs, scratch=()):
    return pl.pallas_call(
        kernel,
        in_specs=[SMEM] * len(scalars) + [WHOLE] * len(operands),
        out_specs=[WHOLE] * len(outs),
        out_shape=list(outs),
        scratch_shapes=list(scratch),
        compiler_params=pltpu.CompilerParams(vmem_limit_bytes=VMEM_BYTES),
    )(*scalars, *operands)


def same(*dims):
    return pl.BlockSpec(dims, lambda i: (0,) * len(dims))


def chunk(*dims):
    return pl.BlockSpec(dims, lambda i: (i,) + (0,) * (len(dims) - 1))


def column(*dims):
    return pl.BlockSpec(dims, lambda i: (0, i))


def like(value):
    dims = value.shape
    once = pl.Buffered(buffer_count=1)
    return pl.BlockSpec(dims, lambda i: (0,) * len(dims), pipeline_mode=once)


def shards(
    node_lat,
    edge_lat,
    edge_src,
    edge_dst,
    edge_count,
    halo_send,
    coarse_of,
    edge_w1,
    edge_w2,
    node_w1,
    node_w2,
    grad_node,
    grad_edge,
):
    core = lax.axis_index("core")
    patch = (lax.axis_index("z") * 4 + lax.axis_index("x")) * 2 + core
    co = jnp.stack([patch, patch, core, core, edge_count[0]]).astype(jnp.int32)
    lists, owned = halo_send[0], coarse_of[0]
    unused = jnp.full((48,), -1, jnp.int32)
    targets = jnp.concatenate([lists[1], lists[0], jnp.tile(owned, 4), unused]).reshape(1, 128)

    packed, to_next, to_prev, node_half = plain_call(
        pack_kernel,
        [co],
        [node_lat, targets, edge_w1, edge_w2, node_w1, node_w2],
        [shape(64, 80, 128), shape(32, 512), shape(32, 512), shape(4, 768, 128)],
    )
    from_prev = shifted(to_next, 1)
    from_next = shifted(to_prev, -1)
    near = exchange(packed, ("z", "x", "feat")).reshape(16, 4, 80, 128)
    indices = [edge_src.reshape(16, 128), edge_dst.reshape(16, 128)]
    indices += [edge_src.reshape(STEPS, CHUNK), edge_dst.reshape(STEPS, CHUNK)]
    indices = [after(value, packed) for value in indices]
    params = pltpu.CompilerParams(vmem_limit_bytes=VMEM_BYTES, dimension_semantics=("arbitrary",))
    high = TABLE + 256
    wide = chunk(CHUNK, 512)
    hot, turned, edge_turned = pl.pallas_call(
        hot_kernel,
        grid=(STEPS,),
        in_specs=[SMEM] + [like(v) for v in indices] + [wide],
        out_specs=[chunk(CHUNK, high), column(high, CHUNK), column(512, CHUNK)],
        out_shape=[shape(2048, high), shape(high, 2048), shape(512, 2048)],
        compiler_params=params,
        cost_estimate=pl.CostEstimate(
            flops=20_000_000, bytes_accessed=14_000_000, transcendentals=0
        ),
    )(co, *indices, edge_lat)
    near = after(near, from_prev, from_next, hot)
    far = other_core(near)
    node_near = exchange(after(node_half, near, far), "feat")

    fixed = [node_lat, from_prev, from_next, near, far]
    wide = chunk(CHUNK, 512)
    edge_out, incoming, act, normed, slope, factor, lookup, first, second = pl.pallas_call(
        forward_kernel,
        grid=(STEPS,),
        in_specs=[SMEM]
        + [like(v) for v in fixed]
        + [wide, chunk(CHUNK, high), column(256, CHUNK)],
        out_specs=[wide, same(256, 512), wide, wide, wide, chunk(CHUNK, 128)]
        + [same(TABLE, 512), same(3, 16, 2, 16, 512), same(512, 512)],
        out_shape=[
            shape(2048, 512),
            shape(256, 512),
            shape(2048, 512),
            shape(2048, 512),
            shape(2048, 512),
            shape(2048, 128, dtype=F32),
            shape(TABLE, 512),
            shape(3, 16, 2, 16, 512),
            shape(512, 512),
        ],
        scratch_shapes=[
            pltpu.VMEM((TABLE + 256, 512), BF16),
            pltpu.VMEM((256, 512), F32),
            pltpu.VMEM((16, 2, 4, 16, 128), BF16),
        ],
        compiler_params=params,
        cost_estimate=pl.CostEstimate(
            flops=7_000_000_000, bytes_accessed=18_000_000, transcendentals=1_000_000
        ),
    )(co, *fixed, edge_lat, hot, turned)

    node_near = after(node_near, incoming)
    node_far = other_core(node_near)
    fixed = [node_lat, incoming, grad_node, node_near, node_far]
    fixed += [first, second, lookup]
    moving = [edge_turned, act, normed, slope, factor, grad_edge, hot, turned]
    tiles = (8, 2, 4, 128, 128)
    node_out, node_total, edge_grad, to_prev, to_next, keep, give = pl.pallas_call(
        backward_kernel,
        grid=(STEPS,),
        in_specs=[SMEM]
        + [like(v) for v in fixed]
        + [column(512, CHUNK), wide, wide, wide, chunk(CHUNK, 128), wide, chunk(CHUNK, 256)]
        + [column(high, CHUNK)],
        out_specs=[same(256, 512), same(256, 512), wide, same(32, 512), same(32, 512)]
        + [same(*tiles), same(*tiles)],
        out_shape=[
            shape(256, 512),
            shape(256, 512, dtype=F32),
            shape(2048, 512),
            shape(32, 512),
            shape(32, 512),
            shape(*tiles),
            shape(*tiles),
        ],
        scratch_shapes=[
            pltpu.VMEM((2, 512, 512), BF16),
            pltpu.VMEM((512, 512), BF16),
            pltpu.VMEM((256, 512), BF16),
            pltpu.VMEM((512, 512), F32),
            pltpu.VMEM((512, 512), F32),
            pltpu.VMEM((TABLE + 256, 512), F32),
            pltpu.VMEM((16, 2, 16, 512), BF16),
            pltpu.VMEM((4, 512, 128), BF16),
            pltpu.VMEM((16, 2, 4, 16, 128), BF16),
        ],
        compiler_params=params,
        cost_estimate=pl.CostEstimate(
            flops=9_000_000_000, bytes_accessed=24_000_000, transcendentals=100_000
        ),
    )(co, *fixed, *moving)

    pair = (keep.astype(F32) + other_core(give).astype(F32)).astype(BF16).reshape(64, 128, 128)
    ahead = shifted(after(to_prev, pair), -1)
    behind = shifted(after(to_next, pair), 1)
    own = jnp.sum(exchange(pair, ("z", "x", "feat")).astype(F32), axis=0).astype(BF16)
    own = after(own, ahead, behind)
    tiles = exchange(repeated(own[:112], 16), ("z", "x"))
    far_tiles = other_core(tiles)
    edge_first, edge_second, node_first, node_second, node_grad = plain_call(
        final_kernel,
        [co],
        [tiles, far_tiles, own, ahead, behind, targets, node_total],
        [
            shape(3, 16, 2, 16, 128, dtype=F32),
            shape(128, 512, dtype=F32),
            shape(2, 16, 2, 16, 128, dtype=F32),
            shape(128, 512, dtype=F32),
            shape(256, 512, dtype=F32),
        ],
        [pltpu.VMEM((128, 512), BF16)],
    )
    return (
        edge_out,
        node_out,
        node_grad,
        edge_grad,
        edge_first.reshape(3, 512, 128),
        edge_second,
        node_first.reshape(2, 512, 128),
        node_second,
    )


def solution(mesh):
    cube = Mesh(mesh.devices.reshape(4, 4, 2, 4), BOTH)
    rows = P(BOTH, None)
    flat = P(BOTH)
    first, second = P(None, None, "feat"), P("feat", None)
    return jax.shard_map(
        shards,
        mesh=cube,
        in_specs=(
            rows,
            rows,
            flat,
            flat,
            flat,
            P(BOTH, None, None),
            rows,
            first,
            second,
            first,
            second,
            rows,
            rows,
        ),
        out_specs=(rows, rows, rows, rows, first, second, first, second),
        check_vma=False,
    )
```

```python
import jax
import jax.numpy as jnp
from jax import lax
from jax.experimental import pallas as pl
from jax.experimental.pallas import tpu as pltpu
from jax.sharding import Mesh
from jax.sharding import PartitionSpec as P

EPSILON = 1e-05
BF16 = jnp.bfloat16
F32 = jnp.float32
BOTH = ("z", "x", "core", "feat")
CHUNK = 512
STEPS = 4
TABLE = 896
MIB = 1024 * 1024


def other_core(value):
    return lax.ppermute(value, "core", [(0, 1), (1, 0)])


def shifted(value, steps):
    return lax.ppermute(value, BOTH, [(k, (k + steps) % 128) for k in range(128)])


def exchange(value, axes):
    return lax.all_to_all(value, axes, 0, 0, tiled=True)


def after(value, *earlier):
    return lax.optimization_barrier((value, *earlier))[0]


def repeated(value, count):
    return jnp.broadcast_to(value[None], (count,) + value.shape)


def dot(left, right):
    return lax.dot_general(left, right, (((1,), (0,)), ((), ())), preferred_element_type=F32)


def dot_nt(left, right):
    return lax.dot_general(left, right, (((1,), (1,)), ((), ())), preferred_element_type=F32)


def dot_tn(left, right):
    return lax.dot_general(left, right, (((0,), (0,)), ((), ())), preferred_element_type=F32)


def mean(values):
    return jnp.mean(values, axis=-1, keepdims=True)


def normalize(values):
    centre = values - mean(values)
    factor = lax.rsqrt(mean(centre * centre) + EPSILON)
    return centre * factor, factor


def normalize_back(upstream, normed, factor):
    return factor * (upstream - mean(upstream) - normed * mean(upstream * normed))


def swish(pre):
    half = 0.5 * pre
    tanh = jnp.tanh(half)
    act = half + half * tanh
    return act, 0.5 * (1.0 + act + tanh * (1.0 - act))


def hot_tiles(rows, count):
    lanes = lax.broadcasted_iota(jnp.int32, (128, 128), 1)
    spread = jnp.transpose(jnp.broadcast_to(rows, (128, 128)))
    return [jnp.where(spread == lanes + 128 * j, 1.0, 0.0).astype(BF16) for j in range(count)]


def hot_kernel(co, src, dst, src_wide, dst_wide, edge, hot, turned, edge_turned):
    step = pl.program_id(0)
    edge_turned[...] = jnp.transpose(edge[...])
    lanes = lax.broadcasted_iota(jnp.int32, (1, 128), 1)
    for r in range(CHUNK // 128):
        row = pl.ds(step * (CHUNK // 128) + r, 1)
        live = lanes + step * CHUNK + r * 128 < co[4]
        tiles = hot_tiles(jnp.where(live, dst[row, :], -1), 2) + hot_tiles(src[row, :], 7)
        hot[r * 128 : (r + 1) * 128, :] = jnp.concatenate(tiles, axis=1)
    place = lax.broadcasted_iota(jnp.int32, (128, CHUNK), 0)
    lanes = lax.broadcasted_iota(jnp.int32, (1, CHUNK), 1)
    src_row = src_wide[pl.ds(step, 1), :]
    dst_row = jnp.where(lanes + step * CHUNK < co[4], dst_wide[pl.ds(step, 1), :], -1)
    for j in range(9):
        match = place + 128 * j == dst_row if j < 2 else place + 128 * (j - 2) == src_row
        turned[j * 128 : (j + 1) * 128, :] = jnp.where(match, 1.0, 0.0).astype(BF16)


def pack_kernel(co, node, targets, edge_first, edge_second, first, second, *outs):
    tiles, to_next, to_prev, packed = outs
    match = lax.broadcasted_iota(jnp.int32, (256, 128), 0) == targets[...]
    rows = dot_tn(jnp.where(match, 1.0, 0.0).astype(BF16), node[...])
    to_next[...] = rows[0:32].astype(BF16)
    to_prev[...] = rows[32:64].astype(BF16)
    group = lax.broadcasted_iota(jnp.int32, (16, 128), 0) // 4
    coarse = jnp.zeros((16, 128), F32)
    for b in range(4):
        coarse = jnp.where(group == b, rows[64:80, b * 128 : (b + 1) * 128], coarse)
    patch = co[0]
    at = pl.ds(pl.multiple_of(patch * 16, 16), 16)
    parts = [edge_first[m, at, :] for m in range(3)]
    row = pl.ds(pl.multiple_of(patch // 4 * 16, 16), 16)
    parts.append(edge_second[row, pl.ds(pl.multiple_of(patch % 4 * 128, 128), 128)])
    parts.append(coarse.astype(BF16))
    tile = jnp.concatenate(parts, axis=0)
    for k in range(64):
        tiles[k] = tile
    at = pl.ds(pl.multiple_of(co[2] * 256, 256), 256)
    row = pl.ds(pl.multiple_of(co[2] * 64, 64), 64)
    for y in range(4):
        for m in range(2):
            packed[y, m * 256 : (m + 1) * 256, :] = first[m, at, :]
        for b in range(4):
            rows = slice(512 + b * 64, 576 + b * 64)
            packed[y, rows, :] = second[row, b * 128 : (b + 1) * 128]


def live_rows(step, count):
    place = lax.broadcasted_iota(jnp.int32, (CHUNK, 1), 0) + step * CHUNK
    return jnp.where(place < count, 1.0, 0.0)


HALVES = (slice(0, CHUNK // 2), slice(CHUNK // 2, CHUNK))


def place_weights(core, near, far, first, second):
    kinds = first.shape[0]
    for part, half in ((near, core), (far, 1 - core)):
        for y in range(4):
            rows = pl.ds(pl.multiple_of(half * 256, 256), 256)
            for m in range(kinds):
                first[m, rows, y * 128 : (y + 1) * 128] = part[y, m * 256 : (m + 1) * 256, :]
            rows = pl.ds(pl.multiple_of(y * 128 + half * 64, 64), 64)
            for b in range(4):
                start = kinds * 256 + b * 64
                second[rows, b * 128 : (b + 1) * 128] = part[y, start : start + 64, :]


def whole(first, m):
    return first[m].reshape(512, 512)


def place_tiles(own_core, near, far, lookup, first, second, coarse):
    for part, core in ((near, own_core), (far, 1 - own_core)):
        for y in range(4):
            block = slice(y * 128, (y + 1) * 128)
            for m in range(3):
                value = part[:, y, m * 16 : (m + 1) * 16, :].reshape(16, 1, 16, 128)
                first[m, :, pl.ds(core, 1), :, block] = value
            for k in range(16):
                rows = slice(y * 128 + k // 2 * 16, y * 128 + k // 2 * 16 + 16)
                columns = pl.ds(pl.multiple_of((k % 2 * 2 + core) * 128, 128), 128)
                second[rows, columns] = part[k, y, 48:64, :]
            coarse[:, pl.ds(core, 1), y] = part[:, y, 64:80, :].reshape(16, 1, 16, 128)
    low = lax.broadcasted_iota(jnp.int32, (64, 8, 128), 1) < 4
    pairs = coarse[...].reshape(64, 2, 16, 128).astype(F32)
    for half in range(2):
        even, odd = pairs[:, 0, half * 8 : half * 8 + 8], pairs[:, 1, half * 8 : half * 8 + 8]
        first_block = jnp.where(low, even, pltpu.roll(odd, 4, 1)).reshape(512, 128)
        other_block = jnp.where(low, pltpu.roll(even, 4, 1), odd).reshape(512, 128)
        lookup[320:832, half * 256 : half * 256 + 128] = first_block.astype(BF16)
        lookup[320:832, half * 256 + 128 : half * 256 + 256] = other_block.astype(BF16)


def forward_kernel(co, node, prev, following, near, far, edge, hot, turned, *refs):
    edge_out, incoming, act_out, normed_out, slope_out, factor_out, lookup, first, second = refs[:9]
    table, total, coarse = refs[9:]
    step = pl.program_id(0)

    @pl.when(step == 0)
    def _():
        lookup[0:256, :] = node[...]
        lookup[256:288, :] = prev[...]
        lookup[288:320, :] = following[...]
        lookup[832:896, :] = jnp.zeros((64, 512), BF16)
        place_tiles(co[2], near, far, lookup, first, second, coarse)
        table[0:256, :] = dot(node[...], whole(first, 2)).astype(BF16)
        table[256:, :] = dot(lookup[...], whole(first, 1)).astype(BF16)
        total[...] = jnp.zeros_like(total)

    live = live_rows(step, co[4])
    pres = [dot(edge[h, :], whole(first, 0)) + dot(hot[h, :], table[...]) for h in HALVES]
    acts = []
    for h, pre in zip(HALVES, pres):
        act, slope = swish(pre)
        acts.append(act.astype(BF16))
        act_out[h, :] = acts[-1]
        slope_out[h, :] = slope.astype(BF16)
    values = [dot(act, second[...]) for act in acts]
    for h, value in zip(HALVES, values):
        centre = value - mean(value)
        factor = lax.rsqrt(mean(centre * centre) + EPSILON) * live[h]
        normed = centre * factor
        normed_out[h, :] = normed.astype(BF16)
        factor_out[h, :] = jnp.broadcast_to(factor, (CHUNK // 2, 128))
        edge_out[h, :] = (edge[h, :].astype(F32) + normed).astype(BF16)
    total[...] += dot(turned[...], edge_out[...])

    @pl.when(step == STEPS - 1)
    def _():
        incoming[...] = total[...].astype(BF16)


def put_columns(co, grad, slot, scratch, keep, give):
    scratch[...] = grad.astype(BF16).reshape(16, 2, 16, 512)
    for target, core in ((keep, co[2]), (give, 1 - co[2])):
        value = scratch[:, pl.ds(core, 1), :, :].reshape(8, 2, 16, 512)
        for y in range(4):
            target[:, :, y, slot * 16 : (slot + 1) * 16, :] = value[:, :, :, y * 128 : (y + 1) * 128]


def put_rows(co, grad, slot, scratch, keep, give):
    for b in range(4):
        scratch[b] = grad[:, b * 128 : (b + 1) * 128].astype(BF16)
    for target, core in ((keep, co[2]), (give, 1 - co[2])):
        for h in range(2):
            value = scratch[2 * h + core].reshape(4, 8, 16, 128)
            for y in range(4):
                target[:, h, y, slot * 16 : (slot + 1) * 16, :] = value[y]


def put_owned(co, grad, scratch, keep, give):
    rows = grad.reshape(64, 8, 512)
    turned = pltpu.roll(rows, 4, 1)
    low = lax.broadcasted_iota(jnp.int32, (64, 8, 128), 1) < 4
    for odd in range(2):
        left, right = (turned, rows) if odd else (rows, turned)
        parts = [
            jnp.where(low, left[:, :, b : b + 128], right[:, :, b + 128 : b + 256]) for b in (0, 256)
        ]
        tile = jnp.concatenate(parts, axis=1).astype(BF16).reshape(16, 2, 2, 16, 128)
        for pair in range(2):
            scratch[:, :, pair * 2 + odd] = tile[:, :, pair]
    for target, core in ((keep, co[2]), (give, 1 - co[2])):
        value = scratch[:, pl.ds(core, 1)].reshape(8, 2, 4, 16, 128)
        target[:, :, :, 112:128, :] = value


def backward_kernel(co, node, incoming, grad_node, near, far, *refs):
    edge_first, edge_second, lookup = refs[:3]
    edge_turned, act, normed, slope, factor, grad_edge, hot, turned = refs[3:11]
    node_out, node_total, edge_grad, to_prev, to_next, keep, give = refs[11:18]
    first, second, spread, sum_second, sum_first, sums, columns, rows, owned = refs[18:]
    step = pl.program_id(0)

    @pl.when(step == 0)
    def _():
        place_weights(co[2], near, far, first, second)
        lat, summed = node[...], incoming[...]
        pre = dot(lat, first[0]) + dot(summed, first[1])
        node_act, node_slope = swish(pre)
        node_act = node_act.astype(BF16)
        node_normed, node_factor = normalize(dot(node_act, second[...]))
        node_out[...] = (lat.astype(F32) + node_normed).astype(BF16)
        upstream = grad_node[...].astype(F32)
        delta = normalize_back(upstream, node_normed, node_factor).astype(BF16)
        put_rows(co, dot_tn(node_act, delta), 6, rows, keep, give)
        pre_grad = (dot_nt(delta, second[...]) * node_slope).astype(BF16)
        put_columns(co, dot_tn(lat, pre_grad), 3, columns, keep, give)
        put_columns(co, dot_tn(summed, pre_grad), 4, columns, keep, give)
        node_total[...] = upstream + dot_nt(pre_grad, first[0])
        spread[...] = dot_nt(pre_grad, first[1]).astype(BF16)
        sum_second[...] = jnp.zeros_like(sum_second)
        sum_first[...] = jnp.zeros_like(sum_first)
        sums[...] = jnp.zeros_like(sums)

    totals = [grad_edge[h, :].astype(F32) + dot(hot[h, :], spread[...]) for h in HALVES]
    deltas = []
    for h, total in zip(HALVES, totals):
        delta = normalize_back(total, normed[h, :].astype(F32), factor[h, 0:1])
        deltas.append(delta.astype(BF16))
    grads = [dot_nt(delta, edge_second[...]) for delta in deltas]
    pre_grads = [(g * slope[h, :].astype(F32)).astype(BF16) for h, g in zip(HALVES, grads)]
    for h, total, pre_grad in zip(HALVES, totals, pre_grads):
        edge_grad[h, :] = (total + dot_nt(pre_grad, whole(edge_first, 0))).astype(BF16)
    pre_grad = jnp.concatenate(pre_grads, axis=0)
    sum_second[...] += dot_tn(act[...], jnp.concatenate(deltas, axis=0))
    sum_first[...] += dot(edge_turned[...], pre_grad)
    sums[...] += dot(turned[...], pre_grad)

    @pl.when(step == STEPS - 1)
    def _():
        put_rows(co, sum_second[...], 5, rows, keep, give)
        put_columns(co, sum_first[...], 0, columns, keep, give)
        received = sums[0:256, :].astype(BF16)
        sent = sums[256:, :].astype(BF16)
        put_columns(co, dot_tn(lookup[...], sent), 1, columns, keep, give)
        put_columns(co, dot_tn(node[...], received), 2, columns, keep, give)
        back = dot_nt(sent, whole(edge_first, 1))
        node_total[...] += back[0:256] + dot_nt(received, whole(edge_first, 2))
        to_prev[...] = back[256:288].astype(BF16)
        to_next[...] = back[288:320].astype(BF16)
        put_owned(co, back[320:832], owned, keep, give)


def final_kernel(co, tiles, far, own, ahead, behind, targets, node_total, *refs):
    edge_first, edge_second, node_first, node_second, node_grad, rows = refs
    for part, core in ((tiles, co[2]), (far, 1 - co[2])):
        for m in range(3):
            value = part[:, m * 16 : (m + 1) * 16, :].astype(F32)
            edge_first[m, :, pl.ds(core, 1)] = value.reshape(16, 1, 16, 128)
        for m in range(2):
            value = part[:, 48 + m * 16 : 64 + m * 16, :].astype(F32)
            node_first[m, :, pl.ds(core, 1)] = value.reshape(16, 1, 16, 128)
        for k in range(16):
            r = k // 2 * 16
            b = pl.ds(pl.multiple_of((k % 2 * 2 + core) * 128, 128), 128)
            edge_second[r : r + 16, b] = part[k, 80:96, :].astype(F32)
            node_second[r : r + 16, b] = part[k, 96:112, :].astype(F32)
    rows[0:32, :] = ahead[...]
    rows[32:64, :] = behind[...]
    group = lax.broadcasted_iota(jnp.int32, (16, 128), 0) // 4
    for b in range(4):
        value = jnp.where(group == b, own[112:128, :].astype(F32), 0.0)
        rows[64:80, b * 128 : (b + 1) * 128] = value.astype(BF16)
    rows[80:128, :] = jnp.zeros((48, 512), BF16)
    match = lax.broadcasted_iota(jnp.int32, (256, 128), 0) == targets[...]
    hot = jnp.where(match, 1.0, 0.0).astype(BF16)
    node_grad[...] = node_total[...] + dot(hot, rows[...])


SMEM = pl.BlockSpec(memory_space=pltpu.SMEM)
WHOLE = pl.BlockSpec(memory_space=pltpu.VMEM)


def shape(*dims, dtype=BF16):
    return jax.ShapeDtypeStruct(dims, dtype)


def plain_call(kernel, scalars, operands, outs, scratch=(), mib=16):
    return pl.pallas_call(
        kernel,
        in_specs=[SMEM] * len(scalars) + [WHOLE] * len(operands),
        out_specs=[WHOLE] * len(outs),
        out_shape=list(outs),
        scratch_shapes=list(scratch),
        compiler_params=pltpu.CompilerParams(vmem_limit_bytes=mib * MIB),
    )(*scalars, *operands)


def same(*dims):
    once = pl.Buffered(buffer_count=1)
    return pl.BlockSpec(dims, lambda i: (0,) * len(dims), pipeline_mode=once)


def chunk(*dims):
    return pl.BlockSpec(dims, lambda i: (i,) + (0,) * (len(dims) - 1))


def limit(mib):
    return pltpu.CompilerParams(
        vmem_limit_bytes=mib * MIB, dimension_semantics=("arbitrary",)
    )


def column(*dims):
    return pl.BlockSpec(dims, lambda i: (0, i))


def like(value):
    return same(*value.shape)


def shards(
    node_lat,
    edge_lat,
    edge_src,
    edge_dst,
    edge_count,
    halo_send,
    coarse_of,
    edge_w1,
    edge_w2,
    node_w1,
    node_w2,
    grad_node,
    grad_edge,
):
    core = lax.axis_index("core")
    patch = (lax.axis_index("z") * 4 + lax.axis_index("x")) * 2 + core
    co = jnp.stack([patch, patch, core, core, edge_count[0]]).astype(jnp.int32)
    lists, owned = halo_send[0], coarse_of[0]
    unused = jnp.full((48,), -1, jnp.int32)
    targets = jnp.concatenate([lists[1], lists[0], jnp.tile(owned, 4), unused]).reshape(1, 128)

    packed, to_next, to_prev, node_half = plain_call(
        pack_kernel,
        [co],
        [node_lat, targets, edge_w1, edge_w2, node_w1, node_w2],
        [shape(64, 80, 128), shape(32, 512), shape(32, 512), shape(4, 768, 128)],
    )
    from_prev = shifted(to_next, 1)
    from_next = shifted(to_prev, -1)
    near = exchange(packed, ("z", "x", "feat")).reshape(16, 4, 80, 128)
    indices = [edge_src.reshape(16, 128), edge_dst.reshape(16, 128)]
    indices += [edge_src.reshape(STEPS, CHUNK), edge_dst.reshape(STEPS, CHUNK)]
    indices = [after(value, packed) for value in indices]
    high = TABLE + 256
    wide = chunk(CHUNK, 512)
    hot, turned, edge_turned = pl.pallas_call(
        hot_kernel,
        grid=(STEPS,),
        in_specs=[SMEM] + [like(v) for v in indices] + [wide],
        out_specs=[chunk(CHUNK, high), column(high, CHUNK), column(512, CHUNK)],
        out_shape=[shape(2048, high), shape(high, 2048), shape(512, 2048)],
        compiler_params=limit(10),
        cost_estimate=pl.CostEstimate(
            flops=20_000_000, bytes_accessed=14_000_000, transcendentals=0
        ),
    )(co, *indices, edge_lat)
    near = after(near, from_prev, from_next, hot)
    far = other_core(near)
    node_near = exchange(after(node_half, near, far), "feat")

    fixed = [node_lat, from_prev, from_next, near, far]
    wide = chunk(CHUNK, 512)
    edge_out, incoming, act, normed, slope, factor, lookup, first, second = pl.pallas_call(
        forward_kernel,
        grid=(STEPS,),
        in_specs=[SMEM]
        + [like(v) for v in fixed]
        + [wide, chunk(CHUNK, high), column(256, CHUNK)],
        out_specs=[wide, same(256, 512), wide, wide, wide, chunk(CHUNK, 128)]
        + [same(TABLE, 512), same(3, 16, 2, 16, 512), same(512, 512)],
        out_shape=[
            shape(2048, 512),
            shape(256, 512),
            shape(2048, 512),
            shape(2048, 512),
            shape(2048, 512),
            shape(2048, 128, dtype=F32),
            shape(TABLE, 512),
            shape(3, 16, 2, 16, 512),
            shape(512, 512),
        ],
        scratch_shapes=[
            pltpu.VMEM((TABLE + 256, 512), BF16),
            pltpu.VMEM((256, 512), F32),
            pltpu.VMEM((16, 2, 4, 16, 128), BF16),
        ],
        compiler_params=limit(16),
        cost_estimate=pl.CostEstimate(
            flops=7_000_000_000, bytes_accessed=18_000_000, transcendentals=1_000_000
        ),
    )(co, *fixed, edge_lat, hot, turned)

    node_near = after(node_near, incoming)
    node_far = other_core(node_near)
    fixed = [node_lat, incoming, grad_node, node_near, node_far]
    fixed += [first, second, lookup]
    moving = [edge_turned, act, normed, slope, factor, grad_edge, hot, turned]
    tiles = (8, 2, 4, 128, 128)
    node_out, node_total, edge_grad, to_prev, to_next, keep, give = pl.pallas_call(
        backward_kernel,
        grid=(STEPS,),
        in_specs=[SMEM]
        + [like(v) for v in fixed]
        + [column(512, CHUNK), wide, wide, wide, chunk(CHUNK, 128), wide, chunk(CHUNK, 256)]
        + [column(high, CHUNK)],
        out_specs=[same(256, 512), same(256, 512), wide, same(32, 512), same(32, 512)]
        + [same(*tiles), same(*tiles)],
        out_shape=[
            shape(256, 512),
            shape(256, 512, dtype=F32),
            shape(2048, 512),
            shape(32, 512),
            shape(32, 512),
            shape(*tiles),
            shape(*tiles),
        ],
        scratch_shapes=[
            pltpu.VMEM((2, 512, 512), BF16),
            pltpu.VMEM((512, 512), BF16),
            pltpu.VMEM((256, 512), BF16),
            pltpu.VMEM((512, 512), F32),
            pltpu.VMEM((512, 512), F32),
            pltpu.VMEM((TABLE + 256, 512), F32),
            pltpu.VMEM((16, 2, 16, 512), BF16),
            pltpu.VMEM((4, 512, 128), BF16),
            pltpu.VMEM((16, 2, 4, 16, 128), BF16),
        ],
        compiler_params=limit(24),
        cost_estimate=pl.CostEstimate(
            flops=9_000_000_000, bytes_accessed=24_000_000, transcendentals=100_000
        ),
    )(co, *fixed, *moving)

    pair = (keep.astype(F32) + other_core(give).astype(F32)).astype(BF16).reshape(64, 128, 128)
    ahead = shifted(after(to_prev, pair), -1)
    behind = shifted(after(to_next, pair), 1)
    own = jnp.sum(exchange(pair, ("z", "x", "feat")).astype(F32), axis=0).astype(BF16)
    own = after(own, ahead, behind)
    tiles = exchange(repeated(own[:112], 16), ("z", "x"))
    far_tiles = other_core(tiles)
    edge_first, edge_second, node_first, node_second, node_grad = plain_call(
        final_kernel,
        [co],
        [tiles, far_tiles, own, ahead, behind, targets, node_total],
        [
            shape(3, 16, 2, 16, 128, dtype=F32),
            shape(128, 512, dtype=F32),
            shape(2, 16, 2, 16, 128, dtype=F32),
            shape(128, 512, dtype=F32),
            shape(256, 512, dtype=F32),
        ],
        [pltpu.VMEM((128, 512), BF16)],
    )
    return (
        edge_out,
        node_out,
        node_grad,
        edge_grad,
        edge_first.reshape(3, 512, 128),
        edge_second,
        node_first.reshape(2, 512, 128),
        node_second,
    )


def solution(mesh):
    cube = Mesh(mesh.devices.reshape(4, 4, 2, 4), BOTH)
    rows = P(BOTH, None)
    flat = P(BOTH)
    first, second = P(None, None, "feat"), P("feat", None)
    return jax.shard_map(
        shards,
        mesh=cube,
        in_specs=(
            rows,
            rows,
            flat,
            flat,
            flat,
            P(BOTH, None, None),
            rows,
            first,
            second,
            first,
            second,
            rows,
            rows,
        ),
        out_specs=(rows, rows, rows, rows, first, second, first, second),
        check_vma=False,
    )
```

```python
import jax
import jax.numpy as jnp
from jax import lax
from jax.experimental import pallas as pl
from jax.experimental.pallas import tpu as pltpu
from jax.sharding import Mesh
from jax.sharding import PartitionSpec as P

EPSILON = 1e-05
BF16 = jnp.bfloat16
F32 = jnp.float32
BOTH = ("z", "x", "core", "feat")
CHUNK = 512
STEPS = 4
TABLE = 896
MIB = 1024 * 1024


def other_core(value):
    return lax.ppermute(value, "core", [(0, 1), (1, 0)])


def shifted(value, steps):
    return lax.ppermute(value, BOTH, [(k, (k + steps) % 128) for k in range(128)])


def exchange(value, axes):
    return lax.all_to_all(value, axes, 0, 0, tiled=True)


def after(value, *earlier):
    return lax.optimization_barrier((value, *earlier))[0]


def repeated(value, count):
    return jnp.broadcast_to(value[None], (count,) + value.shape)


def dot(left, right):
    return lax.dot_general(left, right, (((1,), (0,)), ((), ())), preferred_element_type=F32)


def dot_nt(left, right):
    return lax.dot_general(left, right, (((1,), (1,)), ((), ())), preferred_element_type=F32)


def dot_tn(left, right):
    return lax.dot_general(left, right, (((0,), (0,)), ((), ())), preferred_element_type=F32)


def mean(values):
    return jnp.mean(values, axis=-1, keepdims=True)


def normalize(values):
    centre = values - mean(values)
    factor = lax.rsqrt(mean(centre * centre) + EPSILON)
    return centre * factor, factor


def normalize_back(upstream, normed, factor):
    return factor * (upstream - mean(upstream) - normed * mean(upstream * normed))


def swish(pre):
    half = 0.5 * pre
    tanh = jnp.tanh(half)
    act = half + half * tanh
    return act, 0.5 * (1.0 + act + tanh * (1.0 - act))


def hot_tiles(rows, count):
    lanes = lax.broadcasted_iota(jnp.int32, (128, 128), 1)
    spread = jnp.transpose(jnp.broadcast_to(rows, (128, 128)))
    return [jnp.where(spread == lanes + 128 * j, 1.0, 0.0).astype(BF16) for j in range(count)]


def turned_rows(row, count):
    place = lax.broadcasted_iota(jnp.int32, (128, CHUNK), 0)
    return [jnp.where(place + 128 * j == row, 1.0, 0.0).astype(BF16) for j in range(count)]


def live_targets(step, row, count):
    lanes = lax.broadcasted_iota(jnp.int32, row.shape, 1)
    return jnp.where(lanes + step * CHUNK < count, row, -1)


def hot_kernel(co, dst, src_wide, dst_wide, edge, hot, turned, edge_turned):
    step = pl.program_id(0)
    edge_turned[...] = jnp.transpose(edge[...])
    lanes = lax.broadcasted_iota(jnp.int32, (1, 128), 1)
    for r in range(CHUNK // 128):
        row = pl.ds(step * (CHUNK // 128) + r, 1)
        live = lanes + step * CHUNK + r * 128 < co[4]
        tiles = hot_tiles(jnp.where(live, dst[row, :], -1), 2)
        hot[r * 128 : (r + 1) * 128, :] = jnp.concatenate(tiles, axis=1)
    at = pl.ds(step, 1)
    blocks = turned_rows(live_targets(step, dst_wide[at, :], co[4]), 2)
    blocks += turned_rows(src_wide[at, :], 7)
    for j, block in enumerate(blocks):
        turned[j * 128 : (j + 1) * 128, :] = block


def pack_kernel(co, node, targets, edge_first, edge_second, first, second, *outs):
    tiles, to_next, to_prev, packed = outs
    match = lax.broadcasted_iota(jnp.int32, (256, 128), 0) == targets[...]
    rows = dot_tn(jnp.where(match, 1.0, 0.0).astype(BF16), node[...])
    to_next[...] = rows[0:32].astype(BF16)
    to_prev[...] = rows[32:64].astype(BF16)
    group = lax.broadcasted_iota(jnp.int32, (16, 128), 0) // 4
    coarse = jnp.zeros((16, 128), F32)
    for b in range(4):
        coarse = jnp.where(group == b, rows[64:80, b * 128 : (b + 1) * 128], coarse)
    patch = co[0]
    at = pl.ds(pl.multiple_of(patch * 16, 16), 16)
    parts = [edge_first[m, at, :] for m in range(3)]
    row = pl.ds(pl.multiple_of(patch // 4 * 16, 16), 16)
    parts.append(edge_second[row, pl.ds(pl.multiple_of(patch % 4 * 128, 128), 128)])
    parts.append(coarse.astype(BF16))
    tile = jnp.concatenate(parts, axis=0)
    for k in range(64):
        tiles[k] = tile
    at = pl.ds(pl.multiple_of(co[2] * 256, 256), 256)
    row = pl.ds(pl.multiple_of(co[2] * 64, 64), 64)
    for m in range(2):
        packed[m * 256 : (m + 1) * 256, :] = first[m, at, :]
    for b in range(4):
        packed[512 + b * 64 : 576 + b * 64, :] = second[row, b * 128 : (b + 1) * 128]


def live_rows(step, count):
    place = lax.broadcasted_iota(jnp.int32, (CHUNK, 1), 0) + step * CHUNK
    return jnp.where(place < count, 1.0, 0.0)


HALVES = (slice(0, CHUNK // 2), slice(CHUNK // 2, CHUNK))


def place_weights(co, own_first, own_second, near, far, first, second):
    core, y = co[2], co[3]
    for s in range(4):
        yy = (y - s) & 3
        columns = pl.ds(pl.multiple_of(yy * 128, 128), 128)
        if s == 0:
            for m in range(2):
                first[m, :, columns] = own_first[m]
            second[columns, :] = own_second[...]
            continue
        for part, half in ((near[s - 1], core), (far[s - 1], 1 - core)):
            rows = pl.ds(pl.multiple_of(half * 256, 256), 256)
            for m in range(2):
                first[m, rows, columns] = part[m * 256 : (m + 1) * 256, :]
            rows = pl.ds(pl.multiple_of(yy * 128 + half * 64, 64), 64)
            for b in range(4):
                start = 512 + b * 64
                second[rows, b * 128 : (b + 1) * 128] = part[start : start + 64, :]


def whole(first, m):
    return first[m].reshape(512, 512)


def place_tiles(own_core, near, far, lookup, first, second, coarse):
    for part, core in ((near, own_core), (far, 1 - own_core)):
        for y in range(4):
            block = slice(y * 128, (y + 1) * 128)
            for m in range(3):
                value = part[:, y, m * 16 : (m + 1) * 16, :].reshape(16, 1, 16, 128)
                first[m, :, pl.ds(core, 1), :, block] = value
            for k in range(16):
                rows = slice(y * 128 + k // 2 * 16, y * 128 + k // 2 * 16 + 16)
                columns = pl.ds(pl.multiple_of((k % 2 * 2 + core) * 128, 128), 128)
                second[rows, columns] = part[k, y, 48:64, :]
            coarse[:, pl.ds(core, 1), y] = part[:, y, 64:80, :].reshape(16, 1, 16, 128)
    low = lax.broadcasted_iota(jnp.int32, (64, 8, 128), 1) < 4
    pairs = coarse[...].reshape(64, 2, 16, 128).astype(F32)
    for half in range(2):
        even, odd = pairs[:, 0, half * 8 : half * 8 + 8], pairs[:, 1, half * 8 : half * 8 + 8]
        first_block = jnp.where(low, even, pltpu.roll(odd, 4, 1)).reshape(512, 128)
        other_block = jnp.where(low, pltpu.roll(even, 4, 1), odd).reshape(512, 128)
        lookup[320:832, half * 256 : half * 256 + 128] = first_block.astype(BF16)
        lookup[320:832, half * 256 + 128 : half * 256 + 256] = other_block.astype(BF16)


def forward_kernel(co, node, prev, following, near, far, src, dst, dst_wide, edge, *refs):
    edge_out, incoming, act_out, normed_out, slope_out, factor_out, lookup, first, second = refs[:9]
    table, total, coarse = refs[9:]
    step = pl.program_id(0)

    @pl.when(step == 0)
    def _():
        lookup[0:256, :] = node[...]
        lookup[256:288, :] = prev[...]
        lookup[288:320, :] = following[...]
        lookup[832:896, :] = jnp.zeros((64, 512), BF16)
        place_tiles(co[2], near, far, lookup, first, second, coarse)
        table[0:256, :] = dot(node[...], whole(first, 2)).astype(BF16)
        table[256:, :] = dot(lookup[...], whole(first, 1)).astype(BF16)
        total[...] = jnp.zeros_like(total)

    hots = []
    for r in range(CHUNK // 128):
        row = pl.ds(step * (CHUNK // 128) + r, 1)
        tiles = hot_tiles(dst[row, :], 2) + hot_tiles(src[row, :], 7)
        hots.append(jnp.concatenate(tiles, axis=1))
    hot = jnp.concatenate(hots, axis=0)
    turned = turned_rows(live_targets(step, dst_wide[pl.ds(step, 1), :], co[4]), 2)
    turned = jnp.concatenate(turned, axis=0)
    live = live_rows(step, co[4])
    pres = [dot(edge[h, :], whole(first, 0)) + dot(hot[h, :], table[...]) for h in HALVES]
    acts = []
    for h, pre in zip(HALVES, pres):
        act, slope = swish(pre)
        acts.append(act.astype(BF16))
        act_out[h, :] = acts[-1]
        slope_out[h, :] = slope.astype(BF16)
    values = [dot(act, second[...]) for act in acts]
    for h, value in zip(HALVES, values):
        centre = value - mean(value)
        factor = lax.rsqrt(mean(centre * centre) + EPSILON) * live[h]
        normed = centre * factor
        normed_out[h, :] = normed.astype(BF16)
        factor_out[h, :] = jnp.broadcast_to(factor, (CHUNK // 2, 128))
        edge_out[h, :] = (edge[h, :].astype(F32) + normed).astype(BF16)
    total[...] += dot(turned, edge_out[...])

    @pl.when(step == STEPS - 1)
    def _():
        incoming[...] = total[...].astype(BF16)


def put_columns(co, grad, slot, scratch, keep, give):
    scratch[...] = grad.astype(BF16).reshape(16, 2, 16, 512)
    for target, core in ((keep, co[2]), (give, 1 - co[2])):
        value = scratch[:, pl.ds(core, 1), :, :].reshape(8, 2, 16, 512)
        for y in range(4):
            target[:, :, y, slot * 16 : (slot + 1) * 16, :] = value[:, :, :, y * 128 : (y + 1) * 128]


def put_rows(co, grad, slot, scratch, keep, give):
    for b in range(4):
        scratch[b] = grad[:, b * 128 : (b + 1) * 128].astype(BF16)
    for target, core in ((keep, co[2]), (give, 1 - co[2])):
        for h in range(2):
            value = scratch[2 * h + core].reshape(4, 8, 16, 128)
            for y in range(4):
                target[:, h, y, slot * 16 : (slot + 1) * 16, :] = value[y]


def put_owned(co, grad, scratch, keep, give):
    rows = grad.reshape(64, 8, 512)
    turned = pltpu.roll(rows, 4, 1)
    low = lax.broadcasted_iota(jnp.int32, (64, 8, 128), 1) < 4
    for odd in range(2):
        left, right = (turned, rows) if odd else (rows, turned)
        parts = [
            jnp.where(low, left[:, :, b : b + 128], right[:, :, b + 128 : b + 256]) for b in (0, 256)
        ]
        tile = jnp.concatenate(parts, axis=1).astype(BF16).reshape(16, 2, 2, 16, 128)
        for pair in range(2):
            scratch[:, :, pair * 2 + odd] = tile[:, :, pair]
    for target, core in ((keep, co[2]), (give, 1 - co[2])):
        value = scratch[:, pl.ds(core, 1)].reshape(8, 2, 4, 16, 128)
        target[:, :, :, 112:128, :] = value


def backward_kernel(co, node, incoming, grad_node, own_first, own_second, *refs):
    near, far, refs = refs[:3], refs[3:6], refs[6:]
    edge_first, edge_second, lookup = refs[:3]
    edge_turned, act, normed, slope, factor, grad_edge, hot, turned = refs[3:11]
    node_out, node_total, edge_grad, to_prev, to_next, keep, give = refs[11:18]
    first, second, spread, sum_second, sum_first, sums, columns, rows, owned = refs[18:]
    step = pl.program_id(0)

    @pl.when(step == 0)
    def _():
        place_weights(co, own_first, own_second, near, far, first, second)
        lat, summed = node[...], incoming[...]
        pre = dot(lat, first[0]) + dot(summed, first[1])
        node_act, node_slope = swish(pre)
        node_act = node_act.astype(BF16)
        node_normed, node_factor = normalize(dot(node_act, second[...]))
        node_out[...] = (lat.astype(F32) + node_normed).astype(BF16)
        upstream = grad_node[...].astype(F32)
        delta = normalize_back(upstream, node_normed, node_factor).astype(BF16)
        put_rows(co, dot_tn(node_act, delta), 6, rows, keep, give)
        pre_grad = (dot_nt(delta, second[...]) * node_slope).astype(BF16)
        put_columns(co, dot_tn(lat, pre_grad), 3, columns, keep, give)
        put_columns(co, dot_tn(summed, pre_grad), 4, columns, keep, give)
        node_total[...] = upstream + dot_nt(pre_grad, first[0])
        spread[...] = dot_nt(pre_grad, first[1]).astype(BF16)
        sum_second[...] = jnp.zeros_like(sum_second)
        sum_first[...] = jnp.zeros_like(sum_first)
        sums[...] = jnp.zeros_like(sums)

    totals = [grad_edge[h, :].astype(F32) + dot(hot[h, :], spread[...]) for h in HALVES]
    deltas = []
    for h, total in zip(HALVES, totals):
        delta = normalize_back(total, normed[h, :].astype(F32), factor[h, 0:1])
        deltas.append(delta.astype(BF16))
    grads = [dot_nt(delta, edge_second[...]) for delta in deltas]
    pre_grads = [(g * slope[h, :].astype(F32)).astype(BF16) for h, g in zip(HALVES, grads)]
    for h, total, pre_grad in zip(HALVES, totals, pre_grads):
        edge_grad[h, :] = (total + dot_nt(pre_grad, whole(edge_first, 0))).astype(BF16)
    pre_grad = jnp.concatenate(pre_grads, axis=0)
    sum_second[...] += dot_tn(act[...], jnp.concatenate(deltas, axis=0))
    sum_first[...] += dot(edge_turned[...], pre_grad)
    sums[...] += dot(turned[...], pre_grad)

    @pl.when(step == STEPS - 1)
    def _():
        put_rows(co, sum_second[...], 5, rows, keep, give)
        put_columns(co, sum_first[...], 0, columns, keep, give)
        received = sums[0:256, :].astype(BF16)
        sent = sums[256:, :].astype(BF16)
        put_columns(co, dot_tn(lookup[...], sent), 1, columns, keep, give)
        put_columns(co, dot_tn(node[...], received), 2, columns, keep, give)
        back = dot_nt(sent, whole(edge_first, 1))
        node_total[...] += back[0:256] + dot_nt(received, whole(edge_first, 2))
        to_prev[...] = back[256:288].astype(BF16)
        to_next[...] = back[288:320].astype(BF16)
        put_owned(co, back[320:832], owned, keep, give)


def final_kernel(co, tiles, far, own, ahead, behind, targets, node_total, *refs):
    edge_first, edge_second, node_first, node_second, node_grad, rows = refs
    for part, core in ((tiles, co[2]), (far, 1 - co[2])):
        for m in range(3):
            value = part[:, m * 16 : (m + 1) * 16, :].astype(F32)
            edge_first[m, :, pl.ds(core, 1)] = value.reshape(16, 1, 16, 128)
        for m in range(2):
            value = part[:, 48 + m * 16 : 64 + m * 16, :].astype(F32)
            node_first[m, :, pl.ds(core, 1)] = value.reshape(16, 1, 16, 128)
        for k in range(16):
            r = k // 2 * 16
            b = pl.ds(pl.multiple_of((k % 2 * 2 + core) * 128, 128), 128)
            edge_second[r : r + 16, b] = part[k, 80:96, :].astype(F32)
            node_second[r : r + 16, b] = part[k, 96:112, :].astype(F32)
    rows[0:32, :] = ahead[...]
    rows[32:64, :] = behind[...]
    group = lax.broadcasted_iota(jnp.int32, (16, 128), 0) // 4
    for b in range(4):
        value = jnp.where(group == b, own[112:128, :].astype(F32), 0.0)
        rows[64:80, b * 128 : (b + 1) * 128] = value.astype(BF16)
    rows[80:128, :] = jnp.zeros((48, 512), BF16)
    match = lax.broadcasted_iota(jnp.int32, (256, 128), 0) == targets[...]
    hot = jnp.where(match, 1.0, 0.0).astype(BF16)
    node_grad[...] = node_total[...] + dot(hot, rows[...])


SMEM = pl.BlockSpec(memory_space=pltpu.SMEM)
WHOLE = pl.BlockSpec(memory_space=pltpu.VMEM)


def shape(*dims, dtype=BF16):
    return jax.ShapeDtypeStruct(dims, dtype)


def plain_call(kernel, scalars, operands, outs, scratch=(), mib=16):
    return pl.pallas_call(
        kernel,
        in_specs=[SMEM] * len(scalars) + [WHOLE] * len(operands),
        out_specs=[WHOLE] * len(outs),
        out_shape=list(outs),
        scratch_shapes=list(scratch),
        compiler_params=pltpu.CompilerParams(vmem_limit_bytes=mib * MIB),
    )(*scalars, *operands)


def same(*dims):
    once = pl.Buffered(buffer_count=1)
    return pl.BlockSpec(dims, lambda i: (0,) * len(dims), pipeline_mode=once)


def chunk(*dims):
    return pl.BlockSpec(dims, lambda i: (i,) + (0,) * (len(dims) - 1))


def limit(mib):
    return pltpu.CompilerParams(
        vmem_limit_bytes=mib * MIB, dimension_semantics=("arbitrary",)
    )


def column(*dims):
    return pl.BlockSpec(dims, lambda i: (0, i))


def like(value):
    return same(*value.shape)


def shards(
    node_lat,
    edge_lat,
    edge_src,
    edge_dst,
    edge_count,
    halo_send,
    coarse_of,
    edge_w1,
    edge_w2,
    node_w1,
    node_w2,
    grad_node,
    grad_edge,
):
    core = lax.axis_index("core")
    patch = (lax.axis_index("z") * 4 + lax.axis_index("x")) * 2 + core
    co = jnp.stack([patch, patch, core, lax.axis_index("feat"), edge_count[0]]).astype(jnp.int32)
    lists, owned = halo_send[0], coarse_of[0]
    unused = jnp.full((48,), -1, jnp.int32)
    targets = jnp.concatenate([lists[1], lists[0], jnp.tile(owned, 4), unused]).reshape(1, 128)

    packed, to_next, to_prev, node_half = plain_call(
        pack_kernel,
        [co],
        [node_lat, targets, edge_w1, edge_w2, node_w1, node_w2],
        [shape(64, 80, 128), shape(32, 512), shape(32, 512), shape(768, 128)],
        mib=60,
    )
    from_prev = shifted(to_next, 1)
    from_next = shifted(to_prev, -1)
    near = exchange(packed, ("z", "x", "feat")).reshape(16, 4, 80, 128)
    src, dst = edge_src.reshape(16, 128), edge_dst.reshape(16, 128)
    dst_wide = edge_dst.reshape(STEPS, CHUNK)
    indices = [dst, edge_src.reshape(STEPS, CHUNK), dst_wide]
    indices = [after(value, packed) for value in indices]
    high = TABLE + 256
    wide = chunk(CHUNK, 512)
    hot, turned, edge_turned = pl.pallas_call(
        hot_kernel,
        grid=(STEPS,),
        in_specs=[SMEM] + [like(v) for v in indices] + [wide],
        out_specs=[chunk(CHUNK, 256), column(high, CHUNK), column(512, CHUNK)],
        out_shape=[shape(2048, 256), shape(high, 2048), shape(512, 2048)],
        compiler_params=limit(60),
        cost_estimate=pl.CostEstimate(
            flops=20_000_000, bytes_accessed=14_000_000, transcendentals=0
        ),
    )(co, *indices, edge_lat)
    near = after(near, from_prev, from_next, hot)
    far = other_core(near)
    node_half = after(node_half, near, far)
    node_near = [
        lax.ppermute(node_half, "feat", [(k, (k + s) % 4) for k in range(4)]) for s in (1, 2, 3)
    ]

    fixed = [node_lat, from_prev, from_next, near, far, src, dst, dst_wide]
    wide = chunk(CHUNK, 512)
    edge_out, incoming, act, normed, slope, factor, lookup, first, second = pl.pallas_call(
        forward_kernel,
        grid=(STEPS,),
        in_specs=[SMEM]
        + [like(v) for v in fixed]
        + [wide],
        out_specs=[wide, same(256, 512), wide, wide, wide, chunk(CHUNK, 128)]
        + [same(TABLE, 512), same(3, 16, 2, 16, 512), same(512, 512)],
        out_shape=[
            shape(2048, 512),
            shape(256, 512),
            shape(2048, 512),
            shape(2048, 512),
            shape(2048, 512),
            shape(2048, 128, dtype=F32),
            shape(TABLE, 512),
            shape(3, 16, 2, 16, 512),
            shape(512, 512),
        ],
        scratch_shapes=[
            pltpu.VMEM((TABLE + 256, 512), BF16),
            pltpu.VMEM((256, 512), F32),
            pltpu.VMEM((16, 2, 4, 16, 128), BF16),
        ],
        compiler_params=limit(16),
        cost_estimate=pl.CostEstimate(
            flops=7_000_000_000, bytes_accessed=18_000_000, transcendentals=1_000_000
        ),
    )(co, *fixed, edge_lat)

    node_near = [after(part, incoming) for part in node_near]
    node_far = [other_core(part) for part in node_near]
    fixed = [node_lat, incoming, grad_node, node_w1, node_w2, *node_near, *node_far]
    fixed += [first, second, lookup]
    moving = [edge_turned, act, normed, slope, factor, grad_edge, hot, turned]
    tiles = (8, 2, 4, 128, 128)
    node_out, node_total, edge_grad, to_prev, to_next, keep, give = pl.pallas_call(
        backward_kernel,
        grid=(STEPS,),
        in_specs=[SMEM]
        + [like(v) for v in fixed]
        + [column(512, CHUNK), wide, wide, wide, chunk(CHUNK, 128), wide, chunk(CHUNK, 256)]
        + [column(high, CHUNK)],
        out_specs=[same(256, 512), same(256, 512), wide, same(32, 512), same(32, 512)]
        + [same(*tiles), same(*tiles)],
        out_shape=[
            shape(256, 512),
            shape(256, 512, dtype=F32),
            shape(2048, 512),
            shape(32, 512),
            shape(32, 512),
            shape(*tiles),
            shape(*tiles),
        ],
        scratch_shapes=[
            pltpu.VMEM((2, 512, 512), BF16),
            pltpu.VMEM((512, 512), BF16),
            pltpu.VMEM((256, 512), BF16),
            pltpu.VMEM((512, 512), F32),
            pltpu.VMEM((512, 512), F32),
            pltpu.VMEM((TABLE + 256, 512), F32),
            pltpu.VMEM((16, 2, 16, 512), BF16),
            pltpu.VMEM((4, 512, 128), BF16),
            pltpu.VMEM((16, 2, 4, 16, 128), BF16),
        ],
        compiler_params=limit(24),
        cost_estimate=pl.CostEstimate(
            flops=9_000_000_000, bytes_accessed=24_000_000, transcendentals=100_000
        ),
    )(co, *fixed, *moving)

    pair = (keep.astype(F32) + other_core(give).astype(F32)).astype(BF16).reshape(64, 128, 128)
    ahead = shifted(after(to_prev, pair), -1)
    behind = shifted(after(to_next, pair), 1)
    own = jnp.sum(exchange(pair, ("z", "x", "feat")).astype(F32), axis=0).astype(BF16)
    own = after(own, ahead, behind)
    tiles = exchange(repeated(own[:112], 16), ("z", "x"))
    far_tiles = other_core(tiles)
    edge_first, edge_second, node_first, node_second, node_grad = plain_call(
        final_kernel,
        [co],
        [tiles, far_tiles, own, ahead, behind, targets, node_total],
        [
            shape(3, 16, 2, 16, 128, dtype=F32),
            shape(128, 512, dtype=F32),
            shape(2, 16, 2, 16, 128, dtype=F32),
            shape(128, 512, dtype=F32),
            shape(256, 512, dtype=F32),
        ],
        [pltpu.VMEM((128, 512), BF16)],
    )
    return (
        edge_out,
        node_out,
        node_grad,
        edge_grad,
        edge_first.reshape(3, 512, 128),
        edge_second,
        node_first.reshape(2, 512, 128),
        node_second,
    )


def solution(mesh):
    cube = Mesh(mesh.devices.reshape(4, 4, 2, 4), BOTH)
    rows = P(BOTH, None)
    flat = P(BOTH)
    first, second = P(None, None, "feat"), P("feat", None)
    return jax.shard_map(
        shards,
        mesh=cube,
        in_specs=(
            rows,
            rows,
            flat,
            flat,
            flat,
            P(BOTH, None, None),
            rows,
            first,
            second,
            first,
            second,
            rows,
            rows,
        ),
        out_specs=(rows, rows, rows, rows, first, second, first, second),
        check_vma=False,
    )
```

```python
import jax
import jax.numpy as jnp
from jax import lax
from jax.experimental import pallas as pl
from jax.experimental.pallas import tpu as pltpu
from jax.sharding import Mesh
from jax.sharding import PartitionSpec as P

EPSILON = 1e-05
BF16 = jnp.bfloat16
F32 = jnp.float32
BOTH = ("z", "x", "core", "feat")
CHUNK = 512
STEPS = 4
TABLE = 896
MIB = 1024 * 1024


def other_core(value):
    return lax.ppermute(value, "core", [(0, 1), (1, 0)])


def shifted(value, steps):
    return lax.ppermute(value, BOTH, [(k, (k + steps) % 128) for k in range(128)])


def around(value, steps):
    return lax.ppermute(value, "feat", [(k, (k + steps) % 4) for k in range(4)])


def exchange(value, axes):
    return lax.all_to_all(value, axes, 0, 0, tiled=True)


def after(value, *earlier):
    return lax.optimization_barrier((value, *earlier))[0]


def repeated(value, count):
    return jnp.broadcast_to(value[None], (count,) + value.shape)


def dot(left, right):
    return lax.dot_general(left, right, (((1,), (0,)), ((), ())), preferred_element_type=F32)


def dot_nt(left, right):
    return lax.dot_general(left, right, (((1,), (1,)), ((), ())), preferred_element_type=F32)


def dot_tn(left, right):
    return lax.dot_general(left, right, (((0,), (0,)), ((), ())), preferred_element_type=F32)


def mean(values):
    return jnp.mean(values, axis=-1, keepdims=True)


def normalize(values):
    centre = values - mean(values)
    factor = lax.rsqrt(mean(centre * centre) + EPSILON)
    return centre * factor, factor


def normalize_back(upstream, normed, factor):
    return factor * (upstream - mean(upstream) - normed * mean(upstream * normed))


def swish(pre):
    half = 0.5 * pre
    tanh = jnp.tanh(half)
    act = half + half * tanh
    return act, 0.5 * (1.0 + act + tanh * (1.0 - act))


def hot_tiles(rows, count):
    lanes = lax.broadcasted_iota(jnp.int32, (128, 128), 1)
    spread = jnp.transpose(jnp.broadcast_to(rows, (128, 128)))
    return [jnp.where(spread == lanes + 128 * j, 1.0, 0.0).astype(BF16) for j in range(count)]


def turned_rows(row, count):
    place = lax.broadcasted_iota(jnp.int32, (128, CHUNK), 0)
    return [jnp.where(place + 128 * j == row, 1.0, 0.0).astype(BF16) for j in range(count)]


def live_targets(step, row, count):
    lanes = lax.broadcasted_iota(jnp.int32, row.shape, 1)
    return jnp.where(lanes + step * CHUNK < count, row, -1)


def hot_kernel(co, dst, src_wide, dst_wide, edge, hot, turned, edge_turned):
    step = pl.program_id(0)
    edge_turned[...] = jnp.transpose(edge[...])
    lanes = lax.broadcasted_iota(jnp.int32, (1, 128), 1)
    for r in range(CHUNK // 128):
        row = pl.ds(step * (CHUNK // 128) + r, 1)
        live = lanes + step * CHUNK + r * 128 < co[4]
        tiles = hot_tiles(jnp.where(live, dst[row, :], -1), 2)
        hot[r * 128 : (r + 1) * 128, :] = jnp.concatenate(tiles, axis=1)
    at = pl.ds(step, 1)
    blocks = turned_rows(live_targets(step, dst_wide[at, :], co[4]), 2)
    blocks += turned_rows(src_wide[at, :], 7)
    for j, block in enumerate(blocks):
        turned[j * 128 : (j + 1) * 128, :] = block


def pack_half(core, first, second, packed):
    kinds = first.shape[0]
    at = pl.ds(pl.multiple_of(core * 256, 256), 256)
    row = pl.ds(pl.multiple_of(core * 64, 64), 64)
    for m in range(kinds):
        packed[m * 256 : (m + 1) * 256, :] = first[m, at, :]
    for b in range(4):
        start = kinds * 256 + b * 64
        packed[start : start + 64, :] = second[row, b * 128 : (b + 1) * 128]


def pack_kernel(co, node, targets, edge_first, edge_second, first, second, *outs):
    edge_half, node_half, coarse_out, to_next, to_prev = outs
    match = lax.broadcasted_iota(jnp.int32, (256, 128), 0) == targets[...]
    rows = dot_tn(jnp.where(match, 1.0, 0.0).astype(BF16), node[...])
    to_next[...] = rows[0:32].astype(BF16)
    to_prev[...] = rows[32:64].astype(BF16)
    group = lax.broadcasted_iota(jnp.int32, (16, 128), 0) // 4
    coarse = jnp.zeros((16, 128), F32)
    for b in range(4):
        coarse = jnp.where(group == b, rows[64:80, b * 128 : (b + 1) * 128], coarse)
    coarse_out[...] = coarse.astype(BF16)
    pack_half(co[2], edge_first, edge_second, edge_half)
    pack_half(co[2], first, second, node_half)


def live_rows(step, count):
    place = lax.broadcasted_iota(jnp.int32, (CHUNK, 1), 0) + step * CHUNK
    return jnp.where(place < count, 1.0, 0.0)


HALVES = (slice(0, CHUNK // 2), slice(CHUNK // 2, CHUNK))


def place_half(part, half, yy, first, second, start=0):
    kinds = first.shape[0]
    columns = pl.ds(pl.multiple_of(yy * 128, 128), 128)
    rows = pl.ds(pl.multiple_of(half * 256, 256), 256)
    for m in range(kinds):
        at = m * 256 - start
        if 0 <= at < part.shape[0]:
            first[m, rows, columns] = part[at : at + 256, :]
    rows = pl.ds(pl.multiple_of(yy * 128 + half * 64, 64), 64)
    for b in range(4):
        at = kinds * 256 + b * 64 - start
        if 0 <= at < part.shape[0]:
            second[rows, b * 128 : (b + 1) * 128] = part[at : at + 64, :]


def place_own(co, own_first, own_second, first, second):
    columns = pl.ds(pl.multiple_of(co[3] * 128, 128), 128)
    for m in range(first.shape[0]):
        first[m, :, columns] = own_first[m]
    second[columns, :] = own_second[...]


def place_weights(co, own_first, own_second, near, far, first, second):
    place_own(co, own_first, own_second, first, second)
    for s in (1, 2, 3):
        place_half(near[s - 1], co[2], (co[3] - s) & 3, first, second)
        place_half(far[s - 1], 1 - co[2], (co[3] - s) & 3, first, second)


def place_coarse(co, near, far, lookup, coarse):
    for part, core in ((near, co[2]), (far, 1 - co[2])):
        for s in range(4):
            value = part[:, s * 16 : (s + 1) * 16, :].reshape(16, 1, 1, 16, 128)
            coarse[:, pl.ds(core, 1), pl.ds((co[3] - s) & 3, 1)] = value
    low = lax.broadcasted_iota(jnp.int32, (64, 8, 128), 1) < 4
    pairs = coarse[...].reshape(64, 2, 16, 128).astype(F32)
    for half in range(2):
        even, odd = pairs[:, 0, half * 8 : half * 8 + 8], pairs[:, 1, half * 8 : half * 8 + 8]
        first_block = jnp.where(low, even, pltpu.roll(odd, 4, 1)).reshape(512, 128)
        other_block = jnp.where(low, pltpu.roll(even, 4, 1), odd).reshape(512, 128)
        lookup[320:832, half * 256 : half * 256 + 128] = first_block.astype(BF16)
        lookup[320:832, half * 256 + 128 : half * 256 + 256] = other_block.astype(BF16)


def forward_kernel(co, node, prev, following, own_first, own_second, *refs):
    near, far, refs = refs[:5], refs[5:10], refs[10:]
    src, dst, dst_wide, edge, refs = refs[0], refs[1], refs[2], refs[3], refs[4:]
    edge_out, incoming, act_out, normed_out, slope_out, factor_out, lookup, first, second = refs[:9]
    table, total, coarse = refs[9:]
    step = pl.program_id(0)

    @pl.when(step == 0)
    def _():
        lookup[0:256, :] = node[...]
        lookup[256:288, :] = prev[...]
        lookup[288:320, :] = following[...]
        lookup[832:896, :] = jnp.zeros((64, 512), BF16)
        place_own(co, own_first, own_second, first, second)
        for part, half in ((near, co[2]), (far, 1 - co[2])):
            place_half(part[0], half, (co[3] - 1) & 3, first, second)
            place_half(part[1], half, (co[3] + 1) & 3, first, second)
            place_half(part[2], half, (co[3] + 2) & 3, first, second)
            place_half(part[3], half, (co[3] + 2) & 3, first, second, 512)
        place_coarse(co, near[4], far[4], lookup, coarse)
        table[0:256, :] = dot(node[...], first[2]).astype(BF16)
        table[256:, :] = dot(lookup[...], first[1]).astype(BF16)
        total[...] = jnp.zeros_like(total)

    hots = []
    for r in range(CHUNK // 128):
        row = pl.ds(step * (CHUNK // 128) + r, 1)
        tiles = hot_tiles(dst[row, :], 2) + hot_tiles(src[row, :], 7)
        hots.append(jnp.concatenate(tiles, axis=1))
    hot = jnp.concatenate(hots, axis=0)
    turned = turned_rows(live_targets(step, dst_wide[pl.ds(step, 1), :], co[4]), 2)
    turned = jnp.concatenate(turned, axis=0)
    live = live_rows(step, co[4])
    pres = [dot(edge[h, :], first[0]) + dot(hot[h, :], table[...]) for h in HALVES]
    acts = []
    for h, pre in zip(HALVES, pres):
        act, slope = swish(pre)
        acts.append(act.astype(BF16))
        act_out[h, :] = acts[-1]
        slope_out[h, :] = slope.astype(BF16)
    values = [dot(act, second[...]) for act in acts]
    for h, value in zip(HALVES, values):
        centre = value - mean(value)
        factor = lax.rsqrt(mean(centre * centre) + EPSILON) * live[h]
        normed = centre * factor
        normed_out[h, :] = normed.astype(BF16)
        factor_out[h, :] = jnp.broadcast_to(factor, (CHUNK // 2, 128))
        edge_out[h, :] = (edge[h, :].astype(F32) + normed).astype(BF16)
    total[...] += dot(turned, edge_out[...])

    @pl.when(step == STEPS - 1)
    def _():
        incoming[...] = total[...].astype(BF16)


def put_columns(co, grad, slot, scratch, keep, give):
    scratch[...] = grad.astype(BF16).reshape(16, 2, 16, 512)
    for target, core in ((keep, co[2]), (give, 1 - co[2])):
        value = scratch[:, pl.ds(core, 1), :, :].reshape(8, 2, 16, 512)
        for y in range(4):
            target[:, :, y, slot * 16 : (slot + 1) * 16, :] = value[:, :, :, y * 128 : (y + 1) * 128]


def put_rows(co, grad, slot, scratch, keep, give):
    for b in range(4):
        scratch[b] = grad[:, b * 128 : (b + 1) * 128].astype(BF16)
    for target, core in ((keep, co[2]), (give, 1 - co[2])):
        for h in range(2):
            value = scratch[2 * h + core].reshape(4, 8, 16, 128)
            for y in range(4):
                target[:, h, y, slot * 16 : (slot + 1) * 16, :] = value[y]


def put_owned(co, grad, scratch, keep, give):
    rows = grad.reshape(64, 8, 512)
    turned = pltpu.roll(rows, 4, 1)
    low = lax.broadcasted_iota(jnp.int32, (64, 8, 128), 1) < 4
    for odd in range(2):
        left, right = (turned, rows) if odd else (rows, turned)
        parts = [
            jnp.where(low, left[:, :, b : b + 128], right[:, :, b + 128 : b + 256]) for b in (0, 256)
        ]
        tile = jnp.concatenate(parts, axis=1).astype(BF16).reshape(16, 2, 2, 16, 128)
        for pair in range(2):
            scratch[:, :, pair * 2 + odd] = tile[:, :, pair]
    for target, core in ((keep, co[2]), (give, 1 - co[2])):
        value = scratch[:, pl.ds(core, 1)].reshape(8, 2, 4, 16, 128)
        target[:, :, :, 112:128, :] = value


def backward_kernel(co, node, incoming, grad_node, own_first, own_second, *refs):
    near, far, refs = refs[:3], refs[3:6], refs[6:]
    edge_first, edge_second, lookup = refs[:3]
    edge_turned, act, normed, slope, factor, grad_edge, hot, turned = refs[3:11]
    node_out, node_total, edge_grad, to_prev, to_next, keep, give = refs[11:18]
    first, second, spread, sum_second, sum_first, sums, columns, rows, owned = refs[18:]
    step = pl.program_id(0)

    @pl.when(step == 0)
    def _():
        place_weights(co, own_first, own_second, near, far, first, second)
        lat, summed = node[...], incoming[...]
        pre = dot(lat, first[0]) + dot(summed, first[1])
        node_act, node_slope = swish(pre)
        node_act = node_act.astype(BF16)
        node_normed, node_factor = normalize(dot(node_act, second[...]))
        node_out[...] = (lat.astype(F32) + node_normed).astype(BF16)
        upstream = grad_node[...].astype(F32)
        delta = normalize_back(upstream, node_normed, node_factor).astype(BF16)
        put_rows(co, dot_tn(node_act, delta), 6, rows, keep, give)
        pre_grad = (dot_nt(delta, second[...]) * node_slope).astype(BF16)
        put_columns(co, dot_tn(lat, pre_grad), 3, columns, keep, give)
        put_columns(co, dot_tn(summed, pre_grad), 4, columns, keep, give)
        node_total[...] = upstream + dot_nt(pre_grad, first[0])
        spread[...] = dot_nt(pre_grad, first[1]).astype(BF16)
        sum_second[...] = jnp.zeros_like(sum_second)
        sum_first[...] = jnp.zeros_like(sum_first)
        sums[...] = jnp.zeros_like(sums)

    totals = [grad_edge[h, :].astype(F32) + dot(hot[h, :], spread[...]) for h in HALVES]
    deltas = []
    for h, total in zip(HALVES, totals):
        delta = normalize_back(total, normed[h, :].astype(F32), factor[h, 0:1])
        deltas.append(delta.astype(BF16))
    grads = [dot_nt(delta, edge_second[...]) for delta in deltas]
    pre_grads = [(g * slope[h, :].astype(F32)).astype(BF16) for h, g in zip(HALVES, grads)]
    for h, total, pre_grad in zip(HALVES, totals, pre_grads):
        edge_grad[h, :] = (total + dot_nt(pre_grad, edge_first[0])).astype(BF16)
    pre_grad = jnp.concatenate(pre_grads, axis=0)
    sum_second[...] += dot_tn(act[...], jnp.concatenate(deltas, axis=0))
    sum_first[...] += dot(edge_turned[...], pre_grad)
    sums[...] += dot(turned[...], pre_grad)

    @pl.when(step == STEPS - 1)
    def _():
        put_rows(co, sum_second[...], 5, rows, keep, give)
        put_columns(co, sum_first[...], 0, columns, keep, give)
        received = sums[0:256, :].astype(BF16)
        sent = sums[256:, :].astype(BF16)
        put_columns(co, dot_tn(lookup[...], sent), 1, columns, keep, give)
        put_columns(co, dot_tn(node[...], received), 2, columns, keep, give)
        back = dot_nt(sent, edge_first[1])
        node_total[...] += back[0:256] + dot_nt(received, edge_first[2])
        to_prev[...] = back[256:288].astype(BF16)
        to_next[...] = back[288:320].astype(BF16)
        put_owned(co, back[320:832], owned, keep, give)


def final_kernel(co, tiles, far, own, ahead, behind, targets, node_total, *refs):
    edge_first, edge_second, node_first, node_second, node_grad, rows = refs
    for part, core in ((tiles, co[2]), (far, 1 - co[2])):
        for m in range(3):
            value = part[:, m * 16 : (m + 1) * 16, :].astype(F32)
            edge_first[m, :, pl.ds(core, 1)] = value.reshape(16, 1, 16, 128)
        for m in range(2):
            value = part[:, 48 + m * 16 : 64 + m * 16, :].astype(F32)
            node_first[m, :, pl.ds(core, 1)] = value.reshape(16, 1, 16, 128)
        for k in range(16):
            r = k // 2 * 16
            b = pl.ds(pl.multiple_of((k % 2 * 2 + core) * 128, 128), 128)
            edge_second[r : r + 16, b] = part[k, 80:96, :].astype(F32)
            node_second[r : r + 16, b] = part[k, 96:112, :].astype(F32)
    rows[0:32, :] = ahead[...]
    rows[32:64, :] = behind[...]
    group = lax.broadcasted_iota(jnp.int32, (16, 128), 0) // 4
    for b in range(4):
        value = jnp.where(group == b, own[112:128, :].astype(F32), 0.0)
        rows[64:80, b * 128 : (b + 1) * 128] = value.astype(BF16)
    rows[80:128, :] = jnp.zeros((48, 512), BF16)
    match = lax.broadcasted_iota(jnp.int32, (256, 128), 0) == targets[...]
    hot = jnp.where(match, 1.0, 0.0).astype(BF16)
    node_grad[...] = node_total[...] + dot(hot, rows[...])


SMEM = pl.BlockSpec(memory_space=pltpu.SMEM)
WHOLE = pl.BlockSpec(memory_space=pltpu.VMEM)


def shape(*dims, dtype=BF16):
    return jax.ShapeDtypeStruct(dims, dtype)


def plain_call(kernel, scalars, operands, outs, scratch=(), mib=16):
    return pl.pallas_call(
        kernel,
        in_specs=[SMEM] * len(scalars) + [WHOLE] * len(operands),
        out_specs=[WHOLE] * len(outs),
        out_shape=list(outs),
        scratch_shapes=list(scratch),
        compiler_params=pltpu.CompilerParams(vmem_limit_bytes=mib * MIB),
    )(*scalars, *operands)


def same(*dims):
    once = pl.Buffered(buffer_count=1)
    return pl.BlockSpec(dims, lambda i: (0,) * len(dims), pipeline_mode=once)


def chunk(*dims):
    return pl.BlockSpec(dims, lambda i: (i,) + (0,) * (len(dims) - 1))


def limit(mib):
    return pltpu.CompilerParams(
        vmem_limit_bytes=mib * MIB, dimension_semantics=("arbitrary",)
    )


def column(*dims):
    return pl.BlockSpec(dims, lambda i: (0, i))


def like(value):
    return same(*value.shape)


def shards(
    node_lat,
    edge_lat,
    edge_src,
    edge_dst,
    edge_count,
    halo_send,
    coarse_of,
    edge_w1,
    edge_w2,
    node_w1,
    node_w2,
    grad_node,
    grad_edge,
):
    core = lax.axis_index("core")
    patch = (lax.axis_index("z") * 4 + lax.axis_index("x")) * 2 + core
    co = jnp.stack([patch, patch, core, lax.axis_index("feat"), edge_count[0]]).astype(jnp.int32)
    lists, owned = halo_send[0], coarse_of[0]
    unused = jnp.full((48,), -1, jnp.int32)
    targets = jnp.concatenate([lists[1], lists[0], jnp.tile(owned, 4), unused]).reshape(1, 128)

    edge_half, node_half, coarse_own, to_next, to_prev = plain_call(
        pack_kernel,
        [co],
        [node_lat, targets, edge_w1, edge_w2, node_w1, node_w2],
        [shape(1024, 128), shape(768, 128), shape(16, 128), shape(32, 512), shape(32, 512)],
        mib=60,
    )
    coarse_four = [coarse_own] + [around(coarse_own, s) for s in (1, 2, 3)]
    from_prev = shifted(to_next, 1)
    from_next = shifted(to_prev, -1)
    up, down = around(edge_half, 1), around(edge_half, 3)
    coarse_four = jnp.concatenate(coarse_four, axis=0)
    coarse_near = exchange(repeated(coarse_four, 16), ("z", "x"))
    half_down, half_up = around(down[:512], 3), around(up[512:], 1)
    near = [up, down, half_down, half_up, coarse_near]
    src, dst = edge_src.reshape(16, 128), edge_dst.reshape(16, 128)
    dst_wide = edge_dst.reshape(STEPS, CHUNK)
    indices = [dst, edge_src.reshape(STEPS, CHUNK), dst_wide]
    indices = [after(value, edge_half) for value in indices]
    high = TABLE + 256
    wide = chunk(CHUNK, 512)
    hot, turned, edge_turned = pl.pallas_call(
        hot_kernel,
        grid=(STEPS,),
        in_specs=[SMEM] + [like(v) for v in indices] + [wide],
        out_specs=[chunk(CHUNK, 256), column(high, CHUNK), column(512, CHUNK)],
        out_shape=[shape(2048, 256), shape(high, 2048), shape(512, 2048)],
        compiler_params=limit(60),
        cost_estimate=pl.CostEstimate(
            flops=20_000_000, bytes_accessed=14_000_000, transcendentals=0
        ),
    )(co, *indices, edge_lat)
    far = [other_core(part) for part in near]
    node_half = after(node_half, hot, from_prev, from_next, *far)
    node_near = [around(node_half, s) for s in (1, 2, 3)]

    fixed = [node_lat, from_prev, from_next, edge_w1, edge_w2, *near, *far, src, dst, dst_wide]
    wide = chunk(CHUNK, 512)
    edge_out, incoming, act, normed, slope, factor, lookup, first, second = pl.pallas_call(
        forward_kernel,
        grid=(STEPS,),
        in_specs=[SMEM]
        + [like(v) for v in fixed]
        + [wide],
        out_specs=[wide, same(256, 512), wide, wide, wide, chunk(CHUNK, 128)]
        + [same(TABLE, 512), same(3, 512, 512), same(512, 512)],
        out_shape=[
            shape(2048, 512),
            shape(256, 512),
            shape(2048, 512),
            shape(2048, 512),
            shape(2048, 512),
            shape(2048, 128, dtype=F32),
            shape(TABLE, 512),
            shape(3, 512, 512),
            shape(512, 512),
        ],
        scratch_shapes=[
            pltpu.VMEM((TABLE + 256, 512), BF16),
            pltpu.VMEM((256, 512), F32),
            pltpu.VMEM((16, 2, 4, 16, 128), BF16),
        ],
        compiler_params=limit(16),
        cost_estimate=pl.CostEstimate(
            flops=7_000_000_000, bytes_accessed=18_000_000, transcendentals=1_000_000
        ),
    )(co, *fixed, edge_lat)

    node_near = [after(part, incoming) for part in node_near]
    node_far = [other_core(part) for part in node_near]
    fixed = [node_lat, incoming, grad_node, node_w1, node_w2, *node_near, *node_far]
    fixed += [first, second, lookup]
    moving = [edge_turned, act, normed, slope, factor, grad_edge, hot, turned]
    tiles = (8, 2, 4, 128, 128)
    node_out, node_total, edge_grad, to_prev, to_next, keep, give = pl.pallas_call(
        backward_kernel,
        grid=(STEPS,),
        in_specs=[SMEM]
        + [like(v) for v in fixed]
        + [column(512, CHUNK), wide, wide, wide, chunk(CHUNK, 128), wide, chunk(CHUNK, 256)]
        + [column(high, CHUNK)],
        out_specs=[same(256, 512), same(256, 512), wide, same(32, 512), same(32, 512)]
        + [same(*tiles), same(*tiles)],
        out_shape=[
            shape(256, 512),
            shape(256, 512, dtype=F32),
            shape(2048, 512),
            shape(32, 512),
            shape(32, 512),
            shape(*tiles),
            shape(*tiles),
        ],
        scratch_shapes=[
            pltpu.VMEM((2, 512, 512), BF16),
            pltpu.VMEM((512, 512), BF16),
            pltpu.VMEM((256, 512), BF16),
            pltpu.VMEM((512, 512), F32),
            pltpu.VMEM((512, 512), F32),
            pltpu.VMEM((TABLE + 256, 512), F32),
            pltpu.VMEM((16, 2, 16, 512), BF16),
            pltpu.VMEM((4, 512, 128), BF16),
            pltpu.VMEM((16, 2, 4, 16, 128), BF16),
        ],
        compiler_params=limit(24),
        cost_estimate=pl.CostEstimate(
            flops=9_000_000_000, bytes_accessed=24_000_000, transcendentals=100_000
        ),
    )(co, *fixed, *moving)

    pair = (keep.astype(F32) + other_core(give).astype(F32)).astype(BF16).reshape(64, 128, 128)
    ahead = shifted(after(to_prev, pair), -1)
    behind = shifted(after(to_next, pair), 1)
    own = jnp.sum(exchange(pair, ("z", "x", "feat")).astype(F32), axis=0).astype(BF16)
    own = after(own, ahead, behind)
    tiles = exchange(repeated(own[:112], 16), ("z", "x"))
    far_tiles = other_core(tiles)
    edge_first, edge_second, node_first, node_second, node_grad = plain_call(
        final_kernel,
        [co],
        [tiles, far_tiles, own, ahead, behind, targets, node_total],
        [
            shape(3, 16, 2, 16, 128, dtype=F32),
            shape(128, 512, dtype=F32),
            shape(2, 16, 2, 16, 128, dtype=F32),
            shape(128, 512, dtype=F32),
            shape(256, 512, dtype=F32),
        ],
        [pltpu.VMEM((128, 512), BF16)],
    )
    return (
        edge_out,
        node_out,
        node_grad,
        edge_grad,
        edge_first.reshape(3, 512, 128),
        edge_second,
        node_first.reshape(2, 512, 128),
        node_second,
    )


def solution(mesh):
    cube = Mesh(mesh.devices.reshape(4, 4, 2, 4), BOTH)
    rows = P(BOTH, None)
    flat = P(BOTH)
    first, second = P(None, None, "feat"), P("feat", None)
    return jax.shard_map(
        shards,
        mesh=cube,
        in_specs=(
            rows,
            rows,
            flat,
            flat,
            flat,
            P(BOTH, None, None),
            rows,
            first,
            second,
            first,
            second,
            rows,
            rows,
        ),
        out_specs=(rows, rows, rows, rows, first, second, first, second),
        check_vma=False,
    )
```

```python
import jax
import jax.numpy as jnp
from jax import lax
from jax.experimental import pallas as pl
from jax.experimental.pallas import tpu as pltpu
from jax.sharding import Mesh
from jax.sharding import PartitionSpec as P

EPSILON = 1e-05
BF16 = jnp.bfloat16
F32 = jnp.float32
BOTH = ("z", "x", "core", "feat")
CHUNK = 512
STEPS = 4
TABLE = 896
MIB = 1024 * 1024


def places(count):
    core = lax.axis_index("core")
    patch = (lax.axis_index("z") * 4 + lax.axis_index("x")) * 2 + core
    return patch, patch, core, lax.axis_index("feat"), count[0]


def other_core(value):
    return lax.ppermute(value, "core", [(0, 1), (1, 0)])


def shifted(value, steps):
    return lax.ppermute(value, BOTH, [(k, (k + steps) % 128) for k in range(128)])


def exchange(value, axes):
    return lax.all_to_all(value, axes, 0, 0, tiled=True)


def after(value, *earlier):
    return lax.optimization_barrier((value, *earlier))[0]


def repeated(value, count):
    return jnp.broadcast_to(value[None], (count,) + value.shape)


def dot(left, right):
    return lax.dot_general(left, right, (((1,), (0,)), ((), ())), preferred_element_type=F32)


def dot_nt(left, right):
    return lax.dot_general(left, right, (((1,), (1,)), ((), ())), preferred_element_type=F32)


def dot_tn(left, right):
    return lax.dot_general(left, right, (((0,), (0,)), ((), ())), preferred_element_type=F32)


def mean(values):
    return jnp.mean(values, axis=-1, keepdims=True)


def normalize(values):
    centre = values - mean(values)
    factor = lax.rsqrt(mean(centre * centre) + EPSILON)
    return centre * factor, factor


def normalize_back(upstream, normed, factor):
    return factor * (upstream - mean(upstream) - normed * mean(upstream * normed))


def swish(pre):
    half = 0.5 * pre
    tanh = jnp.tanh(half)
    act = half + half * tanh
    return act, 0.5 * (1.0 + act + tanh * (1.0 - act))


def hot_tiles(rows, count):
    lanes = lax.broadcasted_iota(jnp.int32, (128, 128), 1)
    spread = jnp.transpose(jnp.broadcast_to(rows, (128, 128)))
    return [jnp.where(spread == lanes + 128 * j, 1.0, 0.0).astype(BF16) for j in range(count)]


def turned_rows(row, count):
    place = lax.broadcasted_iota(jnp.int32, (128, CHUNK), 0)
    return [jnp.where(place + 128 * j == row, 1.0, 0.0).astype(BF16) for j in range(count)]


def live_targets(step, row, count):
    lanes = lax.broadcasted_iota(jnp.int32, row.shape, 1)
    return jnp.where(lanes + step * CHUNK < count, row, -1)


def hot_kernel(count, dst, src_wide, dst_wide, edge, hot, turned, edge_turned):
    co = places(count)
    step = pl.program_id(0)
    edge_turned[...] = jnp.transpose(edge[...])
    lanes = lax.broadcasted_iota(jnp.int32, (1, 128), 1)
    for r in range(CHUNK // 128):
        row = pl.ds(step * (CHUNK // 128) + r, 1)
        live = lanes + step * CHUNK + r * 128 < co[4]
        tiles = hot_tiles(jnp.where(live, dst[row, :], -1), 2)
        hot[r * 128 : (r + 1) * 128, :] = jnp.concatenate(tiles, axis=1)
    at = pl.ds(step, 1)
    blocks = turned_rows(live_targets(step, dst_wide[at, :], co[4]), 2)
    blocks += turned_rows(src_wide[at, :], 7)
    for j, block in enumerate(blocks):
        turned[j * 128 : (j + 1) * 128, :] = block


def halo_match(lists):
    place = lax.broadcasted_iota(jnp.int32, (256, 32), 0)
    return [jnp.where(place == lists[k : k + 1, :], 1.0, 0.0).astype(BF16) for k in range(2)]


def coarse_match(owned):
    place = lax.broadcasted_iota(jnp.int32, (256, 16), 0)
    slot = lax.broadcasted_iota(jnp.int32, (256, 16), 1) % 4
    hot = jnp.zeros((256, 16), F32)
    for j in range(4):
        hot = jnp.where((place == owned[0, j]) & (slot == j), 1.0, hot)
    return hot.astype(BF16)


def pack_kernel(count, owned, node, lists, edge_first, edge_second, first, second, *outs):
    tiles, to_next, to_prev, packed = outs
    co = places(count)
    halo_hot, coarse_hot = halo_match(lists), coarse_match(owned)
    to_prev[...] = dot_tn(halo_hot[0], node[...]).astype(BF16)
    to_next[...] = dot_tn(halo_hot[1], node[...]).astype(BF16)
    rows = dot_tn(coarse_hot, node[...])
    group = lax.broadcasted_iota(jnp.int32, (16, 128), 0) // 4
    coarse = jnp.zeros((16, 128), F32)
    for b in range(4):
        coarse = jnp.where(group == b, rows[:, b * 128 : (b + 1) * 128], coarse)
    patch = co[0]
    at = pl.ds(pl.multiple_of(patch * 16, 16), 16)
    parts = [edge_first[m, at, :] for m in range(3)]
    row = pl.ds(pl.multiple_of(patch // 4 * 16, 16), 16)
    parts.append(edge_second[row, pl.ds(pl.multiple_of(patch % 4 * 128, 128), 128)])
    parts.append(coarse.astype(BF16))
    tile = jnp.concatenate(parts, axis=0)
    for k in range(64):
        tiles[k] = tile
    at = pl.ds(pl.multiple_of(co[2] * 256, 256), 256)
    row = pl.ds(pl.multiple_of(co[2] * 64, 64), 64)
    for m in range(2):
        packed[m * 256 : (m + 1) * 256, :] = first[m, at, :]
    for b in range(4):
        packed[512 + b * 64 : 576 + b * 64, :] = second[row, b * 128 : (b + 1) * 128]


def live_rows(step, count):
    place = lax.broadcasted_iota(jnp.int32, (CHUNK, 1), 0) + step * CHUNK
    return jnp.where(place < count, 1.0, 0.0)


HALVES = (slice(0, CHUNK),)


def place_weights(co, own_first, own_second, near, far, first, second):
    core, y = co[2], co[3]
    for s in range(4):
        yy = (y - s) & 3
        columns = pl.ds(pl.multiple_of(yy * 128, 128), 128)
        if s == 0:
            for m in range(2):
                first[m, :, columns] = own_first[m]
            second[columns, :] = own_second[...]
            continue
        for part, half in ((near[s - 1], core), (far[s - 1], 1 - core)):
            rows = pl.ds(pl.multiple_of(half * 256, 256), 256)
            for m in range(2):
                first[m, rows, columns] = part[m * 256 : (m + 1) * 256, :]
            rows = pl.ds(pl.multiple_of(yy * 128 + half * 64, 64), 64)
            for b in range(4):
                start = 512 + b * 64
                second[rows, b * 128 : (b + 1) * 128] = part[start : start + 64, :]


def whole(first, m):
    return first[m].reshape(512, 512)


def place_tiles(own_core, near, far, lookup, first, second, coarse):
    for part, core in ((near, own_core), (far, 1 - own_core)):
        for y in range(4):
            block = slice(y * 128, (y + 1) * 128)
            for m in range(3):
                value = part[:, y, m * 16 : (m + 1) * 16, :].reshape(16, 1, 16, 128)
                first[m, :, pl.ds(core, 1), :, block] = value
            for k in range(16):
                rows = slice(y * 128 + k // 2 * 16, y * 128 + k // 2 * 16 + 16)
                columns = pl.ds(pl.multiple_of((k % 2 * 2 + core) * 128, 128), 128)
                second[rows, columns] = part[k, y, 48:64, :]
            coarse[:, pl.ds(core, 1), y] = part[:, y, 64:80, :].reshape(16, 1, 16, 128)
    low = lax.broadcasted_iota(jnp.int32, (64, 8, 128), 1) < 4
    pairs = coarse[...].reshape(64, 2, 16, 128).astype(F32)
    for half in range(2):
        even, odd = pairs[:, 0, half * 8 : half * 8 + 8], pairs[:, 1, half * 8 : half * 8 + 8]
        first_block = jnp.where(low, even, pltpu.roll(odd, 4, 1)).reshape(512, 128)
        other_block = jnp.where(low, pltpu.roll(even, 4, 1), odd).reshape(512, 128)
        lookup[320:832, half * 256 : half * 256 + 128] = first_block.astype(BF16)
        lookup[320:832, half * 256 + 128 : half * 256 + 256] = other_block.astype(BF16)


def forward_kernel(count, node, prev, following, near, far, src, dst, dst_wide, edge, *refs):
    edge_out, incoming, act_out, normed_out, slope_out, factor_out, lookup, first, second = refs[:9]
    table, total, coarse = refs[9:]
    co = places(count)
    step = pl.program_id(0)

    @pl.when(step == 0)
    def _():
        lookup[0:256, :] = node[...]
        lookup[256:288, :] = prev[...]
        lookup[288:320, :] = following[...]
        lookup[832:896, :] = jnp.zeros((64, 512), BF16)
        place_tiles(co[2], near, far, lookup, first, second, coarse)
        table[0:256, :] = dot(node[...], whole(first, 2)).astype(BF16)
        table[256:, :] = dot(lookup[...], whole(first, 1)).astype(BF16)
        total[...] = jnp.zeros_like(total)

    hots = []
    for r in range(CHUNK // 128):
        row = pl.ds(step * (CHUNK // 128) + r, 1)
        tiles = hot_tiles(dst[row, :], 2) + hot_tiles(src[row, :], 7)
        hots.append(jnp.concatenate(tiles, axis=1))
    hot = jnp.concatenate(hots, axis=0)
    turned = turned_rows(live_targets(step, dst_wide[pl.ds(step, 1), :], co[4]), 2)
    turned = jnp.concatenate(turned, axis=0)
    live = live_rows(step, co[4])
    pres = [dot(edge[h, :], whole(first, 0)) + dot(hot[h, :], table[...]) for h in HALVES]
    acts = []
    for h, pre in zip(HALVES, pres):
        act, slope = swish(pre)
        acts.append(act.astype(BF16))
        act_out[h, :] = acts[-1]
        slope_out[h, :] = slope.astype(BF16)
    values = [dot(act, second[...]) for act in acts]
    for h, value in zip(HALVES, values):
        centre = value - mean(value)
        factor = lax.rsqrt(mean(centre * centre) + EPSILON) * live[h]
        normed = centre * factor
        normed_out[h, :] = normed.astype(BF16)
        factor_out[h, :] = jnp.broadcast_to(factor, (CHUNK, 128))
        edge_out[h, :] = (edge[h, :].astype(F32) + normed).astype(BF16)
    total[...] += dot(turned, edge_out[...])

    @pl.when(step == STEPS - 1)
    def _():
        incoming[...] = total[...].astype(BF16)


def put_columns(co, grad, slot, scratch, keep, give):
    scratch[...] = grad.astype(BF16).reshape(16, 2, 16, 512)
    for target, core in ((keep, co[2]), (give, 1 - co[2])):
        value = scratch[:, pl.ds(core, 1), :, :].reshape(8, 2, 16, 512)
        for y in range(4):
            target[:, :, y, slot * 16 : (slot + 1) * 16, :] = value[:, :, :, y * 128 : (y + 1) * 128]


def put_rows(co, grad, slot, scratch, keep, give):
    for b in range(4):
        scratch[b] = grad[:, b * 128 : (b + 1) * 128].astype(BF16)
    for target, core in ((keep, co[2]), (give, 1 - co[2])):
        for h in range(2):
            value = scratch[2 * h + core].reshape(4, 8, 16, 128)
            for y in range(4):
                target[:, h, y, slot * 16 : (slot + 1) * 16, :] = value[y]


def put_owned(co, grad, scratch, keep, give):
    rows = grad.reshape(64, 8, 512)
    turned = pltpu.roll(rows, 4, 1)
    low = lax.broadcasted_iota(jnp.int32, (64, 8, 128), 1) < 4
    for odd in range(2):
        left, right = (turned, rows) if odd else (rows, turned)
        parts = [
            jnp.where(low, left[:, :, b : b + 128], right[:, :, b + 128 : b + 256]) for b in (0, 256)
        ]
        tile = jnp.concatenate(parts, axis=1).astype(BF16).reshape(16, 2, 2, 16, 128)
        for pair in range(2):
            scratch[:, :, pair * 2 + odd] = tile[:, :, pair]
    for target, core in ((keep, co[2]), (give, 1 - co[2])):
        value = scratch[:, pl.ds(core, 1)].reshape(8, 2, 4, 16, 128)
        target[:, :, :, 112:128, :] = value


def backward_kernel(count, node, incoming, grad_node, own_first, own_second, *refs):
    near, far, refs = refs[:3], refs[3:6], refs[6:]
    co = places(count)
    edge_first, edge_second, lookup = refs[:3]
    edge_turned, act, normed, slope, factor, grad_edge, hot, turned = refs[3:11]
    node_out, node_total, edge_grad, to_prev, to_next, keep, give = refs[11:18]
    first, second, spread, sum_second, sum_first, sums, columns, rows, owned = refs[18:]
    step = pl.program_id(0)

    @pl.when(step == 0)
    def _():
        place_weights(co, own_first, own_second, near, far, first, second)
        lat, summed = node[...], incoming[...]
        pre = dot(lat, first[0]) + dot(summed, first[1])
        node_act, node_slope = swish(pre)
        node_act = node_act.astype(BF16)
        node_normed, node_factor = normalize(dot(node_act, second[...]))
        node_out[...] = (lat.astype(F32) + node_normed).astype(BF16)
        upstream = grad_node[...].astype(F32)
        delta = normalize_back(upstream, node_normed, node_factor).astype(BF16)
        put_rows(co, dot_tn(node_act, delta), 6, rows, keep, give)
        pre_grad = (dot_nt(delta, second[...]) * node_slope).astype(BF16)
        put_columns(co, dot_tn(lat, pre_grad), 3, columns, keep, give)
        put_columns(co, dot_tn(summed, pre_grad), 4, columns, keep, give)
        node_total[...] = upstream + dot_nt(pre_grad, first[0])
        spread[...] = dot_nt(pre_grad, first[1]).astype(BF16)
        sum_second[...] = jnp.zeros_like(sum_second)
        sum_first[...] = jnp.zeros_like(sum_first)
        sums[...] = jnp.zeros_like(sums)

    totals = [grad_edge[h, :].astype(F32) + dot(hot[h, :], spread[...]) for h in HALVES]
    deltas = []
    for h, total in zip(HALVES, totals):
        delta = normalize_back(total, normed[h, :].astype(F32), factor[h, 0:1])
        deltas.append(delta.astype(BF16))
    grads = [dot_nt(delta, edge_second[...]) for delta in deltas]
    pre_grads = [(g * slope[h, :].astype(F32)).astype(BF16) for h, g in zip(HALVES, grads)]
    for h, total, pre_grad in zip(HALVES, totals, pre_grads):
        edge_grad[h, :] = (total + dot_nt(pre_grad, whole(edge_first, 0))).astype(BF16)
    pre_grad = jnp.concatenate(pre_grads, axis=0)
    sum_second[...] += dot_tn(act[...], jnp.concatenate(deltas, axis=0))
    sum_first[...] += dot(edge_turned[...], pre_grad)
    sums[...] += dot(turned[...], pre_grad)

    @pl.when(step == STEPS - 1)
    def _():
        put_rows(co, sum_second[...], 5, rows, keep, give)
        put_columns(co, sum_first[...], 0, columns, keep, give)
        received = sums[0:256, :].astype(BF16)
        sent = sums[256:, :].astype(BF16)
        put_columns(co, dot_tn(lookup[...], sent), 1, columns, keep, give)
        put_columns(co, dot_tn(node[...], received), 2, columns, keep, give)
        back = dot_nt(sent, whole(edge_first, 1))
        node_total[...] += back[0:256] + dot_nt(received, whole(edge_first, 2))
        to_prev[...] = back[256:288].astype(BF16)
        to_next[...] = back[288:320].astype(BF16)
        put_owned(co, back[320:832], owned, keep, give)


def final_kernel(count, owned, tiles, far, own, ahead, behind, lists, node_total, *refs):
    edge_first, edge_second, node_first, node_second, node_grad = refs
    co = places(count)
    for part, core in ((tiles, co[2]), (far, 1 - co[2])):
        for m in range(3):
            value = part[:, m * 16 : (m + 1) * 16, :].astype(F32)
            edge_first[m, :, pl.ds(core, 1)] = value.reshape(16, 1, 16, 128)
        for m in range(2):
            value = part[:, 48 + m * 16 : 64 + m * 16, :].astype(F32)
            node_first[m, :, pl.ds(core, 1)] = value.reshape(16, 1, 16, 128)
        for k in range(16):
            r = k // 2 * 16
            b = pl.ds(pl.multiple_of((k % 2 * 2 + core) * 128, 128), 128)
            edge_second[r : r + 16, b] = part[k, 80:96, :].astype(F32)
            node_second[r : r + 16, b] = part[k, 96:112, :].astype(F32)
    halo_hot, coarse_hot = halo_match(lists), coarse_match(owned)
    group = lax.broadcasted_iota(jnp.int32, (16, 128), 0) // 4
    rows = own[112:128, :].astype(F32)
    blocks = [jnp.where(group == b, rows, 0.0).astype(BF16) for b in range(4)]
    node_grad[...] = (
        node_total[...]
        + dot(halo_hot[1], ahead[...])
        + dot(halo_hot[0], behind[...])
        + dot(coarse_hot, jnp.concatenate(blocks, axis=1))
    )


SMEM = pl.BlockSpec(memory_space=pltpu.SMEM)
WHOLE = pl.BlockSpec(memory_space=pltpu.VMEM)


def shape(*dims, dtype=BF16):
    return jax.ShapeDtypeStruct(dims, dtype)


def plain_call(kernel, scalars, operands, outs, scratch=(), mib=16):
    return pl.pallas_call(
        kernel,
        in_specs=[SMEM] * len(scalars) + [WHOLE] * len(operands),
        out_specs=[WHOLE] * len(outs),
        out_shape=list(outs),
        scratch_shapes=list(scratch),
        compiler_params=pltpu.CompilerParams(vmem_limit_bytes=mib * MIB),
    )(*scalars, *operands)


def same(*dims):
    once = pl.Buffered(buffer_count=1)
    return pl.BlockSpec(dims, lambda i: (0,) * len(dims), pipeline_mode=once)


def chunk(*dims):
    return pl.BlockSpec(dims, lambda i: (i,) + (0,) * (len(dims) - 1))


def limit(mib):
    return pltpu.CompilerParams(
        vmem_limit_bytes=mib * MIB, dimension_semantics=("arbitrary",)
    )


def column(*dims):
    return pl.BlockSpec(dims, lambda i: (0, i))


def like(value):
    return same(*value.shape)


def shards(
    node_lat,
    edge_lat,
    edge_src,
    edge_dst,
    edge_count,
    halo_send,
    coarse_of,
    edge_w1,
    edge_w2,
    node_w1,
    node_w2,
    grad_node,
    grad_edge,
):
    lists = halo_send.reshape(2, 32)
    packed, to_next, to_prev, node_half = plain_call(
        pack_kernel,
        [edge_count, coarse_of],
        [node_lat, lists, edge_w1, edge_w2, node_w1, node_w2],
        [shape(64, 80, 128), shape(32, 512), shape(32, 512), shape(768, 128)],
        mib=60,
    )
    from_prev = shifted(to_next, 1)
    from_next = shifted(to_prev, -1)
    near = exchange(packed, ("z", "x", "feat")).reshape(16, 4, 80, 128)
    src, dst = edge_src.reshape(16, 128), edge_dst.reshape(16, 128)
    dst_wide = edge_dst.reshape(STEPS, CHUNK)
    indices = [dst, edge_src.reshape(STEPS, CHUNK), dst_wide]
    indices = [after(value, packed) for value in indices]
    high = TABLE + 256
    wide = chunk(CHUNK, 512)
    hot, turned, edge_turned = pl.pallas_call(
        hot_kernel,
        grid=(STEPS,),
        in_specs=[SMEM] + [like(v) for v in indices] + [wide],
        out_specs=[chunk(CHUNK, 256), column(high, CHUNK), column(512, CHUNK)],
        out_shape=[shape(2048, 256), shape(high, 2048), shape(512, 2048)],
        compiler_params=limit(60),
        cost_estimate=pl.CostEstimate(
            flops=20_000_000, bytes_accessed=14_000_000, transcendentals=0
        ),
    )(edge_count, *indices, edge_lat)
    near = after(near, from_prev, from_next, hot)
    far = other_core(near)
    node_half = after(node_half, near)
    node_near = [
        lax.ppermute(node_half, "feat", [(k, (k + s) % 4) for k in range(4)]) for s in (1, 2, 3)
    ]

    fixed = [node_lat, from_prev, from_next, near, far, src, dst, dst_wide]
    wide = chunk(CHUNK, 512)
    edge_out, incoming, act, normed, slope, factor, lookup, first, second = pl.pallas_call(
        forward_kernel,
        grid=(STEPS,),
        in_specs=[SMEM]
        + [like(v) for v in fixed]
        + [wide],
        out_specs=[wide, same(256, 512), wide, wide, wide, chunk(CHUNK, 128)]
        + [same(TABLE, 512), same(3, 16, 2, 16, 512), same(512, 512)],
        out_shape=[
            shape(2048, 512),
            shape(256, 512),
            shape(2048, 512),
            shape(2048, 512),
            shape(2048, 512),
            shape(2048, 128, dtype=F32),
            shape(TABLE, 512),
            shape(3, 16, 2, 16, 512),
            shape(512, 512),
        ],
        scratch_shapes=[
            pltpu.VMEM((TABLE + 256, 512), BF16),
            pltpu.VMEM((256, 512), F32),
            pltpu.VMEM((16, 2, 4, 16, 128), BF16),
        ],
        compiler_params=limit(16),
        cost_estimate=pl.CostEstimate(
            flops=7_000_000_000, bytes_accessed=18_000_000, transcendentals=1_000_000
        ),
    )(edge_count, *fixed, edge_lat)

    node_near = [after(part, incoming) for part in node_near]
    node_far = [other_core(part) for part in node_near]
    fixed = [node_lat, incoming, grad_node, node_w1, node_w2, *node_near, *node_far]
    fixed += [first, second, lookup]
    moving = [edge_turned, act, normed, slope, factor, grad_edge, hot, turned]
    tiles = (8, 2, 4, 128, 128)
    node_out, node_total, edge_grad, to_prev, to_next, keep, give = pl.pallas_call(
        backward_kernel,
        grid=(STEPS,),
        in_specs=[SMEM]
        + [like(v) for v in fixed]
        + [column(512, CHUNK), wide, wide, wide, chunk(CHUNK, 128), wide, chunk(CHUNK, 256)]
        + [column(high, CHUNK)],
        out_specs=[same(256, 512), same(256, 512), wide, same(32, 512), same(32, 512)]
        + [same(*tiles), same(*tiles)],
        out_shape=[
            shape(256, 512),
            shape(256, 512, dtype=F32),
            shape(2048, 512),
            shape(32, 512),
            shape(32, 512),
            shape(*tiles),
            shape(*tiles),
        ],
        scratch_shapes=[
            pltpu.VMEM((2, 512, 512), BF16),
            pltpu.VMEM((512, 512), BF16),
            pltpu.VMEM((256, 512), BF16),
            pltpu.VMEM((512, 512), F32),
            pltpu.VMEM((512, 512), F32),
            pltpu.VMEM((TABLE + 256, 512), F32),
            pltpu.VMEM((16, 2, 16, 512), BF16),
            pltpu.VMEM((4, 512, 128), BF16),
            pltpu.VMEM((16, 2, 4, 16, 128), BF16),
        ],
        compiler_params=limit(24),
        cost_estimate=pl.CostEstimate(
            flops=9_000_000_000, bytes_accessed=24_000_000, transcendentals=100_000
        ),
    )(edge_count, *fixed, *moving)

    pair = (keep.astype(F32) + other_core(give).astype(F32)).astype(BF16).reshape(64, 128, 128)
    ahead = shifted(after(to_prev, pair), -1)
    behind = shifted(after(to_next, pair), 1)
    own = jnp.sum(exchange(pair, ("z", "x", "feat")).astype(F32), axis=0).astype(BF16)
    own = after(own, ahead, behind)
    tiles = exchange(repeated(own[:112], 16), ("z", "x"))
    far_tiles = other_core(tiles)
    edge_first, edge_second, node_first, node_second, node_grad = plain_call(
        final_kernel,
        [edge_count, coarse_of],
        [tiles, far_tiles, own, ahead, behind, lists, node_total],
        [
            shape(3, 16, 2, 16, 128, dtype=F32),
            shape(128, 512, dtype=F32),
            shape(2, 16, 2, 16, 128, dtype=F32),
            shape(128, 512, dtype=F32),
            shape(256, 512, dtype=F32),
        ],
    )
    return (
        edge_out,
        node_out,
        node_grad,
        edge_grad,
        edge_first.reshape(3, 512, 128),
        edge_second,
        node_first.reshape(2, 512, 128),
        node_second,
    )


def solution(mesh):
    cube = Mesh(mesh.devices.reshape(4, 4, 2, 4), BOTH)
    rows = P(BOTH, None)
    flat = P(BOTH)
    first, second = P(None, None, "feat"), P("feat", None)
    return jax.shard_map(
        shards,
        mesh=cube,
        in_specs=(
            rows,
            rows,
            flat,
            flat,
            flat,
            P(BOTH, None, None),
            rows,
            first,
            second,
            first,
            second,
            rows,
            rows,
        ),
        out_specs=(rows, rows, rows, rows, first, second, first, second),
        check_vma=False,
    )
```

```python
import jax
import jax.numpy as jnp
from jax import lax
from jax.experimental import pallas as pl
from jax.experimental.pallas import tpu as pltpu
from jax.sharding import Mesh
from jax.sharding import PartitionSpec as P

EPSILON = 1e-05
BF16 = jnp.bfloat16
F32 = jnp.float32
BOTH = ("z", "x", "core", "feat")
CHUNK = 512
STEPS = 4
TABLE = 896
MIB = 1024 * 1024


def places(count):
    core = lax.axis_index("core")
    patch = (lax.axis_index("z") * 4 + lax.axis_index("x")) * 2 + core
    return patch, patch, core, lax.axis_index("feat"), count[0]


def other_core(value):
    return lax.ppermute(value, "core", [(0, 1), (1, 0)])


def shifted(value, steps):
    return lax.ppermute(value, BOTH, [(k, (k + steps) % 128) for k in range(128)])


def exchange(value, axes):
    return lax.all_to_all(value, axes, 0, 0, tiled=True)


def after(value, *earlier):
    return lax.optimization_barrier((value, *earlier))[0]


def repeated(value, count):
    return jnp.broadcast_to(value[None], (count,) + value.shape)


def dot(left, right):
    return lax.dot_general(left, right, (((1,), (0,)), ((), ())), preferred_element_type=F32)


def dot_nt(left, right):
    return lax.dot_general(left, right, (((1,), (1,)), ((), ())), preferred_element_type=F32)


def dot_tn(left, right):
    return lax.dot_general(left, right, (((0,), (0,)), ((), ())), preferred_element_type=F32)


def mean(values):
    return jnp.mean(values, axis=-1, keepdims=True)


def normalize(values):
    centre = values - mean(values)
    factor = lax.rsqrt(mean(centre * centre) + EPSILON)
    return centre * factor, factor


def normalize_back(upstream, normed, factor):
    return factor * (upstream - mean(upstream) - normed * mean(upstream * normed))


def swish(pre):
    half = 0.5 * pre
    tanh = jnp.tanh(half)
    act = half + half * tanh
    return act, 0.5 * (1.0 + act + tanh * (1.0 - act))


def hot_tiles(rows, count):
    lanes = lax.broadcasted_iota(jnp.int32, (128, 128), 1)
    spread = jnp.transpose(jnp.broadcast_to(rows, (128, 128)))
    return [jnp.where(spread == lanes + 128 * j, 1.0, 0.0).astype(BF16) for j in range(count)]


def turned_rows(row, count):
    place = lax.broadcasted_iota(jnp.int32, (128, CHUNK), 0)
    return [jnp.where(place + 128 * j == row, 1.0, 0.0).astype(BF16) for j in range(count)]


def live_targets(step, row, count):
    lanes = lax.broadcasted_iota(jnp.int32, row.shape, 1)
    return jnp.where(lanes + step * CHUNK < count, row, -1)


def hot_kernel(count, dst, src_wide, dst_wide, edge, hot, turned, edge_turned):
    co = places(count)
    step = pl.program_id(0)
    edge_turned[...] = jnp.transpose(edge[...])
    lanes = lax.broadcasted_iota(jnp.int32, (1, 128), 1)
    for r in range(CHUNK // 128):
        row = pl.ds(step * (CHUNK // 128) + r, 1)
        live = lanes + step * CHUNK + r * 128 < co[4]
        tiles = hot_tiles(jnp.where(live, dst[row, :], -1), 2)
        hot[r * 128 : (r + 1) * 128, :] = jnp.concatenate(tiles, axis=1)
    at = pl.ds(step, 1)
    blocks = turned_rows(live_targets(step, dst_wide[at, :], co[4]), 2)
    blocks += turned_rows(src_wide[at, :], 7)
    for j, block in enumerate(blocks):
        turned[j * 128 : (j + 1) * 128, :] = block


def halo_match(lists):
    place = lax.broadcasted_iota(jnp.int32, (256, 32), 0)
    return [jnp.where(place == lists[k : k + 1, :], 1.0, 0.0).astype(BF16) for k in range(2)]


def coarse_match(owned):
    place = lax.broadcasted_iota(jnp.int32, (256, 16), 0)
    slot = lax.broadcasted_iota(jnp.int32, (256, 16), 1) % 4
    hot = jnp.zeros((256, 16), F32)
    for j in range(4):
        hot = jnp.where((place == owned[0, j]) & (slot == j), 1.0, hot)
    return hot.astype(BF16)


def pack_kernel(count, owned, node, lists, edge_first, edge_second, first, second, *outs):
    tiles, to_next, to_prev, packed = outs
    co = places(count)
    halo_hot, coarse_hot = halo_match(lists), coarse_match(owned)
    to_prev[...] = dot_tn(halo_hot[0], node[...]).astype(BF16)
    to_next[...] = dot_tn(halo_hot[1], node[...]).astype(BF16)
    rows = dot_tn(coarse_hot, node[...])
    group = lax.broadcasted_iota(jnp.int32, (16, 128), 0) // 4
    coarse = jnp.zeros((16, 128), F32)
    for b in range(4):
        coarse = jnp.where(group == b, rows[:, b * 128 : (b + 1) * 128], coarse)
    patch = co[0]
    at = pl.ds(pl.multiple_of(patch * 16, 16), 16)
    parts = [edge_first[m, at, :] for m in range(3)]
    row = pl.ds(pl.multiple_of(patch // 4 * 16, 16), 16)
    parts.append(edge_second[row, pl.ds(pl.multiple_of(patch % 4 * 128, 128), 128)])
    parts.append(coarse.astype(BF16))
    tile = jnp.concatenate(parts, axis=0)
    for k in range(64):
        tiles[k] = tile
    at = pl.ds(pl.multiple_of(co[2] * 256, 256), 256)
    row = pl.ds(pl.multiple_of(co[2] * 64, 64), 64)
    for m in range(2):
        packed[m * 256 : (m + 1) * 256, :] = first[m, at, :]
    for b in range(4):
        packed[512 + b * 64 : 576 + b * 64, :] = second[row, b * 128 : (b + 1) * 128]


def live_rows(step, start, count):
    place = lax.broadcasted_iota(jnp.int32, (STRIP, 1), 0) + (step * CHUNK + start)
    return jnp.where(place < count, 1.0, 0.0)


STRIP = 64
STRIPS = [slice(r, r + STRIP) for r in range(0, CHUNK, STRIP)]


def place_weights(co, own_first, own_second, near, far, first, second):
    core, y = co[2], co[3]
    for s in range(4):
        yy = (y - s) & 3
        columns = pl.ds(pl.multiple_of(yy * 128, 128), 128)
        if s == 0:
            for m in range(2):
                first[m, :, columns] = own_first[m]
            second[columns, :] = own_second[...]
            continue
        for part, half in ((near[s - 1], core), (far[s - 1], 1 - core)):
            rows = pl.ds(pl.multiple_of(half * 256, 256), 256)
            for m in range(2):
                first[m, rows, columns] = part[m * 256 : (m + 1) * 256, :]
            rows = pl.ds(pl.multiple_of(yy * 128 + half * 64, 64), 64)
            for b in range(4):
                start = 512 + b * 64
                second[rows, b * 128 : (b + 1) * 128] = part[start : start + 64, :]


def whole(first, m):
    return first[m].reshape(512, 512)


def place_tiles(own_core, near, far, lookup, first, second, coarse):
    for part, core in ((near, own_core), (far, 1 - own_core)):
        for y in range(4):
            block = slice(y * 128, (y + 1) * 128)
            for m in range(3):
                value = part[:, y, m * 16 : (m + 1) * 16, :].reshape(16, 1, 16, 128)
                first[m, :, pl.ds(core, 1), :, block] = value
            for k in range(16):
                rows = slice(y * 128 + k // 2 * 16, y * 128 + k // 2 * 16 + 16)
                columns = pl.ds(pl.multiple_of((k % 2 * 2 + core) * 128, 128), 128)
                second[rows, columns] = part[k, y, 48:64, :]
            coarse[:, pl.ds(core, 1), y] = part[:, y, 64:80, :].reshape(16, 1, 16, 128)
    low = lax.broadcasted_iota(jnp.int32, (64, 8, 128), 1) < 4
    pairs = coarse[...].reshape(64, 2, 16, 128).astype(F32)
    for half in range(2):
        even, odd = pairs[:, 0, half * 8 : half * 8 + 8], pairs[:, 1, half * 8 : half * 8 + 8]
        first_block = jnp.where(low, even, pltpu.roll(odd, 4, 1)).reshape(512, 128)
        other_block = jnp.where(low, pltpu.roll(even, 4, 1), odd).reshape(512, 128)
        lookup[320:832, half * 256 : half * 256 + 128] = first_block.astype(BF16)
        lookup[320:832, half * 256 + 128 : half * 256 + 256] = other_block.astype(BF16)


def forward_kernel(count, node, prev, following, near, far, src, dst, dst_wide, edge, *refs):
    edge_out, incoming, act_out, normed_out, slope_out, factor_out, lookup, first, second = refs[:9]
    table, total, coarse, hot, turned, held = refs[9:]
    co = places(count)
    step = pl.program_id(0)

    @pl.when(step == 0)
    def _():
        lookup[0:256, :] = node[...]
        lookup[256:288, :] = prev[...]
        lookup[288:320, :] = following[...]
        lookup[832:896, :] = jnp.zeros((64, 512), BF16)
        place_tiles(co[2], near, far, lookup, first, second, coarse)
        table[0:256, :] = dot(node[...], whole(first, 2)).astype(BF16)
        table[256:, :] = dot(lookup[...], whole(first, 1)).astype(BF16)
        total[...] = jnp.zeros_like(total)

    for r in range(CHUNK // 128):
        row = pl.ds(step * (CHUNK // 128) + r, 1)
        tiles = hot_tiles(dst[row, :], 2) + hot_tiles(src[row, :], 7)
        for j, tile in enumerate(tiles):
            hot[r * 128 : (r + 1) * 128, j * 128 : (j + 1) * 128] = tile
    blocks = turned_rows(live_targets(step, dst_wide[pl.ds(step, 1), :], co[4]), 2)
    for j, block in enumerate(blocks):
        turned[j * 128 : (j + 1) * 128, :] = block
    held[...] = dot(edge[...], whole(first, 0)) + dot(hot[...], table[...])
    for h in STRIPS:
        act, slope = swish(held[h, :])
        act_out[h, :] = act.astype(BF16)
        slope_out[h, :] = slope.astype(BF16)
    held[...] = dot(act_out[...], second[...])
    for h in STRIPS:
        value = held[h, :]
        centre = value - mean(value)
        live = live_rows(step, h.start, co[4])
        factor = lax.rsqrt(mean(centre * centre) + EPSILON) * live
        normed = centre * factor
        normed_out[h, :] = normed.astype(BF16)
        factor_out[h, :] = jnp.broadcast_to(factor, (STRIP, 128))
        edge_out[h, :] = (edge[h, :].astype(F32) + normed).astype(BF16)
    total[...] += dot(turned[...], edge_out[...])

    @pl.when(step == STEPS - 1)
    def _():
        incoming[...] = total[...].astype(BF16)


def put_columns(co, grad, slot, scratch, keep, give):
    scratch[...] = grad.astype(BF16).reshape(16, 2, 16, 512)
    for target, core in ((keep, co[2]), (give, 1 - co[2])):
        value = scratch[:, pl.ds(core, 1), :, :].reshape(8, 2, 16, 512)
        for y in range(4):
            target[:, :, y, slot * 16 : (slot + 1) * 16, :] = value[:, :, :, y * 128 : (y + 1) * 128]


def put_rows(co, grad, slot, scratch, keep, give):
    for b in range(4):
        scratch[b] = grad[:, b * 128 : (b + 1) * 128].astype(BF16)
    for target, core in ((keep, co[2]), (give, 1 - co[2])):
        for h in range(2):
            value = scratch[2 * h + core].reshape(4, 8, 16, 128)
            for y in range(4):
                target[:, h, y, slot * 16 : (slot + 1) * 16, :] = value[y]


def put_owned(co, grad, scratch, keep, give):
    rows = grad.reshape(64, 8, 512)
    turned = pltpu.roll(rows, 4, 1)
    low = lax.broadcasted_iota(jnp.int32, (64, 8, 128), 1) < 4
    for odd in range(2):
        left, right = (turned, rows) if odd else (rows, turned)
        parts = [
            jnp.where(low, left[:, :, b : b + 128], right[:, :, b + 128 : b + 256]) for b in (0, 256)
        ]
        tile = jnp.concatenate(parts, axis=1).astype(BF16).reshape(16, 2, 2, 16, 128)
        for pair in range(2):
            scratch[:, :, pair * 2 + odd] = tile[:, :, pair]
    for target, core in ((keep, co[2]), (give, 1 - co[2])):
        value = scratch[:, pl.ds(core, 1)].reshape(8, 2, 4, 16, 128)
        target[:, :, :, 112:128, :] = value


def backward_kernel(count, node, incoming, grad_node, own_first, own_second, *refs):
    near, far, refs = refs[:3], refs[3:6], refs[6:]
    co = places(count)
    edge_first, edge_second, lookup = refs[:3]
    edge_turned, act, normed, slope, factor, grad_edge, hot, turned = refs[3:11]
    node_out, node_total, edge_grad, to_prev, to_next, keep, give = refs[11:18]
    first, second, spread, sum_second, sum_first, sums, columns, rows, owned = refs[18:27]
    held, back, deltas, pre_grads = refs[27:]
    step = pl.program_id(0)

    @pl.when(step == 0)
    def _():
        place_weights(co, own_first, own_second, near, far, first, second)
        lat, summed = node[...], incoming[...]
        pre = dot(lat, first[0]) + dot(summed, first[1])
        node_act, node_slope = swish(pre)
        node_act = node_act.astype(BF16)
        node_normed, node_factor = normalize(dot(node_act, second[...]))
        node_out[...] = (lat.astype(F32) + node_normed).astype(BF16)
        upstream = grad_node[...].astype(F32)
        delta = normalize_back(upstream, node_normed, node_factor).astype(BF16)
        put_rows(co, dot_tn(node_act, delta), 6, rows, keep, give)
        pre_grad = (dot_nt(delta, second[...]) * node_slope).astype(BF16)
        put_columns(co, dot_tn(lat, pre_grad), 3, columns, keep, give)
        put_columns(co, dot_tn(summed, pre_grad), 4, columns, keep, give)
        node_total[...] = upstream + dot_nt(pre_grad, first[0])
        spread[...] = dot_nt(pre_grad, first[1]).astype(BF16)
        sum_second[...] = jnp.zeros_like(sum_second)
        sum_first[...] = jnp.zeros_like(sum_first)
        sums[...] = jnp.zeros_like(sums)

    held[...] = dot(hot[...], spread[...])
    for h in STRIPS:
        total = grad_edge[h, :].astype(F32) + held[h, :]
        held[h, :] = total
        delta = normalize_back(total, normed[h, :].astype(F32), factor[h, 0:1])
        deltas[h, :] = delta.astype(BF16)
    back[...] = dot_nt(deltas[...], edge_second[...])
    for h in STRIPS:
        pre_grads[h, :] = (back[h, :] * slope[h, :].astype(F32)).astype(BF16)
    back[...] = dot_nt(pre_grads[...], whole(edge_first, 0))
    for h in STRIPS:
        edge_grad[h, :] = (held[h, :] + back[h, :]).astype(BF16)
    sum_second[...] += dot_tn(act[...], deltas[...])
    sum_first[...] += dot(edge_turned[...], pre_grads[...])
    sums[...] += dot(turned[...], pre_grads[...])

    @pl.when(step == STEPS - 1)
    def _():
        put_rows(co, sum_second[...], 5, rows, keep, give)
        put_columns(co, sum_first[...], 0, columns, keep, give)
        received = sums[0:256, :].astype(BF16)
        sent = sums[256:, :].astype(BF16)
        put_columns(co, dot_tn(lookup[...], sent), 1, columns, keep, give)
        put_columns(co, dot_tn(node[...], received), 2, columns, keep, give)
        remote = dot_nt(sent, whole(edge_first, 1))
        node_total[...] += remote[0:256] + dot_nt(received, whole(edge_first, 2))
        to_prev[...] = remote[256:288].astype(BF16)
        to_next[...] = remote[288:320].astype(BF16)
        put_owned(co, remote[320:832], owned, keep, give)


def final_kernel(count, owned, tiles, far, own, ahead, behind, lists, node_total, *refs):
    edge_first, edge_second, node_first, node_second, node_grad = refs
    co = places(count)
    for part, core in ((tiles, co[2]), (far, 1 - co[2])):
        for m in range(3):
            value = part[:, m * 16 : (m + 1) * 16, :].astype(F32)
            edge_first[m, :, pl.ds(core, 1)] = value.reshape(16, 1, 16, 128)
        for m in range(2):
            value = part[:, 48 + m * 16 : 64 + m * 16, :].astype(F32)
            node_first[m, :, pl.ds(core, 1)] = value.reshape(16, 1, 16, 128)
        for k in range(16):
            r = k // 2 * 16
            b = pl.ds(pl.multiple_of((k % 2 * 2 + core) * 128, 128), 128)
            edge_second[r : r + 16, b] = part[k, 80:96, :].astype(F32)
            node_second[r : r + 16, b] = part[k, 96:112, :].astype(F32)
    halo_hot, coarse_hot = halo_match(lists), coarse_match(owned)
    group = lax.broadcasted_iota(jnp.int32, (16, 128), 0) // 4
    rows = own[112:128, :].astype(F32)
    blocks = [jnp.where(group == b, rows, 0.0).astype(BF16) for b in range(4)]
    node_grad[...] = (
        node_total[...]
        + dot(halo_hot[1], ahead[...])
        + dot(halo_hot[0], behind[...])
        + dot(coarse_hot, jnp.concatenate(blocks, axis=1))
    )


SMEM = pl.BlockSpec(memory_space=pltpu.SMEM)
WHOLE = pl.BlockSpec(memory_space=pltpu.VMEM)


def shape(*dims, dtype=BF16):
    return jax.ShapeDtypeStruct(dims, dtype)


def plain_call(kernel, scalars, operands, outs, scratch=(), mib=16):
    return pl.pallas_call(
        kernel,
        in_specs=[SMEM] * len(scalars) + [WHOLE] * len(operands),
        out_specs=[WHOLE] * len(outs),
        out_shape=list(outs),
        scratch_shapes=list(scratch),
        compiler_params=pltpu.CompilerParams(vmem_limit_bytes=mib * MIB),
    )(*scalars, *operands)


def same(*dims):
    once = pl.Buffered(buffer_count=1)
    return pl.BlockSpec(dims, lambda i: (0,) * len(dims), pipeline_mode=once)


def chunk(*dims):
    return pl.BlockSpec(dims, lambda i: (i,) + (0,) * (len(dims) - 1))


def limit(mib):
    return pltpu.CompilerParams(
        vmem_limit_bytes=mib * MIB, dimension_semantics=("arbitrary",)
    )


def column(*dims):
    return pl.BlockSpec(dims, lambda i: (0, i))


def like(value):
    return same(*value.shape)


def shards(
    node_lat,
    edge_lat,
    edge_src,
    edge_dst,
    edge_count,
    halo_send,
    coarse_of,
    edge_w1,
    edge_w2,
    node_w1,
    node_w2,
    grad_node,
    grad_edge,
):
    lists = halo_send.reshape(2, 32)
    packed, to_next, to_prev, node_half = plain_call(
        pack_kernel,
        [edge_count, coarse_of],
        [node_lat, lists, edge_w1, edge_w2, node_w1, node_w2],
        [shape(64, 80, 128), shape(32, 512), shape(32, 512), shape(768, 128)],
        mib=60,
    )
    from_prev = shifted(to_next, 1)
    from_next = shifted(to_prev, -1)
    near = exchange(packed, ("z", "x", "feat")).reshape(16, 4, 80, 128)
    src, dst = edge_src.reshape(16, 128), edge_dst.reshape(16, 128)
    dst_wide = edge_dst.reshape(STEPS, CHUNK)
    indices = [dst, edge_src.reshape(STEPS, CHUNK), dst_wide]
    indices = [after(value, packed) for value in indices]
    high = TABLE + 256
    wide = chunk(CHUNK, 512)
    hot, turned, edge_turned = pl.pallas_call(
        hot_kernel,
        grid=(STEPS,),
        in_specs=[SMEM] + [like(v) for v in indices] + [wide],
        out_specs=[chunk(CHUNK, 256), column(high, CHUNK), column(512, CHUNK)],
        out_shape=[shape(2048, 256), shape(high, 2048), shape(512, 2048)],
        compiler_params=limit(60),
        cost_estimate=pl.CostEstimate(
            flops=20_000_000, bytes_accessed=14_000_000, transcendentals=0
        ),
    )(edge_count, *indices, edge_lat)
    near = after(near, from_prev, from_next, hot)
    far = other_core(near)
    node_half = after(node_half, near)
    node_near = [
        lax.ppermute(node_half, "feat", [(k, (k + s) % 4) for k in range(4)]) for s in (1, 2, 3)
    ]

    fixed = [node_lat, from_prev, from_next, near, far, src, dst, dst_wide]
    wide = chunk(CHUNK, 512)
    edge_out, incoming, act, normed, slope, factor, lookup, first, second = pl.pallas_call(
        forward_kernel,
        grid=(STEPS,),
        in_specs=[SMEM]
        + [like(v) for v in fixed]
        + [wide],
        out_specs=[wide, same(256, 512), wide, wide, wide, chunk(CHUNK, 128)]
        + [same(TABLE, 512), same(3, 16, 2, 16, 512), same(512, 512)],
        out_shape=[
            shape(2048, 512),
            shape(256, 512),
            shape(2048, 512),
            shape(2048, 512),
            shape(2048, 512),
            shape(2048, 128, dtype=F32),
            shape(TABLE, 512),
            shape(3, 16, 2, 16, 512),
            shape(512, 512),
        ],
        scratch_shapes=[
            pltpu.VMEM((TABLE + 256, 512), BF16),
            pltpu.VMEM((256, 512), F32),
            pltpu.VMEM((16, 2, 4, 16, 128), BF16),
            pltpu.VMEM((CHUNK, high), BF16),
            pltpu.VMEM((256, CHUNK), BF16),
            pltpu.VMEM((CHUNK, 512), F32),
        ],
        compiler_params=limit(16),
        cost_estimate=pl.CostEstimate(
            flops=7_000_000_000, bytes_accessed=18_000_000, transcendentals=1_000_000
        ),
    )(edge_count, *fixed, edge_lat)

    node_near = [after(part, incoming) for part in node_near]
    node_far = [other_core(part) for part in node_near]
    fixed = [node_lat, incoming, grad_node, node_w1, node_w2, *node_near, *node_far]
    fixed += [first, second, lookup]
    moving = [edge_turned, act, normed, slope, factor, grad_edge, hot, turned]
    tiles = (8, 2, 4, 128, 128)
    node_out, node_total, edge_grad, to_prev, to_next, keep, give = pl.pallas_call(
        backward_kernel,
        grid=(STEPS,),
        in_specs=[SMEM]
        + [like(v) for v in fixed]
        + [column(512, CHUNK), wide, wide, wide, chunk(CHUNK, 128), wide, chunk(CHUNK, 256)]
        + [column(high, CHUNK)],
        out_specs=[same(256, 512), same(256, 512), wide, same(32, 512), same(32, 512)]
        + [same(*tiles), same(*tiles)],
        out_shape=[
            shape(256, 512),
            shape(256, 512, dtype=F32),
            shape(2048, 512),
            shape(32, 512),
            shape(32, 512),
            shape(*tiles),
            shape(*tiles),
        ],
        scratch_shapes=[
            pltpu.VMEM((2, 512, 512), BF16),
            pltpu.VMEM((512, 512), BF16),
            pltpu.VMEM((256, 512), BF16),
            pltpu.VMEM((512, 512), F32),
            pltpu.VMEM((512, 512), F32),
            pltpu.VMEM((TABLE + 256, 512), F32),
            pltpu.VMEM((16, 2, 16, 512), BF16),
            pltpu.VMEM((4, 512, 128), BF16),
            pltpu.VMEM((16, 2, 4, 16, 128), BF16),
            pltpu.VMEM((CHUNK, 512), F32),
            pltpu.VMEM((CHUNK, 512), F32),
            pltpu.VMEM((CHUNK, 512), BF16),
            pltpu.VMEM((CHUNK, 512), BF16),
        ],
        compiler_params=limit(24),
        cost_estimate=pl.CostEstimate(
            flops=9_000_000_000, bytes_accessed=24_000_000, transcendentals=100_000
        ),
    )(edge_count, *fixed, *moving)

    pair = (keep.astype(F32) + other_core(give).astype(F32)).astype(BF16).reshape(64, 128, 128)
    ahead = shifted(after(to_prev, pair), -1)
    behind = shifted(after(to_next, pair), 1)
    own = jnp.sum(exchange(pair, ("z", "x", "feat")).astype(F32), axis=0).astype(BF16)
    own = after(own, ahead, behind)
    tiles = exchange(repeated(own[:112], 16), ("z", "x"))
    far_tiles = other_core(tiles)
    edge_first, edge_second, node_first, node_second, node_grad = plain_call(
        final_kernel,
        [edge_count, coarse_of],
        [tiles, far_tiles, own, ahead, behind, lists, node_total],
        [
            shape(3, 16, 2, 16, 128, dtype=F32),
            shape(128, 512, dtype=F32),
            shape(2, 16, 2, 16, 128, dtype=F32),
            shape(128, 512, dtype=F32),
            shape(256, 512, dtype=F32),
        ],
    )
    return (
        edge_out,
        node_out,
        node_grad,
        edge_grad,
        edge_first.reshape(3, 512, 128),
        edge_second,
        node_first.reshape(2, 512, 128),
        node_second,
    )


def solution(mesh):
    cube = Mesh(mesh.devices.reshape(4, 4, 2, 4), BOTH)
    rows = P(BOTH, None)
    flat = P(BOTH)
    first, second = P(None, None, "feat"), P("feat", None)
    return jax.shard_map(
        shards,
        mesh=cube,
        in_specs=(
            rows,
            rows,
            flat,
            flat,
            flat,
            P(BOTH, None, None),
            rows,
            first,
            second,
            first,
            second,
            rows,
            rows,
        ),
        out_specs=(rows, rows, rows, rows, first, second, first, second),
        check_vma=False,
    )
```

```python
import jax
import jax.numpy as jnp
from jax import lax
from jax.experimental import pallas as pl
from jax.experimental.pallas import tpu as pltpu
from jax.sharding import Mesh
from jax.sharding import PartitionSpec as P

EPSILON = 1e-05
BF16 = jnp.bfloat16
F32 = jnp.float32
BOTH = ("z", "x", "core", "feat")
CHUNK = 512
STEPS = 4
TABLE = 896
MIB = 1024 * 1024


def places(count):
    core = lax.axis_index("core")
    patch = (lax.axis_index("z") * 4 + lax.axis_index("x")) * 2 + core
    return patch, patch, core, lax.axis_index("feat"), count[0]


def other_core(value):
    return lax.ppermute(value, "core", [(0, 1), (1, 0)])


def shifted(value, steps):
    return lax.ppermute(value, BOTH, [(k, (k + steps) % 128) for k in range(128)])


def exchange(value, axes):
    return lax.all_to_all(value, axes, 0, 0, tiled=True)


def after(value, *earlier):
    return lax.optimization_barrier((value, *earlier))[0]


def repeated(value, count):
    return jnp.broadcast_to(value[None], (count,) + value.shape)


def dot(left, right):
    return lax.dot_general(left, right, (((1,), (0,)), ((), ())), preferred_element_type=F32)


def dot_nt(left, right):
    return lax.dot_general(left, right, (((1,), (1,)), ((), ())), preferred_element_type=F32)


def dot_tn(left, right):
    return lax.dot_general(left, right, (((0,), (0,)), ((), ())), preferred_element_type=F32)


def mean(values):
    return jnp.mean(values, axis=-1, keepdims=True)


def normalize(values):
    centre = values - mean(values)
    factor = lax.rsqrt(mean(centre * centre) + EPSILON)
    return centre * factor, factor


def normalize_back(upstream, normed, factor):
    return factor * (upstream - mean(upstream) - normed * mean(upstream * normed))


def swish(pre):
    half = 0.5 * pre
    tanh = jnp.tanh(half)
    act = half + half * tanh
    return act, 0.5 * (1.0 + act + tanh * (1.0 - act))


def hot_tiles(rows, count):
    lanes = lax.broadcasted_iota(jnp.int32, (128, 128), 1)
    spread = jnp.transpose(jnp.broadcast_to(rows, (128, 128)))
    return [jnp.where(spread == lanes + 128 * j, 1.0, 0.0).astype(BF16) for j in range(count)]


def turned_rows(row, count):
    place = lax.broadcasted_iota(jnp.int32, (128, CHUNK), 0)
    return [jnp.where(place + 128 * j == row, 1.0, 0.0).astype(BF16) for j in range(count)]


def live_targets(step, row, count):
    lanes = lax.broadcasted_iota(jnp.int32, row.shape, 1)
    return jnp.where(lanes + step * CHUNK < count, row, -1)


def hot_kernel(count, dst, src_wide, dst_wide, edge, hot, turned, edge_turned):
    co = places(count)
    step = pl.program_id(0)
    edge_turned[...] = jnp.transpose(edge[...])
    lanes = lax.broadcasted_iota(jnp.int32, (1, 128), 1)
    for r in range(CHUNK // 128):
        row = pl.ds(step * (CHUNK // 128) + r, 1)
        live = lanes + step * CHUNK + r * 128 < co[4]
        tiles = hot_tiles(jnp.where(live, dst[row, :], -1), 2)
        hot[r * 128 : (r + 1) * 128, :] = jnp.concatenate(tiles, axis=1)
    at = pl.ds(step, 1)
    blocks = turned_rows(live_targets(step, dst_wide[at, :], co[4]), 2)
    blocks += turned_rows(src_wide[at, :], 7)
    for j, block in enumerate(blocks):
        turned[j * 128 : (j + 1) * 128, :] = block


def halo_match(lists):
    place = lax.broadcasted_iota(jnp.int32, (256, 32), 0)
    return [jnp.where(place == lists[k : k + 1, :], 1.0, 0.0).astype(BF16) for k in range(2)]


def coarse_match(owned):
    place = lax.broadcasted_iota(jnp.int32, (256, 16), 0)
    slot = lax.broadcasted_iota(jnp.int32, (256, 16), 1) % 4
    hot = jnp.zeros((256, 16), F32)
    for j in range(4):
        hot = jnp.where((place == owned[0, j]) & (slot == j), 1.0, hot)
    return hot.astype(BF16)


def pack_kernel(count, owned, node, lists, edge_first, edge_second, first, second, *outs):
    tiles, to_next, to_prev, packed = outs
    co = places(count)
    halo_hot, coarse_hot = halo_match(lists), coarse_match(owned)
    to_prev[...] = dot_tn(halo_hot[0], node[...]).astype(BF16)
    to_next[...] = dot_tn(halo_hot[1], node[...]).astype(BF16)
    rows = dot_tn(coarse_hot, node[...])
    group = lax.broadcasted_iota(jnp.int32, (16, 128), 0) // 4
    coarse = jnp.zeros((16, 128), F32)
    for b in range(4):
        coarse = jnp.where(group == b, rows[:, b * 128 : (b + 1) * 128], coarse)
    patch = co[0]
    at = pl.ds(pl.multiple_of(patch * 16, 16), 16)
    parts = [edge_first[m, at, :] for m in range(3)]
    row = pl.ds(pl.multiple_of(patch // 4 * 16, 16), 16)
    parts.append(edge_second[row, pl.ds(pl.multiple_of(patch % 4 * 128, 128), 128)])
    parts.append(coarse.astype(BF16))
    tile = jnp.concatenate(parts, axis=0)
    for k in range(64):
        tiles[k] = tile
    at = pl.ds(pl.multiple_of(co[2] * 256, 256), 256)
    row = pl.ds(pl.multiple_of(co[2] * 64, 64), 64)
    for m in range(2):
        packed[m * 256 : (m + 1) * 256, :] = first[m, at, :]
    for b in range(4):
        packed[512 + b * 64 : 576 + b * 64, :] = second[row, b * 128 : (b + 1) * 128]


def live_rows(step, start, count):
    place = lax.broadcasted_iota(jnp.int32, (STRIP, 1), 0) + (step * CHUNK + start)
    return jnp.where(place < count, 1.0, 0.0)


STRIP = 64
STRIPS = [slice(r, r + STRIP) for r in range(0, CHUNK, STRIP)]


def place_weights(co, own_first, own_second, near, far, first, second):
    core, y = co[2], co[3]
    for s in range(4):
        yy = (y - s) & 3
        columns = pl.ds(pl.multiple_of(yy * 128, 128), 128)
        if s == 0:
            for m in range(2):
                first[m, :, columns] = own_first[m]
            second[columns, :] = own_second[...]
            continue
        for part, half in ((near[s - 1], core), (far[s - 1], 1 - core)):
            rows = pl.ds(pl.multiple_of(half * 256, 256), 256)
            for m in range(2):
                first[m, rows, columns] = part[m * 256 : (m + 1) * 256, :]
            rows = pl.ds(pl.multiple_of(yy * 128 + half * 64, 64), 64)
            for b in range(4):
                start = 512 + b * 64
                second[rows, b * 128 : (b + 1) * 128] = part[start : start + 64, :]


def whole(first, m):
    return first[m].reshape(512, 512)


def place_tiles(own_core, near, far, lookup, first, second, coarse):
    for part, core in ((near, own_core), (far, 1 - own_core)):
        for y in range(4):
            block = slice(y * 128, (y + 1) * 128)
            for m in range(3):
                value = part[:, y, m * 16 : (m + 1) * 16, :].reshape(16, 1, 16, 128)
                first[m, :, pl.ds(core, 1), :, block] = value
            for k in range(16):
                rows = slice(y * 128 + k // 2 * 16, y * 128 + k // 2 * 16 + 16)
                columns = pl.ds(pl.multiple_of((k % 2 * 2 + core) * 128, 128), 128)
                second[rows, columns] = part[k, y, 48:64, :]
            coarse[:, pl.ds(core, 1), y] = part[:, y, 64:80, :].reshape(16, 1, 16, 128)
    low = lax.broadcasted_iota(jnp.int32, (64, 8, 128), 1) < 4
    pairs = coarse[...].reshape(64, 2, 16, 128).astype(F32)
    for half in range(2):
        even, odd = pairs[:, 0, half * 8 : half * 8 + 8], pairs[:, 1, half * 8 : half * 8 + 8]
        first_block = jnp.where(low, even, pltpu.roll(odd, 4, 1)).reshape(512, 128)
        other_block = jnp.where(low, pltpu.roll(even, 4, 1), odd).reshape(512, 128)
        lookup[320:832, half * 256 : half * 256 + 128] = first_block.astype(BF16)
        lookup[320:832, half * 256 + 128 : half * 256 + 256] = other_block.astype(BF16)


def forward_kernel(count, node, prev, following, near, far, src, dst, dst_wide, edge, *refs):
    edge_out, incoming, act_out, normed_out, slope_out, factor_out, lookup, first, second = refs[:9]
    table, total, coarse, hot, turned, held = refs[9:]
    co = places(count)
    step = pl.program_id(0)

    @pl.when(step == 0)
    def _():
        lookup[0:256, :] = node[...]
        lookup[256:288, :] = prev[...]
        lookup[288:320, :] = following[...]
        lookup[832:896, :] = jnp.zeros((64, 512), BF16)
        place_tiles(co[2], near, far, lookup, first, second, coarse)
        table[0:256, :] = dot(node[...], whole(first, 2)).astype(BF16)
        table[256:, :] = dot(lookup[...], whole(first, 1)).astype(BF16)
        total[...] = jnp.zeros_like(total)

    for r in range(CHUNK // 128):
        row = pl.ds(step * (CHUNK // 128) + r, 1)
        tiles = hot_tiles(dst[row, :], 2) + hot_tiles(src[row, :], 7)
        for j, tile in enumerate(tiles):
            hot[r * 128 : (r + 1) * 128, j * 128 : (j + 1) * 128] = tile
    blocks = turned_rows(live_targets(step, dst_wide[pl.ds(step, 1), :], co[4]), 2)
    for j, block in enumerate(blocks):
        turned[j * 128 : (j + 1) * 128, :] = block
    held[...] = dot(edge[...], whole(first, 0)) + dot(hot[...], table[...])
    for h in STRIPS:
        act, slope = swish(held[h, :])
        act_out[h, :] = act.astype(BF16)
        slope_out[h, :] = slope.astype(BF16)
    held[...] = dot(act_out[...], second[...])
    for h in STRIPS:
        value = held[h, :]
        centre = value - mean(value)
        live = live_rows(step, h.start, co[4])
        factor = lax.rsqrt(mean(centre * centre) + EPSILON) * live
        normed = centre * factor
        normed_out[h, :] = normed.astype(BF16)
        factor_out[h, :] = jnp.broadcast_to(factor, (STRIP, 128))
        edge_out[h, :] = (edge[h, :].astype(F32) + normed).astype(BF16)
    total[...] += dot(turned[...], edge_out[...])

    @pl.when(step == STEPS - 1)
    def _():
        incoming[...] = total[...].astype(BF16)


def put_columns(co, grad, slot, scratch, keep, give):
    scratch[...] = grad.astype(BF16).reshape(16, 2, 16, 512)
    for target, core in ((keep, co[2]), (give, 1 - co[2])):
        value = scratch[:, pl.ds(core, 1), :, :].reshape(8, 2, 16, 512)
        for y in range(4):
            target[:, :, y, slot * 16 : (slot + 1) * 16, :] = value[:, :, :, y * 128 : (y + 1) * 128]


def put_rows(co, grad, slot, scratch, keep, give):
    for b in range(4):
        scratch[b] = grad[:, b * 128 : (b + 1) * 128].astype(BF16)
    for target, core in ((keep, co[2]), (give, 1 - co[2])):
        for h in range(2):
            value = scratch[2 * h + core].reshape(4, 8, 16, 128)
            for y in range(4):
                target[:, h, y, slot * 16 : (slot + 1) * 16, :] = value[y]


def put_owned(co, grad, scratch, keep, give):
    rows = grad.reshape(64, 8, 512)
    turned = pltpu.roll(rows, 4, 1)
    low = lax.broadcasted_iota(jnp.int32, (64, 8, 128), 1) < 4
    for odd in range(2):
        left, right = (turned, rows) if odd else (rows, turned)
        parts = [
            jnp.where(low, left[:, :, b : b + 128], right[:, :, b + 128 : b + 256]) for b in (0, 256)
        ]
        tile = jnp.concatenate(parts, axis=1).astype(BF16).reshape(16, 2, 2, 16, 128)
        for pair in range(2):
            scratch[:, :, pair * 2 + odd] = tile[:, :, pair]
    for target, core in ((keep, co[2]), (give, 1 - co[2])):
        value = scratch[:, pl.ds(core, 1)].reshape(8, 2, 4, 16, 128)
        target[:, :, :, 112:128, :] = value


def backward_kernel(count, node, incoming, grad_node, own_first, own_second, *refs):
    near, far, refs = refs[:3], refs[3:6], refs[6:]
    co = places(count)
    edge_first, edge_second, lookup = refs[:3]
    edge_turned, act, normed, slope, factor, grad_edge, hot, turned = refs[3:11]
    node_out, node_total, pre_grads, to_prev, to_next, keep, give, spread = refs[11:19]
    first, second, sum_second, sum_first, sums, columns, rows, owned = refs[19:27]
    held, back, deltas = refs[27:]
    step = pl.program_id(0)

    @pl.when(step == 0)
    def _():
        place_weights(co, own_first, own_second, near, far, first, second)
        lat, summed = node[...], incoming[...]
        pre = dot(lat, first[0]) + dot(summed, first[1])
        node_act, node_slope = swish(pre)
        node_act = node_act.astype(BF16)
        node_normed, node_factor = normalize(dot(node_act, second[...]))
        node_out[...] = (lat.astype(F32) + node_normed).astype(BF16)
        upstream = grad_node[...].astype(F32)
        delta = normalize_back(upstream, node_normed, node_factor).astype(BF16)
        put_rows(co, dot_tn(node_act, delta), 6, rows, keep, give)
        pre_grad = (dot_nt(delta, second[...]) * node_slope).astype(BF16)
        put_columns(co, dot_tn(lat, pre_grad), 3, columns, keep, give)
        put_columns(co, dot_tn(summed, pre_grad), 4, columns, keep, give)
        node_total[...] = upstream + dot_nt(pre_grad, first[0])
        spread[...] = dot_nt(pre_grad, first[1]).astype(BF16)
        sum_second[...] = jnp.zeros_like(sum_second)
        sum_first[...] = jnp.zeros_like(sum_first)
        sums[...] = jnp.zeros_like(sums)

    held[...] = dot(hot[...], spread[...])
    for h in STRIPS:
        total = grad_edge[h, :].astype(F32) + held[h, :]
        delta = normalize_back(total, normed[h, :].astype(F32), factor[h, 0:1])
        deltas[h, :] = delta.astype(BF16)
    back[...] = dot_nt(deltas[...], edge_second[...])
    for h in STRIPS:
        pre_grads[h, :] = (back[h, :] * slope[h, :].astype(F32)).astype(BF16)
    sum_second[...] += dot_tn(act[...], deltas[...])
    sum_first[...] += dot(edge_turned[...], pre_grads[...])
    sums[...] += dot(turned[...], pre_grads[...])

    @pl.when(step == STEPS - 1)
    def _():
        put_rows(co, sum_second[...], 5, rows, keep, give)
        put_columns(co, sum_first[...], 0, columns, keep, give)
        received = sums[0:256, :].astype(BF16)
        sent = sums[256:, :].astype(BF16)
        put_columns(co, dot_tn(lookup[...], sent), 1, columns, keep, give)
        put_columns(co, dot_tn(node[...], received), 2, columns, keep, give)
        remote = dot_nt(sent, whole(edge_first, 1))
        node_total[...] += remote[0:256] + dot_nt(received, whole(edge_first, 2))
        to_prev[...] = remote[256:288].astype(BF16)
        to_next[...] = remote[288:320].astype(BF16)
        put_owned(co, remote[320:832], owned, keep, give)


def edge_kernel(spread, first, grad_edge, hot, pre_grads, edge_grad):
    total = grad_edge[...].astype(F32) + dot(hot[...], spread[...])
    edge_grad[...] = (total + dot_nt(pre_grads[...], whole(first, 0))).astype(BF16)


def final_kernel(count, owned, tiles, far, own, ahead, behind, lists, node_total, *refs):
    edge_first, edge_second, node_first, node_second, node_grad = refs
    co = places(count)
    for part, core in ((tiles, co[2]), (far, 1 - co[2])):
        for m in range(3):
            value = part[:, m * 16 : (m + 1) * 16, :].astype(F32)
            edge_first[m, :, pl.ds(core, 1)] = value.reshape(16, 1, 16, 128)
        for m in range(2):
            value = part[:, 48 + m * 16 : 64 + m * 16, :].astype(F32)
            node_first[m, :, pl.ds(core, 1)] = value.reshape(16, 1, 16, 128)
        for k in range(16):
            r = k // 2 * 16
            b = pl.ds(pl.multiple_of((k % 2 * 2 + core) * 128, 128), 128)
            edge_second[r : r + 16, b] = part[k, 80:96, :].astype(F32)
            node_second[r : r + 16, b] = part[k, 96:112, :].astype(F32)
    halo_hot, coarse_hot = halo_match(lists), coarse_match(owned)
    group = lax.broadcasted_iota(jnp.int32, (16, 128), 0) // 4
    rows = own[112:128, :].astype(F32)
    blocks = [jnp.where(group == b, rows, 0.0).astype(BF16) for b in range(4)]
    node_grad[...] = (
        node_total[...]
        + dot(halo_hot[1], ahead[...])
        + dot(halo_hot[0], behind[...])
        + dot(coarse_hot, jnp.concatenate(blocks, axis=1))
    )


SMEM = pl.BlockSpec(memory_space=pltpu.SMEM)
WHOLE = pl.BlockSpec(memory_space=pltpu.VMEM)


def shape(*dims, dtype=BF16):
    return jax.ShapeDtypeStruct(dims, dtype)


def plain_call(kernel, scalars, operands, outs, scratch=(), mib=16):
    return pl.pallas_call(
        kernel,
        in_specs=[SMEM] * len(scalars) + [WHOLE] * len(operands),
        out_specs=[WHOLE] * len(outs),
        out_shape=list(outs),
        scratch_shapes=list(scratch),
        compiler_params=pltpu.CompilerParams(vmem_limit_bytes=mib * MIB),
    )(*scalars, *operands)


def same(*dims):
    once = pl.Buffered(buffer_count=1)
    return pl.BlockSpec(dims, lambda i: (0,) * len(dims), pipeline_mode=once)


def chunk(*dims):
    return pl.BlockSpec(dims, lambda i: (i,) + (0,) * (len(dims) - 1))


def limit(mib):
    return pltpu.CompilerParams(
        vmem_limit_bytes=mib * MIB, dimension_semantics=("arbitrary",)
    )


def column(*dims):
    return pl.BlockSpec(dims, lambda i: (0, i))


def like(value):
    return same(*value.shape)


def shards(
    node_lat,
    edge_lat,
    edge_src,
    edge_dst,
    edge_count,
    halo_send,
    coarse_of,
    edge_w1,
    edge_w2,
    node_w1,
    node_w2,
    grad_node,
    grad_edge,
):
    lists = halo_send.reshape(2, 32)
    packed, to_next, to_prev, node_half = plain_call(
        pack_kernel,
        [edge_count, coarse_of],
        [node_lat, lists, edge_w1, edge_w2, node_w1, node_w2],
        [shape(64, 80, 128), shape(32, 512), shape(32, 512), shape(768, 128)],
        mib=60,
    )
    from_prev = shifted(to_next, 1)
    from_next = shifted(to_prev, -1)
    near = exchange(packed, ("z", "x", "feat")).reshape(16, 4, 80, 128)
    src, dst = edge_src.reshape(16, 128), edge_dst.reshape(16, 128)
    dst_wide = edge_dst.reshape(STEPS, CHUNK)
    indices = [dst, edge_src.reshape(STEPS, CHUNK), dst_wide]
    indices = [after(value, packed) for value in indices]
    high = TABLE + 256
    wide = chunk(CHUNK, 512)
    hot, turned, edge_turned = pl.pallas_call(
        hot_kernel,
        grid=(STEPS,),
        in_specs=[SMEM] + [like(v) for v in indices] + [wide],
        out_specs=[chunk(CHUNK, 256), column(high, CHUNK), column(512, CHUNK)],
        out_shape=[shape(2048, 256), shape(high, 2048), shape(512, 2048)],
        compiler_params=limit(60),
        cost_estimate=pl.CostEstimate(
            flops=20_000_000, bytes_accessed=14_000_000, transcendentals=0
        ),
    )(edge_count, *indices, edge_lat)
    near = after(near, from_prev, from_next, hot)
    far = other_core(near)
    node_half = after(node_half, near)
    node_near = [
        lax.ppermute(node_half, "feat", [(k, (k + s) % 4) for k in range(4)]) for s in (1, 2, 3)
    ]

    fixed = [node_lat, from_prev, from_next, near, far, src, dst, dst_wide]
    wide = chunk(CHUNK, 512)
    edge_out, incoming, act, normed, slope, factor, lookup, first, second = pl.pallas_call(
        forward_kernel,
        grid=(STEPS,),
        in_specs=[SMEM]
        + [like(v) for v in fixed]
        + [wide],
        out_specs=[wide, same(256, 512), wide, wide, wide, chunk(CHUNK, 128)]
        + [same(TABLE, 512), same(3, 16, 2, 16, 512), same(512, 512)],
        out_shape=[
            shape(2048, 512),
            shape(256, 512),
            shape(2048, 512),
            shape(2048, 512),
            shape(2048, 512),
            shape(2048, 128, dtype=F32),
            shape(TABLE, 512),
            shape(3, 16, 2, 16, 512),
            shape(512, 512),
        ],
        scratch_shapes=[
            pltpu.VMEM((TABLE + 256, 512), BF16),
            pltpu.VMEM((256, 512), F32),
            pltpu.VMEM((16, 2, 4, 16, 128), BF16),
            pltpu.VMEM((CHUNK, high), BF16),
            pltpu.VMEM((256, CHUNK), BF16),
            pltpu.VMEM((CHUNK, 512), F32),
        ],
        compiler_params=limit(16),
        cost_estimate=pl.CostEstimate(
            flops=7_000_000_000, bytes_accessed=18_000_000, transcendentals=1_000_000
        ),
    )(edge_count, *fixed, edge_lat)

    node_near = [after(part, incoming) for part in node_near]
    node_far = [other_core(part) for part in node_near]
    fixed = [node_lat, incoming, grad_node, node_w1, node_w2, *node_near, *node_far]
    fixed += [first, second, lookup]
    moving = [edge_turned, act, normed, slope, factor, grad_edge, hot, turned]
    tiles = (8, 2, 4, 128, 128)
    node_out, node_total, pre_grads, to_prev, to_next, keep, give, spread = pl.pallas_call(
        backward_kernel,
        grid=(STEPS,),
        in_specs=[SMEM]
        + [like(v) for v in fixed]
        + [column(512, CHUNK), wide, wide, wide, chunk(CHUNK, 128), wide, chunk(CHUNK, 256)]
        + [column(high, CHUNK)],
        out_specs=[same(256, 512), same(256, 512), wide, same(32, 512), same(32, 512)]
        + [same(*tiles), same(*tiles), same(256, 512)],
        out_shape=[
            shape(256, 512),
            shape(256, 512, dtype=F32),
            shape(2048, 512),
            shape(32, 512),
            shape(32, 512),
            shape(*tiles),
            shape(*tiles),
            shape(256, 512),
        ],
        scratch_shapes=[
            pltpu.VMEM((2, 512, 512), BF16),
            pltpu.VMEM((512, 512), BF16),
            pltpu.VMEM((512, 512), F32),
            pltpu.VMEM((512, 512), F32),
            pltpu.VMEM((TABLE + 256, 512), F32),
            pltpu.VMEM((16, 2, 16, 512), BF16),
            pltpu.VMEM((4, 512, 128), BF16),
            pltpu.VMEM((16, 2, 4, 16, 128), BF16),
            pltpu.VMEM((CHUNK, 512), F32),
            pltpu.VMEM((CHUNK, 512), F32),
            pltpu.VMEM((CHUNK, 512), BF16),
        ],
        compiler_params=limit(24),
        cost_estimate=pl.CostEstimate(
            flops=9_000_000_000, bytes_accessed=24_000_000, transcendentals=100_000
        ),
    )(edge_count, *fixed, *moving)

    pair = (keep.astype(F32) + other_core(give).astype(F32)).astype(BF16).reshape(64, 128, 128)
    edge_first = after(first, pair)
    edge_grad = pl.pallas_call(
        edge_kernel,
        grid=(STEPS,),
        in_specs=[same(256, 512), same(3, 16, 2, 16, 512), wide, chunk(CHUNK, 256), wide],
        out_specs=wide,
        out_shape=shape(2048, 512),
        input_output_aliases={4: 0},
        compiler_params=limit(60),
        cost_estimate=pl.CostEstimate(
            flops=1_600_000_000, bytes_accessed=9_000_000, transcendentals=0
        ),
    )(spread, edge_first, grad_edge, hot, pre_grads)
    ahead = shifted(after(to_prev, pair), -1)
    behind = shifted(after(to_next, pair), 1)
    own = jnp.sum(exchange(pair, ("z", "x", "feat")).astype(F32), axis=0).astype(BF16)
    own = after(own, ahead, behind, edge_grad)
    tiles = exchange(repeated(own[:112], 16), ("z", "x"))
    far_tiles = other_core(tiles)
    edge_first, edge_second, node_first, node_second, node_grad = plain_call(
        final_kernel,
        [edge_count, coarse_of],
        [tiles, far_tiles, own, ahead, behind, lists, node_total],
        [
            shape(3, 16, 2, 16, 128, dtype=F32),
            shape(128, 512, dtype=F32),
            shape(2, 16, 2, 16, 128, dtype=F32),
            shape(128, 512, dtype=F32),
            shape(256, 512, dtype=F32),
        ],
    )
    return (
        edge_out,
        node_out,
        node_grad,
        edge_grad,
        edge_first.reshape(3, 512, 128),
        edge_second,
        node_first.reshape(2, 512, 128),
        node_second,
    )


def solution(mesh):
    cube = Mesh(mesh.devices.reshape(4, 4, 2, 4), BOTH)
    rows = P(BOTH, None)
    flat = P(BOTH)
    first, second = P(None, None, "feat"), P("feat", None)
    return jax.shard_map(
        shards,
        mesh=cube,
        in_specs=(
            rows,
            rows,
            flat,
            flat,
            flat,
            P(BOTH, None, None),
            rows,
            first,
            second,
            first,
            second,
            rows,
            rows,
        ),
        out_specs=(rows, rows, rows, rows, first, second, first, second),
        check_vma=False,
    )
```

```python
import jax
import jax.numpy as jnp
from jax import lax
from jax.experimental import pallas as pl
from jax.experimental.pallas import tpu as pltpu
from jax.sharding import Mesh
from jax.sharding import PartitionSpec as P

EPSILON = 1e-05
BF16 = jnp.bfloat16
F32 = jnp.float32
BOTH = ("z", "x", "core", "feat")
CHUNK = 512
STEPS = 4
TABLE = 896
MIB = 1024 * 1024


def places(count):
    core = lax.axis_index("core")
    patch = (lax.axis_index("z") * 4 + lax.axis_index("x")) * 2 + core
    return patch, patch, core, lax.axis_index("feat"), count[0]


def other_core(value):
    return lax.ppermute(value, "core", [(0, 1), (1, 0)])


def shifted(value, steps):
    return lax.ppermute(value, BOTH, [(k, (k + steps) % 128) for k in range(128)])


def exchange(value, axes):
    return lax.all_to_all(value, axes, 0, 0, tiled=True)


def after(value, *earlier):
    return lax.optimization_barrier((value, *earlier))[0]


def repeated(value, count):
    return jnp.broadcast_to(value[None], (count,) + value.shape)


def dot(left, right):
    return lax.dot_general(left, right, (((1,), (0,)), ((), ())), preferred_element_type=F32)


def dot_nt(left, right):
    return lax.dot_general(left, right, (((1,), (1,)), ((), ())), preferred_element_type=F32)


def dot_tn(left, right):
    return lax.dot_general(left, right, (((0,), (0,)), ((), ())), preferred_element_type=F32)


def mean(values):
    return jnp.mean(values, axis=-1, keepdims=True)


def normalize(values):
    centre = values - mean(values)
    factor = lax.rsqrt(mean(centre * centre) + EPSILON)
    return centre * factor, factor


def normalize_back(upstream, normed, factor):
    return factor * (upstream - mean(upstream) - normed * mean(upstream * normed))


def swish(pre):
    half = 0.5 * pre
    tanh = jnp.tanh(half)
    act = half + half * tanh
    return act, 0.5 * (1.0 + act + tanh * (1.0 - act))


def hot_tiles(rows, count):
    lanes = lax.broadcasted_iota(jnp.int32, (128, 128), 1)
    spread = jnp.transpose(jnp.broadcast_to(rows, (128, 128)))
    return [jnp.where(spread == lanes + 128 * j, 1.0, 0.0).astype(BF16) for j in range(count)]


def turned_rows(row, count):
    place = lax.broadcasted_iota(jnp.int32, (128, CHUNK), 0)
    return [jnp.where(place + 128 * j == row, 1.0, 0.0).astype(BF16) for j in range(count)]


def live_targets(step, row, count):
    lanes = lax.broadcasted_iota(jnp.int32, row.shape, 1)
    return jnp.where(lanes + step * CHUNK < count, row, -1)


def hot_kernel(count, dst, src_wide, dst_wide, edge, hot, turned, edge_turned):
    co = places(count)
    step = pl.program_id(0)
    edge_turned[...] = jnp.transpose(edge[...])
    lanes = lax.broadcasted_iota(jnp.int32, (1, 128), 1)
    for r in range(CHUNK // 128):
        row = pl.ds(step * (CHUNK // 128) + r, 1)
        live = lanes + step * CHUNK + r * 128 < co[4]
        tiles = hot_tiles(jnp.where(live, dst[row, :], -1), 2)
        hot[r * 128 : (r + 1) * 128, :] = jnp.concatenate(tiles, axis=1)
    at = pl.ds(step, 1)
    blocks = turned_rows(live_targets(step, dst_wide[at, :], co[4]), 2)
    blocks += turned_rows(src_wide[at, :], 7)
    for j, block in enumerate(blocks):
        turned[j * 128 : (j + 1) * 128, :] = block


def halo_match(lists):
    place = lax.broadcasted_iota(jnp.int32, (256, 32), 0)
    return [jnp.where(place == lists[k : k + 1, :], 1.0, 0.0).astype(BF16) for k in range(2)]


def coarse_match(owned):
    place = lax.broadcasted_iota(jnp.int32, (256, 16), 0)
    slot = lax.broadcasted_iota(jnp.int32, (256, 16), 1) % 4
    hot = jnp.zeros((256, 16), F32)
    for j in range(4):
        hot = jnp.where((place == owned[0, j]) & (slot == j), 1.0, hot)
    return hot.astype(BF16)


def pack_kernel(count, owned, node, lists, edge_first, edge_second, first, second, *outs):
    tiles, to_next, to_prev, packed = outs
    co = places(count)
    halo_hot, coarse_hot = halo_match(lists), coarse_match(owned)
    to_prev[...] = dot_tn(halo_hot[0], node[...]).astype(BF16)
    to_next[...] = dot_tn(halo_hot[1], node[...]).astype(BF16)
    rows = dot_tn(coarse_hot, node[...])
    group = lax.broadcasted_iota(jnp.int32, (16, 128), 0) // 4
    coarse = jnp.zeros((16, 128), F32)
    for b in range(4):
        coarse = jnp.where(group == b, rows[:, b * 128 : (b + 1) * 128], coarse)
    patch = co[0]
    at = pl.ds(pl.multiple_of(patch * 16, 16), 16)
    parts = [edge_first[m, at, :] for m in range(3)]
    row = pl.ds(pl.multiple_of(patch // 4 * 16, 16), 16)
    parts.append(edge_second[row, pl.ds(pl.multiple_of(patch % 4 * 128, 128), 128)])
    parts.append(coarse.astype(BF16))
    tile = jnp.concatenate(parts, axis=0)
    for k in range(64):
        tiles[k] = tile
    at = pl.ds(pl.multiple_of(co[2] * 256, 256), 256)
    row = pl.ds(pl.multiple_of(co[2] * 64, 64), 64)
    for m in range(2):
        packed[m * 256 : (m + 1) * 256, :] = first[m, at, :]
    for b in range(4):
        packed[512 + b * 64 : 576 + b * 64, :] = second[row, b * 128 : (b + 1) * 128]


def live_rows(step, start, count):
    place = lax.broadcasted_iota(jnp.int32, (STRIP, 1), 0) + (step * CHUNK + start)
    return jnp.where(place < count, 1.0, 0.0)


STRIP = 64
STRIPS = [slice(r, r + STRIP) for r in range(0, CHUNK, STRIP)]


def place_weights(co, own_first, own_second, near, far, first, second):
    core, y = co[2], co[3]
    for s in range(4):
        yy = (y - s) & 3
        columns = pl.ds(pl.multiple_of(yy * 128, 128), 128)
        if s == 0:
            for m in range(2):
                first[m, :, columns] = own_first[m]
            second[columns, :] = own_second[...]
            continue
        for part, half in ((near[s - 1], core), (far[s - 1], 1 - core)):
            rows = pl.ds(pl.multiple_of(half * 256, 256), 256)
            for m in range(2):
                first[m, rows, columns] = part[m * 256 : (m + 1) * 256, :]
            rows = pl.ds(pl.multiple_of(yy * 128 + half * 64, 64), 64)
            for b in range(4):
                start = 512 + b * 64
                second[rows, b * 128 : (b + 1) * 128] = part[start : start + 64, :]


def whole(first, m):
    return first[m].reshape(512, 512)


def place_tiles(own_core, near, far, lookup, first, second, coarse):
    for part, core in ((near, own_core), (far, 1 - own_core)):
        for y in range(4):
            block = slice(y * 128, (y + 1) * 128)
            for m in range(3):
                value = part[:, y, m * 16 : (m + 1) * 16, :].reshape(16, 1, 16, 128)
                first[m, :, pl.ds(core, 1), :, block] = value
            for k in range(16):
                rows = slice(y * 128 + k // 2 * 16, y * 128 + k // 2 * 16 + 16)
                columns = pl.ds(pl.multiple_of((k % 2 * 2 + core) * 128, 128), 128)
                second[rows, columns] = part[k, y, 48:64, :]
            coarse[:, pl.ds(core, 1), y] = part[:, y, 64:80, :].reshape(16, 1, 16, 128)
    low = lax.broadcasted_iota(jnp.int32, (64, 8, 128), 1) < 4
    pairs = coarse[...].reshape(64, 2, 16, 128).astype(F32)
    for half in range(2):
        even, odd = pairs[:, 0, half * 8 : half * 8 + 8], pairs[:, 1, half * 8 : half * 8 + 8]
        first_block = jnp.where(low, even, pltpu.roll(odd, 4, 1)).reshape(512, 128)
        other_block = jnp.where(low, pltpu.roll(even, 4, 1), odd).reshape(512, 128)
        lookup[320:832, half * 256 : half * 256 + 128] = first_block.astype(BF16)
        lookup[320:832, half * 256 + 128 : half * 256 + 256] = other_block.astype(BF16)


def forward_kernel(count, node, prev, following, near, far, src, dst, dst_wide, edge, *refs):
    edge_out, incoming, act_out, normed_out, slope_out, factor_out, lookup, first, second = refs[:9]
    table, total, coarse, hot, turned, held = refs[9:]
    co = places(count)
    step = pl.program_id(0)

    @pl.when(step == 0)
    def _():
        lookup[0:256, :] = node[...]
        lookup[256:288, :] = prev[...]
        lookup[288:320, :] = following[...]
        lookup[832:896, :] = jnp.zeros((64, 512), BF16)
        place_tiles(co[2], near, far, lookup, first, second, coarse)
        table[0:256, :] = dot(node[...], whole(first, 2)).astype(BF16)
        table[256:, :] = dot(lookup[...], whole(first, 1)).astype(BF16)
        total[...] = jnp.zeros_like(total)

    for r in range(CHUNK // 128):
        row = pl.ds(step * (CHUNK // 128) + r, 1)
        tiles = hot_tiles(dst[row, :], 2) + hot_tiles(src[row, :], 7)
        for j, tile in enumerate(tiles):
            hot[r * 128 : (r + 1) * 128, j * 128 : (j + 1) * 128] = tile
    blocks = turned_rows(live_targets(step, dst_wide[pl.ds(step, 1), :], co[4]), 2)
    for j, block in enumerate(blocks):
        turned[j * 128 : (j + 1) * 128, :] = block
    held[...] = dot(edge[...], whole(first, 0)) + dot(hot[...], table[...])
    for h in STRIPS:
        act, slope = swish(held[h, :])
        act_out[h, :] = act.astype(BF16)
        slope_out[h, :] = slope.astype(BF16)
    held[...] = dot(act_out[...], second[...])
    for h in STRIPS:
        value = held[h, :]
        centre = value - mean(value)
        live = live_rows(step, h.start, co[4])
        factor = lax.rsqrt(mean(centre * centre) + EPSILON) * live
        normed = centre * factor
        normed_out[h, :] = normed.astype(BF16)
        factor_out[h, :] = jnp.broadcast_to(factor, (STRIP, 128))
        edge_out[h, :] = (edge[h, :].astype(F32) + normed).astype(BF16)
    total[...] += dot(turned[...], edge_out[...])

    @pl.when(step == STEPS - 1)
    def _():
        incoming[...] = total[...].astype(BF16)


def put_columns(co, grad, slot, scratch, keep, give):
    scratch[...] = grad.astype(BF16).reshape(16, 2, 16, 512)
    for target, core in ((keep, co[2]), (give, 1 - co[2])):
        value = scratch[:, pl.ds(core, 1), :, :].reshape(8, 2, 16, 512)
        for y in range(4):
            target[:, :, y, slot * 16 : (slot + 1) * 16, :] = value[:, :, :, y * 128 : (y + 1) * 128]


def put_rows(co, grad, slot, scratch, keep, give):
    for b in range(4):
        scratch[b] = grad[:, b * 128 : (b + 1) * 128].astype(BF16)
    for target, core in ((keep, co[2]), (give, 1 - co[2])):
        for h in range(2):
            value = scratch[2 * h + core].reshape(4, 8, 16, 128)
            for y in range(4):
                target[:, h, y, slot * 16 : (slot + 1) * 16, :] = value[y]


def put_owned(co, grad, scratch, keep, give):
    rows = grad.reshape(64, 8, 512)
    turned = pltpu.roll(rows, 4, 1)
    low = lax.broadcasted_iota(jnp.int32, (64, 8, 128), 1) < 4
    for odd in range(2):
        left, right = (turned, rows) if odd else (rows, turned)
        parts = [
            jnp.where(low, left[:, :, b : b + 128], right[:, :, b + 128 : b + 256]) for b in (0, 256)
        ]
        tile = jnp.concatenate(parts, axis=1).astype(BF16).reshape(16, 2, 2, 16, 128)
        for pair in range(2):
            scratch[:, :, pair * 2 + odd] = tile[:, :, pair]
    for target, core in ((keep, co[2]), (give, 1 - co[2])):
        value = scratch[:, pl.ds(core, 1)].reshape(8, 2, 4, 16, 128)
        target[:, :, :, 112:128, :] = value


def backward_kernel(count, node, incoming, grad_node, own_first, own_second, *refs):
    near, far, refs = refs[:3], refs[3:6], refs[6:]
    co = places(count)
    edge_first, edge_second, lookup = refs[:3]
    edge_turned, act, normed, slope, factor, grad_edge, hot, turned = refs[3:11]
    node_out, node_total, pre_grads, to_prev, to_next, keep, give, spread = refs[11:19]
    first, second, sum_second, sum_first, sums, columns, rows, owned = refs[19:27]
    held, back, deltas = refs[27:]
    place_weights(co, own_first, own_second, near, far, first, second)
    lat, summed = node[...], incoming[...]
    pre = dot(lat, first[0]) + dot(summed, first[1])
    node_act, node_slope = swish(pre)
    node_act = node_act.astype(BF16)
    node_normed, node_factor = normalize(dot(node_act, second[...]))
    node_out[...] = (lat.astype(F32) + node_normed).astype(BF16)
    upstream = grad_node[...].astype(F32)
    delta = normalize_back(upstream, node_normed, node_factor).astype(BF16)
    put_rows(co, dot_tn(node_act, delta), 6, rows, keep, give)
    pre_grad = (dot_nt(delta, second[...]) * node_slope).astype(BF16)
    put_columns(co, dot_tn(lat, pre_grad), 3, columns, keep, give)
    put_columns(co, dot_tn(summed, pre_grad), 4, columns, keep, give)
    node_total[...] = upstream + dot_nt(pre_grad, first[0])
    spread[...] = dot_nt(pre_grad, first[1]).astype(BF16)
    sum_second[...] = jnp.zeros_like(sum_second)
    sum_first[...] = jnp.zeros_like(sum_first)
    sums[...] = jnp.zeros_like(sums)

    def block(step, carry):
        at = pl.ds(pl.multiple_of(step * CHUNK, CHUNK), CHUNK)
        normed_at, slope_at, factor_at = normed.at[at], slope.at[at], factor.at[at]
        grad_at, pre_at, columns_at = grad_edge.at[at], pre_grads.at[at], edge_turned.at[:, at]
        held[...] = dot(hot[at, :], spread[...])
        for h in STRIPS:
            total = grad_at[h, :].astype(F32) + held[h, :]
            delta = normalize_back(total, normed_at[h, :].astype(F32), factor_at[h, 0:1])
            deltas[h, :] = delta.astype(BF16)
        back[...] = dot_nt(deltas[...], edge_second[...])
        for h in STRIPS:
            pre_at[h, :] = (back[h, :] * slope_at[h, :].astype(F32)).astype(BF16)
        sum_second[...] += dot_tn(act[at, :], deltas[...])
        sum_first[...] += dot(columns_at[...], pre_at[...])
        sums[...] += dot(turned[:, at], pre_at[...])
        return carry

    lax.fori_loop(0, STEPS, block, 0)
    put_rows(co, sum_second[...], 5, rows, keep, give)
    put_columns(co, sum_first[...], 0, columns, keep, give)
    received = sums[0:256, :].astype(BF16)
    sent = sums[256:, :].astype(BF16)
    put_columns(co, dot_tn(lookup[...], sent), 1, columns, keep, give)
    put_columns(co, dot_tn(node[...], received), 2, columns, keep, give)
    remote = dot_nt(sent, whole(edge_first, 1))
    node_total[...] += remote[0:256] + dot_nt(received, whole(edge_first, 2))
    to_prev[...] = remote[256:288].astype(BF16)
    to_next[...] = remote[288:320].astype(BF16)
    put_owned(co, remote[320:832], owned, keep, give)


def edge_kernel(spread, first, grad_edge, hot, pre_grads, edge_grad):
    total = grad_edge[...].astype(F32) + dot(hot[...], spread[...])
    edge_grad[...] = (total + dot_nt(pre_grads[...], whole(first, 0))).astype(BF16)


def final_kernel(count, owned, tiles, far, own, ahead, behind, lists, node_total, *refs):
    edge_first, edge_second, node_first, node_second, node_grad = refs
    co = places(count)
    for part, core in ((tiles, co[2]), (far, 1 - co[2])):
        for m in range(3):
            value = part[:, m * 16 : (m + 1) * 16, :].astype(F32)
            edge_first[m, :, pl.ds(core, 1)] = value.reshape(16, 1, 16, 128)
        for m in range(2):
            value = part[:, 48 + m * 16 : 64 + m * 16, :].astype(F32)
            node_first[m, :, pl.ds(core, 1)] = value.reshape(16, 1, 16, 128)
        for k in range(16):
            r = k // 2 * 16
            b = pl.ds(pl.multiple_of((k % 2 * 2 + core) * 128, 128), 128)
            edge_second[r : r + 16, b] = part[k, 80:96, :].astype(F32)
            node_second[r : r + 16, b] = part[k, 96:112, :].astype(F32)
    halo_hot, coarse_hot = halo_match(lists), coarse_match(owned)
    group = lax.broadcasted_iota(jnp.int32, (16, 128), 0) // 4
    rows = own[112:128, :].astype(F32)
    blocks = [jnp.where(group == b, rows, 0.0).astype(BF16) for b in range(4)]
    node_grad[...] = (
        node_total[...]
        + dot(halo_hot[1], ahead[...])
        + dot(halo_hot[0], behind[...])
        + dot(coarse_hot, jnp.concatenate(blocks, axis=1))
    )


SMEM = pl.BlockSpec(memory_space=pltpu.SMEM)
WHOLE = pl.BlockSpec(memory_space=pltpu.VMEM)


def shape(*dims, dtype=BF16):
    return jax.ShapeDtypeStruct(dims, dtype)


def plain_call(kernel, scalars, operands, outs, scratch=(), mib=16):
    return pl.pallas_call(
        kernel,
        in_specs=[SMEM] * len(scalars) + [WHOLE] * len(operands),
        out_specs=[WHOLE] * len(outs),
        out_shape=list(outs),
        scratch_shapes=list(scratch),
        compiler_params=pltpu.CompilerParams(vmem_limit_bytes=mib * MIB),
    )(*scalars, *operands)


def same(*dims):
    once = pl.Buffered(buffer_count=1)
    return pl.BlockSpec(dims, lambda i: (0,) * len(dims), pipeline_mode=once)


def chunk(*dims):
    return pl.BlockSpec(dims, lambda i: (i,) + (0,) * (len(dims) - 1))


def limit(mib):
    return pltpu.CompilerParams(
        vmem_limit_bytes=mib * MIB, dimension_semantics=("arbitrary",)
    )


def column(*dims):
    return pl.BlockSpec(dims, lambda i: (0, i))


def like(value):
    return same(*value.shape)


def shards(
    node_lat,
    edge_lat,
    edge_src,
    edge_dst,
    edge_count,
    halo_send,
    coarse_of,
    edge_w1,
    edge_w2,
    node_w1,
    node_w2,
    grad_node,
    grad_edge,
):
    lists = halo_send.reshape(2, 32)
    packed, to_next, to_prev, node_half = plain_call(
        pack_kernel,
        [edge_count, coarse_of],
        [node_lat, lists, edge_w1, edge_w2, node_w1, node_w2],
        [shape(64, 80, 128), shape(32, 512), shape(32, 512), shape(768, 128)],
        mib=60,
    )
    from_prev = shifted(to_next, 1)
    from_next = shifted(to_prev, -1)
    near = exchange(packed, ("z", "x", "feat")).reshape(16, 4, 80, 128)
    src, dst = edge_src.reshape(16, 128), edge_dst.reshape(16, 128)
    dst_wide = edge_dst.reshape(STEPS, CHUNK)
    indices = [dst, edge_src.reshape(STEPS, CHUNK), dst_wide]
    indices = [after(value, packed) for value in indices]
    high = TABLE + 256
    wide = chunk(CHUNK, 512)
    hot, turned, edge_turned = pl.pallas_call(
        hot_kernel,
        grid=(STEPS,),
        in_specs=[SMEM] + [like(v) for v in indices] + [wide],
        out_specs=[chunk(CHUNK, 256), column(high, CHUNK), column(512, CHUNK)],
        out_shape=[shape(2048, 256), shape(high, 2048), shape(512, 2048)],
        compiler_params=limit(60),
        cost_estimate=pl.CostEstimate(
            flops=20_000_000, bytes_accessed=14_000_000, transcendentals=0
        ),
    )(edge_count, *indices, edge_lat)
    near = after(near, from_prev, from_next, hot)
    far = other_core(near)
    node_half = after(node_half, near)
    node_near = [
        lax.ppermute(node_half, "feat", [(k, (k + s) % 4) for k in range(4)]) for s in (1, 2, 3)
    ]

    fixed = [node_lat, from_prev, from_next, near, far, src, dst, dst_wide]
    wide = chunk(CHUNK, 512)
    edge_out, incoming, act, normed, slope, factor, lookup, first, second = pl.pallas_call(
        forward_kernel,
        grid=(STEPS,),
        in_specs=[SMEM]
        + [like(v) for v in fixed]
        + [wide],
        out_specs=[wide, same(256, 512), wide, wide, wide, chunk(CHUNK, 128)]
        + [same(TABLE, 512), same(3, 16, 2, 16, 512), same(512, 512)],
        out_shape=[
            shape(2048, 512),
            shape(256, 512),
            shape(2048, 512),
            shape(2048, 512),
            shape(2048, 512),
            shape(2048, 128, dtype=F32),
            shape(TABLE, 512),
            shape(3, 16, 2, 16, 512),
            shape(512, 512),
        ],
        scratch_shapes=[
            pltpu.VMEM((TABLE + 256, 512), BF16),
            pltpu.VMEM((256, 512), F32),
            pltpu.VMEM((16, 2, 4, 16, 128), BF16),
            pltpu.VMEM((CHUNK, high), BF16),
            pltpu.VMEM((256, CHUNK), BF16),
            pltpu.VMEM((CHUNK, 512), F32),
        ],
        compiler_params=limit(16),
        cost_estimate=pl.CostEstimate(
            flops=7_000_000_000, bytes_accessed=18_000_000, transcendentals=1_000_000
        ),
    )(edge_count, *fixed, edge_lat)

    node_near = [after(part, incoming) for part in node_near]
    node_far = [other_core(part) for part in node_near]
    fixed = [node_lat, incoming, grad_node, node_w1, node_w2, *node_near, *node_far]
    fixed += [first, second, lookup]
    moving = [edge_turned, act, normed, slope, factor, grad_edge, hot, turned]
    tiles = (8, 2, 4, 128, 128)
    node_out, node_total, pre_grads, to_prev, to_next, keep, give, spread = plain_call(
        backward_kernel,
        [edge_count],
        fixed + moving,
        [
            shape(256, 512),
            shape(256, 512, dtype=F32),
            shape(2048, 512),
            shape(32, 512),
            shape(32, 512),
            shape(*tiles),
            shape(*tiles),
            shape(256, 512),
        ],
        [
            pltpu.VMEM((2, 512, 512), BF16),
            pltpu.VMEM((512, 512), BF16),
            pltpu.VMEM((512, 512), F32),
            pltpu.VMEM((512, 512), F32),
            pltpu.VMEM((TABLE + 256, 512), F32),
            pltpu.VMEM((16, 2, 16, 512), BF16),
            pltpu.VMEM((4, 512, 128), BF16),
            pltpu.VMEM((16, 2, 4, 16, 128), BF16),
            pltpu.VMEM((CHUNK, 512), F32),
            pltpu.VMEM((CHUNK, 512), F32),
            pltpu.VMEM((CHUNK, 512), BF16),
        ],
        mib=34,
    )

    pair = (keep.astype(F32) + other_core(give).astype(F32)).astype(BF16).reshape(64, 128, 128)
    edge_first = after(first, pair)
    edge_grad = pl.pallas_call(
        edge_kernel,
        grid=(STEPS,),
        in_specs=[same(256, 512), same(3, 16, 2, 16, 512), wide, chunk(CHUNK, 256), wide],
        out_specs=wide,
        out_shape=shape(2048, 512),
        input_output_aliases={4: 0},
        compiler_params=limit(60),
        cost_estimate=pl.CostEstimate(
            flops=1_600_000_000, bytes_accessed=9_000_000, transcendentals=0
        ),
    )(spread, edge_first, grad_edge, hot, pre_grads)
    ahead = shifted(after(to_prev, pair), -1)
    behind = shifted(after(to_next, pair), 1)
    own = jnp.sum(exchange(pair, ("z", "x", "feat")).astype(F32), axis=0).astype(BF16)
    own = after(own, ahead, behind, edge_grad)
    tiles = exchange(repeated(own[:112], 16), ("z", "x"))
    far_tiles = other_core(tiles)
    edge_first, edge_second, node_first, node_second, node_grad = plain_call(
        final_kernel,
        [edge_count, coarse_of],
        [tiles, far_tiles, own, ahead, behind, lists, node_total],
        [
            shape(3, 16, 2, 16, 128, dtype=F32),
            shape(128, 512, dtype=F32),
            shape(2, 16, 2, 16, 128, dtype=F32),
            shape(128, 512, dtype=F32),
            shape(256, 512, dtype=F32),
        ],
    )
    return (
        edge_out,
        node_out,
        node_grad,
        edge_grad,
        edge_first.reshape(3, 512, 128),
        edge_second,
        node_first.reshape(2, 512, 128),
        node_second,
    )


def solution(mesh):
    cube = Mesh(mesh.devices.reshape(4, 4, 2, 4), BOTH)
    rows = P(BOTH, None)
    flat = P(BOTH)
    first, second = P(None, None, "feat"), P("feat", None)
    return jax.shard_map(
        shards,
        mesh=cube,
        in_specs=(
            rows,
            rows,
            flat,
            flat,
            flat,
            P(BOTH, None, None),
            rows,
            first,
            second,
            first,
            second,
            rows,
            rows,
        ),
        out_specs=(rows, rows, rows, rows, first, second, first, second),
        check_vma=False,
    )
```

```python
import jax
import jax.numpy as jnp
from jax import lax
from jax.experimental import pallas as pl
from jax.experimental.pallas import tpu as pltpu
from jax.sharding import Mesh
from jax.sharding import PartitionSpec as P

EPSILON = 1e-05
BF16 = jnp.bfloat16
F32 = jnp.float32
BOTH = ("z", "x", "core", "feat")
CHUNK = 512
STEPS = 4
TABLE = 896
MIB = 1024 * 1024


def places(count):
    core = lax.axis_index("core")
    patch = (lax.axis_index("z") * 4 + lax.axis_index("x")) * 2 + core
    return patch, patch, core, lax.axis_index("feat"), count[0]


def other_core(value):
    return lax.ppermute(value, "core", [(0, 1), (1, 0)])


def shifted(value, steps):
    return lax.ppermute(value, BOTH, [(k, (k + steps) % 128) for k in range(128)])


def exchange(value, axes):
    return lax.all_to_all(value, axes, 0, 0, tiled=True)


def after(value, *earlier):
    return lax.optimization_barrier((value, *earlier))[0]


def repeated(value, count):
    return jnp.broadcast_to(value[None], (count,) + value.shape)


def dot(left, right):
    return lax.dot_general(left, right, (((1,), (0,)), ((), ())), preferred_element_type=F32)


def dot_nt(left, right):
    return lax.dot_general(left, right, (((1,), (1,)), ((), ())), preferred_element_type=F32)


def dot_tn(left, right):
    return lax.dot_general(left, right, (((0,), (0,)), ((), ())), preferred_element_type=F32)


def mean(values):
    return jnp.mean(values, axis=-1, keepdims=True)


def normalize(values):
    centre = values - mean(values)
    factor = lax.rsqrt(mean(centre * centre) + EPSILON)
    return centre * factor, factor


def normalize_back(upstream, normed, factor):
    return factor * (upstream - mean(upstream) - normed * mean(upstream * normed))


def swish(pre):
    half = 0.5 * pre
    tanh = jnp.tanh(half)
    act = half + half * tanh
    return act, 0.5 * (1.0 + act + tanh * (1.0 - act))


def hot_tiles(rows, count):
    lanes = lax.broadcasted_iota(jnp.int32, (128, 128), 1)
    spread = jnp.transpose(jnp.broadcast_to(rows, (128, 128)))
    return [jnp.where(spread == lanes + 128 * j, 1.0, 0.0).astype(BF16) for j in range(count)]


def turned_rows(row, count):
    place = lax.broadcasted_iota(jnp.int32, (128, CHUNK), 0)
    return [jnp.where(place + 128 * j == row, 1.0, 0.0).astype(BF16) for j in range(count)]


def live_targets(step, row, count):
    lanes = lax.broadcasted_iota(jnp.int32, row.shape, 1)
    return jnp.where(lanes + step * CHUNK < count, row, -1)


def hot_kernel(count, dst, src_wide, dst_wide, edge, hot, turned, edge_turned):
    co = places(count)
    step = pl.program_id(0)
    edge_turned[...] = jnp.transpose(edge[...])
    lanes = lax.broadcasted_iota(jnp.int32, (1, 128), 1)
    for r in range(CHUNK // 128):
        row = pl.ds(step * (CHUNK // 128) + r, 1)
        live = lanes + step * CHUNK + r * 128 < co[4]
        tiles = hot_tiles(jnp.where(live, dst[row, :], -1), 2)
        hot[r * 128 : (r + 1) * 128, :] = jnp.concatenate(tiles, axis=1)
    at = pl.ds(step, 1)
    blocks = turned_rows(live_targets(step, dst_wide[at, :], co[4]), 2)
    blocks += turned_rows(src_wide[at, :], 7)
    for j, block in enumerate(blocks):
        turned[j * 128 : (j + 1) * 128, :] = block


def halo_match(lists):
    place = lax.broadcasted_iota(jnp.int32, (256, 32), 0)
    return [jnp.where(place == lists[k : k + 1, :], 1.0, 0.0).astype(BF16) for k in range(2)]


def coarse_match(owned):
    place = lax.broadcasted_iota(jnp.int32, (256, 16), 0)
    slot = lax.broadcasted_iota(jnp.int32, (256, 16), 1) % 4
    hot = jnp.zeros((256, 16), F32)
    for j in range(4):
        hot = jnp.where((place == owned[0, j]) & (slot == j), 1.0, hot)
    return hot.astype(BF16)


def pack_kernel(count, owned, node, lists, edge_first, edge_second, first, second, *outs):
    tiles, to_next, to_prev, packed = outs
    co = places(count)
    halo_hot, coarse_hot = halo_match(lists), coarse_match(owned)
    to_prev[...] = dot_tn(halo_hot[0], node[...]).astype(BF16)
    to_next[...] = dot_tn(halo_hot[1], node[...]).astype(BF16)
    rows = dot_tn(coarse_hot, node[...])
    group = lax.broadcasted_iota(jnp.int32, (16, 128), 0) // 4
    coarse = jnp.zeros((16, 128), F32)
    for b in range(4):
        coarse = jnp.where(group == b, rows[:, b * 128 : (b + 1) * 128], coarse)
    patch = co[0]
    at = pl.ds(pl.multiple_of(patch * 16, 16), 16)
    parts = [edge_first[m, at, :] for m in range(3)]
    row = pl.ds(pl.multiple_of(patch // 4 * 16, 16), 16)
    parts.append(edge_second[row, pl.ds(pl.multiple_of(patch % 4 * 128, 128), 128)])
    parts.append(coarse.astype(BF16))
    tile = jnp.concatenate(parts, axis=0)
    for k in range(64):
        tiles[k] = tile
    at = pl.ds(pl.multiple_of(co[2] * 256, 256), 256)
    row = pl.ds(pl.multiple_of(co[2] * 64, 64), 64)
    for m in range(2):
        packed[m * 256 : (m + 1) * 256, :] = first[m, at, :]
    for b in range(4):
        packed[512 + b * 64 : 576 + b * 64, :] = second[row, b * 128 : (b + 1) * 128]


def live_rows(step, start, count):
    place = lax.broadcasted_iota(jnp.int32, (STRIP, 1), 0) + (step * CHUNK + start)
    return jnp.where(place < count, 1.0, 0.0)


STRIP = 64
STRIPS = [slice(r, r + STRIP) for r in range(0, CHUNK, STRIP)]


def place_weights(co, own_first, own_second, near, far, first, second):
    core, y = co[2], co[3]
    for s in range(4):
        yy = (y - s) & 3
        columns = pl.ds(pl.multiple_of(yy * 128, 128), 128)
        if s == 0:
            for m in range(2):
                first[m, :, columns] = own_first[m]
            second[columns, :] = own_second[...]
            continue
        for part, half in ((near[s - 1], core), (far[s - 1], 1 - core)):
            rows = pl.ds(pl.multiple_of(half * 256, 256), 256)
            for m in range(2):
                first[m, rows, columns] = part[m * 256 : (m + 1) * 256, :]
            rows = pl.ds(pl.multiple_of(yy * 128 + half * 64, 64), 64)
            for b in range(4):
                start = 512 + b * 64
                second[rows, b * 128 : (b + 1) * 128] = part[start : start + 64, :]


def whole(first, m):
    return first[m].reshape(512, 512)


def place_tiles(own_core, near, far, lookup, first, second, coarse):
    for part, core in ((near, own_core), (far, 1 - own_core)):
        for y in range(4):
            block = slice(y * 128, (y + 1) * 128)
            for m in range(3):
                value = part[:, y, m * 16 : (m + 1) * 16, :].reshape(16, 1, 16, 128)
                first[m, :, pl.ds(core, 1), :, block] = value
            for k in range(16):
                rows = slice(y * 128 + k // 2 * 16, y * 128 + k // 2 * 16 + 16)
                columns = pl.ds(pl.multiple_of((k % 2 * 2 + core) * 128, 128), 128)
                second[rows, columns] = part[k, y, 48:64, :]
            coarse[:, pl.ds(core, 1), y] = part[:, y, 64:80, :].reshape(16, 1, 16, 128)
    low = lax.broadcasted_iota(jnp.int32, (64, 8, 128), 1) < 4
    pairs = coarse[...].reshape(64, 2, 16, 128).astype(F32)
    for half in range(2):
        even, odd = pairs[:, 0, half * 8 : half * 8 + 8], pairs[:, 1, half * 8 : half * 8 + 8]
        first_block = jnp.where(low, even, pltpu.roll(odd, 4, 1)).reshape(512, 128)
        other_block = jnp.where(low, pltpu.roll(even, 4, 1), odd).reshape(512, 128)
        lookup[320:832, half * 256 : half * 256 + 128] = first_block.astype(BF16)
        lookup[320:832, half * 256 + 128 : half * 256 + 256] = other_block.astype(BF16)


def forward_kernel(count, node, prev, following, near, far, src, dst, dst_wide, edge, *refs):
    edge_out, incoming, act_out, normed_out, slope_out, factor_out, lookup, first, second = refs[:9]
    table, total, coarse, hot, turned, held = refs[9:]
    co = places(count)
    step = pl.program_id(0)

    @pl.when(step == 0)
    def _():
        lookup[0:256, :] = node[...]
        lookup[256:288, :] = prev[...]
        lookup[288:320, :] = following[...]
        lookup[832:896, :] = jnp.zeros((64, 512), BF16)
        place_tiles(co[2], near, far, lookup, first, second, coarse)
        table[0:256, :] = dot(node[...], whole(first, 2)).astype(BF16)
        table[256:, :] = dot(lookup[...], whole(first, 1)).astype(BF16)
        total[...] = jnp.zeros_like(total)

    for r in range(CHUNK // 128):
        row = pl.ds(step * (CHUNK // 128) + r, 1)
        tiles = hot_tiles(dst[row, :], 2) + hot_tiles(src[row, :], 7)
        for j, tile in enumerate(tiles):
            hot[r * 128 : (r + 1) * 128, j * 128 : (j + 1) * 128] = tile
    blocks = turned_rows(live_targets(step, dst_wide[pl.ds(step, 1), :], co[4]), 2)
    for j, block in enumerate(blocks):
        turned[j * 128 : (j + 1) * 128, :] = block
    held[...] = dot(edge[...], whole(first, 0)) + dot(hot[...], table[...])
    for h in STRIPS:
        act, slope = swish(held[h, :])
        act_out[h, :] = act.astype(BF16)
        slope_out[h, :] = slope.astype(BF16)
    held[...] = dot(act_out[...], second[...])
    for h in STRIPS:
        value = held[h, :]
        centre = value - mean(value)
        live = live_rows(step, h.start, co[4])
        factor = lax.rsqrt(mean(centre * centre) + EPSILON) * live
        normed = centre * factor
        normed_out[h, :] = normed.astype(BF16)
        factor_out[h, :] = jnp.broadcast_to(factor, (STRIP, 128))
        edge_out[h, :] = (edge[h, :].astype(F32) + normed).astype(BF16)
    total[...] += dot(turned[...], edge_out[...])

    @pl.when(step == STEPS - 1)
    def _():
        incoming[...] = total[...].astype(BF16)


def put_columns(co, grad, slot, scratch, keep, give):
    scratch[...] = grad.astype(BF16).reshape(16, 2, 16, 512)
    for target, core in ((keep, co[2]), (give, 1 - co[2])):
        value = scratch[:, pl.ds(core, 1), :, :].reshape(8, 2, 16, 512)
        for y in range(4):
            target[:, :, y, slot * 16 : (slot + 1) * 16, :] = value[:, :, :, y * 128 : (y + 1) * 128]


def put_rows(co, grad, slot, scratch, keep, give):
    for b in range(4):
        scratch[b] = grad[:, b * 128 : (b + 1) * 128].astype(BF16)
    for target, core in ((keep, co[2]), (give, 1 - co[2])):
        for h in range(2):
            value = scratch[2 * h + core].reshape(4, 8, 16, 128)
            for y in range(4):
                target[:, h, y, slot * 16 : (slot + 1) * 16, :] = value[y]


def put_owned(co, grad, scratch, keep, give):
    rows = grad.reshape(64, 8, 512)
    turned = pltpu.roll(rows, 4, 1)
    low = lax.broadcasted_iota(jnp.int32, (64, 8, 128), 1) < 4
    for odd in range(2):
        left, right = (turned, rows) if odd else (rows, turned)
        parts = [
            jnp.where(low, left[:, :, b : b + 128], right[:, :, b + 128 : b + 256]) for b in (0, 256)
        ]
        tile = jnp.concatenate(parts, axis=1).astype(BF16).reshape(16, 2, 2, 16, 128)
        for pair in range(2):
            scratch[:, :, pair * 2 + odd] = tile[:, :, pair]
    for target, core in ((keep, co[2]), (give, 1 - co[2])):
        value = scratch[:, pl.ds(core, 1)].reshape(8, 2, 4, 16, 128)
        target[:, :, :, 112:128, :] = value


def backward_kernel(count, node, incoming, grad_node, own_first, own_second, *refs):
    near, far, refs = refs[:3], refs[3:6], refs[6:]
    co = places(count)
    edge_first, edge_second, lookup = refs[:3]
    edge_turned, act, normed, slope, factor, grad_edge, hot, turned = refs[3:11]
    node_out, node_total, pre_grads, to_prev, to_next, keep, give, spread = refs[11:19]
    first, second, sum_second, sum_first, sums, columns, rows, owned = refs[19:27]
    held, back, deltas = refs[27:]
    step = pl.program_id(0)

    @pl.when(step == 0)
    def _():
        place_weights(co, own_first, own_second, near, far, first, second)
        lat, summed = node[...], incoming[...]
        pre = dot(lat, first[0]) + dot(summed, first[1])
        node_act, node_slope = swish(pre)
        node_act = node_act.astype(BF16)
        node_normed, node_factor = normalize(dot(node_act, second[...]))
        node_out[...] = (lat.astype(F32) + node_normed).astype(BF16)
        upstream = grad_node[...].astype(F32)
        delta = normalize_back(upstream, node_normed, node_factor).astype(BF16)
        put_rows(co, dot_tn(node_act, delta), 6, rows, keep, give)
        pre_grad = (dot_nt(delta, second[...]) * node_slope).astype(BF16)
        put_columns(co, dot_tn(lat, pre_grad), 3, columns, keep, give)
        put_columns(co, dot_tn(summed, pre_grad), 4, columns, keep, give)
        node_total[...] = upstream + dot_nt(pre_grad, first[0])
        spread[...] = dot_nt(pre_grad, first[1]).astype(BF16)
        sum_second[...] = jnp.zeros_like(sum_second)
        sum_first[...] = jnp.zeros_like(sum_first)
        sums[...] = jnp.zeros_like(sums)

    held[...] = dot(hot[...], spread[...])
    for h in STRIPS:
        total = grad_edge[h, :].astype(F32) + held[h, :]
        delta = normalize_back(total, normed[h, :].astype(F32), factor[h, 0:1])
        deltas[h, :] = delta.astype(BF16)
    back[...] = dot_nt(deltas[...], edge_second[...])
    for h in STRIPS:
        pre_grads[h, :] = (back[h, :] * slope[h, :].astype(F32)).astype(BF16)
    sum_second[...] += dot_tn(act[...], deltas[...])
    sum_first[...] += dot(edge_turned[...], pre_grads[...])
    sums[...] += dot(turned[...], pre_grads[...])

    @pl.when(step == STEPS - 1)
    def _():
        put_rows(co, sum_second[...], 5, rows, keep, give)
        put_columns(co, sum_first[...], 0, columns, keep, give)
        received = sums[0:256, :].astype(BF16)
        sent = sums[256:, :].astype(BF16)
        put_columns(co, dot_tn(lookup[...], sent), 1, columns, keep, give)
        put_columns(co, dot_tn(node[...], received), 2, columns, keep, give)
        remote = dot_nt(sent, whole(edge_first, 1))
        node_total[...] += remote[0:256] + dot_nt(received, whole(edge_first, 2))
        to_prev[...] = remote[256:288].astype(BF16)
        to_next[...] = remote[288:320].astype(BF16)
        put_owned(co, remote[320:832], owned, keep, give)


def pair_kernel(keep, got, pair):
    for a in range(8):
        for b in range(2):
            pair[a, b] = (keep[a, b].astype(F32) + got[a, b].astype(F32)).astype(BF16)


def edge_kernel(spread, first, grad_edge, hot, pre_grads, edge_grad):
    total = grad_edge[...].astype(F32) + dot(hot[...], spread[...])
    edge_grad[...] = (total + dot_nt(pre_grads[...], whole(first, 0))).astype(BF16)


def final_kernel(count, owned, tiles, far, own, ahead, behind, lists, node_total, *refs):
    edge_first, edge_second, node_first, node_second, node_grad = refs
    co = places(count)
    for part, core in ((tiles, co[2]), (far, 1 - co[2])):
        for m in range(3):
            value = part[:, m * 16 : (m + 1) * 16, :].astype(F32)
            edge_first[m, :, pl.ds(core, 1)] = value.reshape(16, 1, 16, 128)
        for m in range(2):
            value = part[:, 48 + m * 16 : 64 + m * 16, :].astype(F32)
            node_first[m, :, pl.ds(core, 1)] = value.reshape(16, 1, 16, 128)
        for k in range(16):
            r = k // 2 * 16
            b = pl.ds(pl.multiple_of((k % 2 * 2 + core) * 128, 128), 128)
            edge_second[r : r + 16, b] = part[k, 80:96, :].astype(F32)
            node_second[r : r + 16, b] = part[k, 96:112, :].astype(F32)
    halo_hot, coarse_hot = halo_match(lists), coarse_match(owned)
    group = lax.broadcasted_iota(jnp.int32, (16, 128), 0) // 4
    rows = own[112:128, :].astype(F32)
    blocks = [jnp.where(group == b, rows, 0.0).astype(BF16) for b in range(4)]
    node_grad[...] = (
        node_total[...]
        + dot(halo_hot[1], ahead[...])
        + dot(halo_hot[0], behind[...])
        + dot(coarse_hot, jnp.concatenate(blocks, axis=1))
    )


SMEM = pl.BlockSpec(memory_space=pltpu.SMEM)
WHOLE = pl.BlockSpec(memory_space=pltpu.VMEM)


def shape(*dims, dtype=BF16):
    return jax.ShapeDtypeStruct(dims, dtype)


def plain_call(kernel, scalars, operands, outs, scratch=(), mib=16):
    return pl.pallas_call(
        kernel,
        in_specs=[SMEM] * len(scalars) + [WHOLE] * len(operands),
        out_specs=[WHOLE] * len(outs),
        out_shape=list(outs),
        scratch_shapes=list(scratch),
        compiler_params=pltpu.CompilerParams(vmem_limit_bytes=mib * MIB),
    )(*scalars, *operands)


def same(*dims):
    once = pl.Buffered(buffer_count=1)
    return pl.BlockSpec(dims, lambda i: (0,) * len(dims), pipeline_mode=once)


def chunk(*dims):
    return pl.BlockSpec(dims, lambda i: (i,) + (0,) * (len(dims) - 1))


def limit(mib):
    return pltpu.CompilerParams(
        vmem_limit_bytes=mib * MIB, dimension_semantics=("arbitrary",)
    )


def column(*dims):
    return pl.BlockSpec(dims, lambda i: (0, i))


def like(value):
    return same(*value.shape)


def shards(
    node_lat,
    edge_lat,
    edge_src,
    edge_dst,
    edge_count,
    halo_send,
    coarse_of,
    edge_w1,
    edge_w2,
    node_w1,
    node_w2,
    grad_node,
    grad_edge,
):
    lists = halo_send.reshape(2, 32)
    packed, to_next, to_prev, node_half = plain_call(
        pack_kernel,
        [edge_count, coarse_of],
        [node_lat, lists, edge_w1, edge_w2, node_w1, node_w2],
        [shape(64, 80, 128), shape(32, 512), shape(32, 512), shape(768, 128)],
        mib=60,
    )
    from_prev = shifted(to_next, 1)
    from_next = shifted(to_prev, -1)
    near = exchange(packed, ("z", "x", "feat")).reshape(16, 4, 80, 128)
    src, dst = edge_src.reshape(16, 128), edge_dst.reshape(16, 128)
    dst_wide = edge_dst.reshape(STEPS, CHUNK)
    indices = [dst, edge_src.reshape(STEPS, CHUNK), dst_wide]
    indices = [after(value, packed) for value in indices]
    high = TABLE + 256
    wide = chunk(CHUNK, 512)
    hot, turned, edge_turned = pl.pallas_call(
        hot_kernel,
        grid=(STEPS,),
        in_specs=[SMEM] + [like(v) for v in indices] + [wide],
        out_specs=[chunk(CHUNK, 256), column(high, CHUNK), column(512, CHUNK)],
        out_shape=[shape(2048, 256), shape(high, 2048), shape(512, 2048)],
        compiler_params=limit(60),
        cost_estimate=pl.CostEstimate(
            flops=20_000_000, bytes_accessed=14_000_000, transcendentals=0
        ),
    )(edge_count, *indices, edge_lat)
    near = after(near, from_prev, from_next, hot)
    far = other_core(near)
    node_half = after(node_half, near)
    node_near = [
        lax.ppermute(node_half, "feat", [(k, (k + s) % 4) for k in range(4)]) for s in (1, 2, 3)
    ]

    fixed = [node_lat, from_prev, from_next, near, far, src, dst, dst_wide]
    wide = chunk(CHUNK, 512)
    edge_out, incoming, act, normed, slope, factor, lookup, first, second = pl.pallas_call(
        forward_kernel,
        grid=(STEPS,),
        in_specs=[SMEM]
        + [like(v) for v in fixed]
        + [wide],
        out_specs=[wide, same(256, 512), wide, wide, wide, chunk(CHUNK, 128)]
        + [same(TABLE, 512), same(3, 16, 2, 16, 512), same(512, 512)],
        out_shape=[
            shape(2048, 512),
            shape(256, 512),
            shape(2048, 512),
            shape(2048, 512),
            shape(2048, 512),
            shape(2048, 128, dtype=F32),
            shape(TABLE, 512),
            shape(3, 16, 2, 16, 512),
            shape(512, 512),
        ],
        scratch_shapes=[
            pltpu.VMEM((TABLE + 256, 512), BF16),
            pltpu.VMEM((256, 512), F32),
            pltpu.VMEM((16, 2, 4, 16, 128), BF16),
            pltpu.VMEM((CHUNK, high), BF16),
            pltpu.VMEM((256, CHUNK), BF16),
            pltpu.VMEM((CHUNK, 512), F32),
        ],
        compiler_params=limit(16),
        cost_estimate=pl.CostEstimate(
            flops=7_000_000_000, bytes_accessed=18_000_000, transcendentals=1_000_000
        ),
    )(edge_count, *fixed, edge_lat)

    node_near = [after(part, incoming) for part in node_near]
    node_far = [other_core(part) for part in node_near]
    fixed = [node_lat, incoming, grad_node, node_w1, node_w2, *node_near, *node_far]
    fixed += [first, second, lookup]
    moving = [edge_turned, act, normed, slope, factor, grad_edge, hot, turned]
    tiles = (8, 2, 4, 128, 128)
    node_out, node_total, pre_grads, to_prev, to_next, keep, give, spread = pl.pallas_call(
        backward_kernel,
        grid=(STEPS,),
        in_specs=[SMEM]
        + [like(v) for v in fixed]
        + [column(512, CHUNK), wide, wide, wide, chunk(CHUNK, 128), wide, chunk(CHUNK, 256)]
        + [column(high, CHUNK)],
        out_specs=[same(256, 512), same(256, 512), wide, same(32, 512), same(32, 512)]
        + [same(*tiles), same(*tiles), same(256, 512)],
        out_shape=[
            shape(256, 512),
            shape(256, 512, dtype=F32),
            shape(2048, 512),
            shape(32, 512),
            shape(32, 512),
            shape(*tiles),
            shape(*tiles),
            shape(256, 512),
        ],
        scratch_shapes=[
            pltpu.VMEM((2, 512, 512), BF16),
            pltpu.VMEM((512, 512), BF16),
            pltpu.VMEM((512, 512), F32),
            pltpu.VMEM((512, 512), F32),
            pltpu.VMEM((TABLE + 256, 512), F32),
            pltpu.VMEM((16, 2, 16, 512), BF16),
            pltpu.VMEM((4, 512, 128), BF16),
            pltpu.VMEM((16, 2, 4, 16, 128), BF16),
            pltpu.VMEM((CHUNK, 512), F32),
            pltpu.VMEM((CHUNK, 512), F32),
            pltpu.VMEM((CHUNK, 512), BF16),
        ],
        compiler_params=limit(24),
        cost_estimate=pl.CostEstimate(
            flops=9_000_000_000, bytes_accessed=24_000_000, transcendentals=100_000
        ),
    )(edge_count, *fixed, *moving)

    (pair,) = plain_call(pair_kernel, [], [keep, other_core(give)], [shape(*tiles)])
    pair = pair.reshape(64, 128, 128)
    edge_first = after(first, pair)
    edge_grad = pl.pallas_call(
        edge_kernel,
        grid=(STEPS,),
        in_specs=[same(256, 512), same(3, 16, 2, 16, 512), wide, chunk(CHUNK, 256), wide],
        out_specs=wide,
        out_shape=shape(2048, 512),
        input_output_aliases={4: 0},
        compiler_params=limit(60),
        cost_estimate=pl.CostEstimate(
            flops=1_600_000_000, bytes_accessed=9_000_000, transcendentals=0
        ),
    )(spread, edge_first, grad_edge, hot, pre_grads)
    ahead = shifted(after(to_prev, pair), -1)
    behind = shifted(after(to_next, pair), 1)
    own = jnp.sum(exchange(pair, ("z", "x", "feat")).astype(F32), axis=0).astype(BF16)
    own = after(own, ahead, behind, edge_grad)
    tiles = exchange(repeated(own[:112], 16), ("z", "x"))
    far_tiles = other_core(tiles)
    edge_first, edge_second, node_first, node_second, node_grad = plain_call(
        final_kernel,
        [edge_count, coarse_of],
        [tiles, far_tiles, own, ahead, behind, lists, node_total],
        [
            shape(3, 16, 2, 16, 128, dtype=F32),
            shape(128, 512, dtype=F32),
            shape(2, 16, 2, 16, 128, dtype=F32),
            shape(128, 512, dtype=F32),
            shape(256, 512, dtype=F32),
        ],
    )
    return (
        edge_out,
        node_out,
        node_grad,
        edge_grad,
        edge_first.reshape(3, 512, 128),
        edge_second,
        node_first.reshape(2, 512, 128),
        node_second,
    )


def solution(mesh):
    cube = Mesh(mesh.devices.reshape(4, 4, 2, 4), BOTH)
    rows = P(BOTH, None)
    flat = P(BOTH)
    first, second = P(None, None, "feat"), P("feat", None)
    return jax.shard_map(
        shards,
        mesh=cube,
        in_specs=(
            rows,
            rows,
            flat,
            flat,
            flat,
            P(BOTH, None, None),
            rows,
            first,
            second,
            first,
            second,
            rows,
            rows,
        ),
        out_specs=(rows, rows, rows, rows, first, second, first, second),
        check_vma=False,
    )
```
